32 devices in a mesh: row: 4 (over y, x), col: 8 (over z, core).
Axes of the slice: x: 2, y: 2, z: 4, core: 2. Of those that a mesh axis runs over, the one named last changes fastest.
Arguments:
- tiles: bfloat16 [4, 8, 32, 256, 256], P('row', 'col'), may hold values from -6 to 6
- tile_ids: int32 [4, 8, 2, 32], P('row', 'col'), may hold values from 0 to 7, as said below
- tile_count: int32 [4, 8], P('row', 'col'), may hold values from 8 to 32
- query_degree: int32 [8192], P('row'), may hold values from 1 to 32
- product_degree: int32 [16384], P('col'), may hold values from 1 to 32
- panel: float32 [64, 16384], P(None, ('col', 'row')), may hold values from -6 to 6
Outputs:
- basis: float32 [64, 16384], P(None, ('col', 'row'))
The draws below stay inside these ranges and needn't reach their ends.
Inputs may be any that keep to these rules, and one draw needn't show every extreme that they name: `tile_ids`: on each device the 32 (tile row, tile column) pairs are distinct; tile row is below 8 and tile column below 8.
All inputs are finite; a program needn't handle non-finite values.
Results may differ from the reference program's by a relative error of at most 0.0042.
Values may be sent and summed in bfloat16 or wider, within the bound.
No kernel may reach another device: no remote copies, remote signals or barrier semaphores. Data moves between devices by JAX's collectives and lax.ppermute only.
A program may use at most 64 MiB of HBM per device.

```python
import jax
import jax.numpy as jnp
from jax import lax

TS = 256
R = 64
QB = 8
PB = 8
KT = 32
ITERS = 2
NQ = 8192
NP = 16384
N_ROW = 4
N_COL = 8


def draw_degrees(key, length, stream):
    key = jax.random.fold_in(key, stream)
    first_key, second_key = jax.random.split(key)
    factor = jax.random.randint(first_key, (length,), 1, 5)
    exponent = jax.random.randint(second_key, (length,), 0, 4)
    degree = factor * jnp.left_shift(jnp.ones((length,), jnp.int32), exponent)
    return degree.at[0].set(32).at[1].set(1).astype(jnp.int32)


def draw_query_degree(key, part):
    return draw_degrees(key, NQ, 11)


def draw_product_degree(key, part):
    return draw_degrees(key, NP, 12)


def draw_tile_ids(key, part):
    key = jax.random.fold_in(key, 21)
    device_keys = jax.random.split(key, N_ROW * N_COL)

    def device_order(device_key):
        remaining = 1 + jax.random.permutation(device_key, QB * PB - 2)
        positions = jnp.concatenate([jnp.array([QB * PB - 1], jnp.int32), jnp.array([0], jnp.int32), remaining.astype(jnp.int32)])[:KT]
        return jnp.stack([positions // PB, positions % PB])
    return jax.vmap(device_order)(device_keys).reshape(N_ROW, N_COL, 2, KT).astype(jnp.int32)


def draw_tile_count(key, part):
    key = jax.random.fold_in(key, 31)
    lowest = max(2, KT // 4)
    counts = jax.random.randint(key, (N_ROW * N_COL,), lowest, KT + 1)
    return counts.at[0].set(KT).at[1].set(lowest).reshape(N_ROW, N_COL).astype(jnp.int32)


def steps_of(rng, shape, shards, smallest, largest):
    factor_of, own = 1.0, jax.random.fold_in(rng, 6)
    for dim, parts in shards:
        steps = jnp.exp(jax.random.uniform(jax.random.fold_in(own, dim), (parts,), jnp.float32, smallest / len(shards), largest / len(shards)))
        factor_of = factor_of * jnp.repeat(steps, shape[dim] // parts).reshape([-1 if axis == dim else 1 for axis in range(len(shape))])
    return factor_of


def scatter_about(key, extent, width, reach, cuts=(), kind=jnp.bfloat16):
    factor_of = steps_of(key, extent, cuts, -0.22, 0.18) if cuts else 1.0
    result = jax.random.normal(key, extent, jnp.float32) * width * factor_of
    return jnp.minimum(jnp.maximum(result, -reach), reach).astype(kind)


def setup_inputs(seed: int = 0) -> dict:
    key_list = jax.random.split(jax.random.key(seed), 7)
    return {
        "tiles": scatter_about(key_list[0], (N_ROW, N_COL, KT, TS, TS), 1.0, 6.0, ((0, 4), (1, 8))),
        "tile_ids": draw_tile_ids(jax.random.fold_in(key_list[6], 71), 0),
        "tile_count": draw_tile_count(jax.random.fold_in(key_list[6], 71), 0),
        "query_degree": draw_query_degree(jax.random.fold_in(key_list[6], 71), 0),
        "product_degree": draw_product_degree(jax.random.fold_in(key_list[6], 71), 0),
        "panel": scatter_about(key_list[5], (R, NP), 1.0, 6.0, ((1, 32),), jnp.float32),
    }


HIGH = lax.Precision.HIGHEST

def reference(tiles, tile_ids, tile_count, query_degree, product_degree, panel):
    qscale = 1.0 / jnp.sqrt(query_degree.astype(jnp.float32))
    pscale = 1.0 / jnp.sqrt(product_degree.astype(jnp.float32))
    live_slot = (jnp.arange(KT, dtype=jnp.int32)[None, None, :] < tile_count[:, :, None]).astype(jnp.float32)
    row_hot = (tile_ids[:, :, 0, :, None] == jnp.arange(QB, dtype=jnp.int32)).astype(jnp.float32) * live_slot[..., None]
    col_hot = (tile_ids[:, :, 1, :, None] == jnp.arange(PB, dtype=jnp.int32)).astype(jnp.float32) * live_slot[..., None]
    qgrid = qscale.reshape(N_ROW, 1, QB, TS)
    pgrid = pscale.reshape(N_COL, 1, PB, TS)
    current = panel
    for iteration in range(ITERS):
        scaled = (current * pscale[None, :]).astype(jnp.bfloat16).astype(jnp.float32)
        scaled_blocks = jnp.transpose(scaled.reshape(R, N_COL, PB, TS), (1, 0, 2, 3))

        def query_rows(inputs):
            tiles_r, rhot_r, chot_r = inputs

            def device_terms(running, items):
                tile_set, rhot, chot, block = items
                picked = jnp.einsum('kp,rpj->rkj', chot, block, precision=HIGH)
                products = jnp.einsum('rkj,kij->kri', picked, tile_set.astype(jnp.float32), precision=HIGH)
                return (running + jnp.einsum('kq,kri->rqi', rhot, products, precision=HIGH), None)
            running, unused = lax.scan(device_terms, jnp.zeros((R, QB, TS), jnp.float32), (tiles_r, rhot_r, chot_r, scaled_blocks))
            return running
        row_sums = lax.map(query_rows, (tiles, row_hot, col_hot))
        query_panel = (row_sums * qgrid).astype(jnp.bfloat16).astype(jnp.float32)

        def product_rows(running, items):
            tiles_r, rhot_r, chot_r, ublock = items

            def device_terms(inputs):
                tile_set, rhot, chot = inputs
                picked = jnp.einsum('kq,rqi->rki', rhot, ublock, precision=HIGH)
                products = jnp.einsum('rki,kij->krj', picked, tile_set.astype(jnp.float32), precision=HIGH)
                return jnp.einsum('kp,krj->rpj', chot, products, precision=HIGH)
            return (running + lax.map(device_terms, (tiles_r, rhot_r, chot_r)), None)
        col_sums, unused = lax.scan(product_rows, jnp.zeros((N_COL, R, PB, TS), jnp.float32), (tiles, row_hot, col_hot, query_panel))
        lifted = jnp.transpose(col_sums * pgrid, (1, 0, 2, 3)).reshape(R, N_COL * PB * TS)
        gram = jnp.einsum('ri,si->rs', lifted, lifted, precision=HIGH)
        lower = jnp.linalg.cholesky(gram)
        current = lax.linalg.triangular_solve(lower, lifted, left_side=True, lower=True)
    return current * jnp.sqrt(jnp.float32(NP))
```

```python
import functools
import math

import jax
import jax.numpy as jnp
from jax import lax
from jax.experimental import pallas as pl
from jax.experimental.pallas import tpu as pltpu
from jax.sharding import PartitionSpec as P

ITERS = 2
GROUP = 8
PANEL_STEP = 4
HIGH = lax.Precision.HIGHEST
VMEM_BYTES = 40 * 1024 * 1024
NT = (((1,), (1,)), ((), ()))
NN = (((1,), (0,)), ((), ()))


def pack(block_refs, held, side):
    count, _, share = block_refs.shape
    for block in range(count):
        if share >= side:
            per = share // side
            for piece in range(per):
                held[block * per + piece] = block_refs[block, :, piece * side : (piece + 1) * side]
        else:
            per = side // share
            at = (block % per) * share
            held[block // per, :, at : at + share] = block_refs[block]


def unpack(total, out_ref, side):
    count, _, share = out_ref.shape
    for block in range(count):
        if share >= side:
            per = share // side
            for piece in range(per):
                out_ref[block, :, piece * side : (piece + 1) * side] = total[
                    block * per + piece
                ].astype(out_ref.dtype)
        else:
            per = side // share
            at = (block % per) * share
            out_ref[block] = total[block // per, :, at : at + share].astype(out_ref.dtype)


def product_body(source, target, dims, ids, live, block_ref, tile_ref, out_ref, held, total):
    side = tile_ref.shape[1]
    slots = tile_ref.shape[0]
    tiles = total.shape[0] - 1
    pack(block_ref, held, side)
    total[...] = jnp.zeros_like(total)
    count = live[0]

    def group(g, carry):
        for lane in range(GROUP):
            slot = g * GROUP + lane
            take = ids[source, slot]
            give = jnp.where(slot < count, ids[target, slot], tiles)
            total[give] += lax.dot_general(
                held[take], tile_ref[slot], dims, preferred_element_type=jnp.float32
            )
        return carry

    lax.fori_loop(0, jnp.minimum((count + GROUP - 1) // GROUP, slots // GROUP), group, 0)
    unpack(total, out_ref, side)


def product(blocks, tile_set, ids, live, source, target, dims, pieces, share, in_tiles, out_tiles, dtype):
    width = blocks.shape[1]
    slots, side, _ = tile_set.shape
    return pl.pallas_call(
        functools.partial(product_body, source, target, dims),
        out_shape=jax.ShapeDtypeStruct((pieces, width, share), dtype),
        grid_spec=pltpu.PrefetchScalarGridSpec(
            num_scalar_prefetch=2,
            grid=(),
            in_specs=[pl.BlockSpec(memory_space=pltpu.VMEM)] * 2,
            out_specs=pl.BlockSpec(memory_space=pltpu.VMEM),
            scratch_shapes=[
                pltpu.VMEM((in_tiles, width, side), jnp.bfloat16),
                pltpu.VMEM((out_tiles + 1, width, side), jnp.float32),
            ],
        ),
        compiler_params=pltpu.CompilerParams(vmem_limit_bytes=VMEM_BYTES),
        cost_estimate=pl.CostEstimate(
            flops=2 * slots * width * side * side, bytes_accessed=2 * slots * side * side, transcendentals=0
        ),
        name="product",
    )(ids, live, blocks, tile_set)


def lift_body(part_ref, scale_ref, lifted_ref, gram_ref):
    total = part_ref[0]
    for part in range(1, part_ref.shape[0]):
        total = total + part_ref[part]
    lifted = total * scale_ref[...]
    lifted_ref[...] = lifted
    gram_ref[...] = lax.dot_general(
        lifted, lifted, NT, precision=HIGH, preferred_element_type=jnp.float32
    )


def lift(parts, scale):
    _, width, share = parts.shape
    return pl.pallas_call(
        lift_body,
        out_shape=(
            jax.ShapeDtypeStruct((width, share), jnp.float32),
            jax.ShapeDtypeStruct((width, width), jnp.float32),
        ),
        compiler_params=pltpu.CompilerParams(vmem_limit_bytes=VMEM_BYTES),
        name="lift",
    )(parts, scale)


def inverse_factor(gram):
    width = gram.shape[0]
    rows = lax.broadcasted_iota(jnp.int32, (width, width), 0)
    cols = lax.broadcasted_iota(jnp.int32, (width, width), 1)
    work = jnp.concatenate([gram, (rows == cols).astype(jnp.float32)], axis=1)
    done = []
    for first in range(0, width, PANEL_STEP):
        base = first // 8 * 8
        height = width - base
        ids = lax.broadcasted_iota(jnp.int32, (height, 2 * width), 0) + base
        columns = [
            jnp.broadcast_to(work[:, first + j : first + j + 1], (height, 2 * width))
            for j in range(PANEL_STEP)
        ]
        for j in range(PANEL_STEP):
            k = first + j
            at = k - base
            pivot = columns[j][at : at + 1, :]
            factor = jnp.where(ids > k, columns[j] * (1.0 / pivot), 0.0)
            row = work[at : at + 1, :]
            done.append(row * lax.rsqrt(pivot))
            work = work - factor * row
            for later in range(j + 1, PANEL_STEP):
                columns[later] = columns[later] - factor * columns[later][at : at + 1, :]
        after = (first + PANEL_STEP) // 8 * 8
        if after > base:
            work = work[after - base :, :]
    return jnp.concatenate(done, axis=0)[:, width:]


def solve_body(after, gram_ref, lifted_ref, scale_ref, out_ref):
    gram = gram_ref[0]
    for part in range(1, gram_ref.shape[0]):
        gram = gram + gram_ref[part]
    current = lax.dot_general(
        inverse_factor(gram), lifted_ref[...], NN, precision=HIGH, preferred_element_type=jnp.float32
    )
    if after is None:
        out_ref[...] = (current * scale_ref[...]).astype(out_ref.dtype)
    else:
        out_ref[...] = current * after


def solve(grams, lifted, scale, after):
    return pl.pallas_call(
        functools.partial(solve_body, after),
        out_shape=jax.ShapeDtypeStruct(lifted.shape, jnp.bfloat16 if after is None else jnp.float32),
        compiler_params=pltpu.CompilerParams(vmem_limit_bytes=VMEM_BYTES),
        name="solve",
    )(grams, lifted, scale)


def exchange(parts, axis):
    return lax.all_to_all(parts, axis, 0, 0)


def gather_by_exchange(block, axis):
    count = lax.axis_size(axis)
    return exchange(jnp.broadcast_to(block[None], (count, *block.shape)), axis)


def gather_by_permute(block, axis):
    count = lax.axis_size(axis)
    at = lax.axis_index(axis)
    pieces = [block]
    for step in range(1, count):
        pieces.append(
            lax.ppermute(block, axis, [(i, (i + step) % count) for i in range(count)])
        )
    order = lax.rem(at - jnp.arange(count, dtype=jnp.int32) + count, count)
    return jnp.stack(pieces)[order]


def shards(tiles, tile_ids, tile_count, query_degree, product_degree, panel):
    tile_set = tiles[0, 0]
    ids = tile_ids[0, 0]
    live = tile_count[0]
    side = tile_set.shape[1]
    queries, products = query_degree.shape[0], product_degree.shape[0]
    query_tiles, product_tiles = queries // side, products // side
    n_row, n_col = lax.axis_size("row"), lax.axis_size("col")
    row_at, col_at = lax.axis_index("row"), lax.axis_index("col")
    share = panel.shape[1]
    columns = queries // n_col
    my_pscale = 1.0 / jnp.sqrt(
        lax.dynamic_slice_in_dim(product_degree, row_at * share, share).astype(jnp.float32)
    )[None, :]
    my_qscale = 1.0 / jnp.sqrt(
        lax.dynamic_slice_in_dim(query_degree, col_at * columns, columns).astype(jnp.float32)
    )[None, :]
    root_count = math.sqrt(products * n_col)
    scaled = (panel * my_pscale).astype(jnp.bfloat16)
    for iteration in range(ITERS):
        last = iteration == ITERS - 1
        if iteration == 0:
            blocks = gather_by_permute(scaled, "row")
        else:
            blocks = lax.all_gather(scaled, "row")
        sums = product(
            blocks, tile_set, ids, live, 1, 0, NT, n_col, columns, product_tiles, query_tiles, jnp.bfloat16
        )
        query_sum = jnp.sum(exchange(sums, "col").astype(jnp.float32), axis=0)
        rounded = (query_sum * my_qscale).astype(jnp.bfloat16)
        if iteration == 0:
            blocks = lax.all_gather(rounded, "col")
        else:
            blocks = gather_by_exchange(rounded, "col")
        sums = product(
            blocks, tile_set, ids, live, 0, 1, NN, n_row, share, query_tiles, product_tiles, jnp.float32
        )
        lifted, gram = lift(exchange(sums, "row"), my_pscale)
        if iteration == 0:
            grams = lax.all_gather(gram, ("row", "col"))
        else:
            grams = gather_by_exchange(jnp.sum(gather_by_exchange(gram, "row"), axis=0), "col")
        scaled = solve(grams, lifted, my_pscale, root_count if last else None)
    return scaled


def solution(mesh):
    in_specs = (
        P("row", "col", None, None, None),
        P("row", "col", None, None),
        P("row", "col"),
        P("row"),
        P("col"),
        P(None, ("col", "row")),
    )
    out_specs = P(None, ("col", "row"))
    return jax.shard_map(shards, mesh=mesh, in_specs=in_specs, out_specs=out_specs, check_vma=False)
```

```python
import functools
import math

import jax
import jax.numpy as jnp
from jax import lax
from jax.experimental import pallas as pl
from jax.experimental.pallas import tpu as pltpu
from jax.sharding import PartitionSpec as P

ITERS = 2
GROUP = 8
PANEL_STEP = 4
HIGH = lax.Precision.HIGHEST
VMEM_BYTES = 40 * 1024 * 1024
NT = (((1,), (1,)), ((), ()))
NN = (((1,), (0,)), ((), ()))

def inverse_factor(gram):
    width = gram.shape[0]
    rows = lax.broadcasted_iota(jnp.int32, (width, width), 0)
    cols = lax.broadcasted_iota(jnp.int32, (width, width), 1)
    work = jnp.concatenate([gram, (rows == cols).astype(jnp.float32)], axis=1)
    done = []
    for first in range(0, width, PANEL_STEP):
        base = first // 8 * 8
        height = width - base
        ids = lax.broadcasted_iota(jnp.int32, (height, 2 * width), 0) + base
        columns = [
            jnp.broadcast_to(work[:, first + j : first + j + 1], (height, 2 * width))
            for j in range(PANEL_STEP)
        ]
        for j in range(PANEL_STEP):
            k = first + j
            at = k - base
            pivot = columns[j][at : at + 1, :]
            factor = jnp.where(ids > k, columns[j] * (1.0 / pivot), 0.0)
            row = work[at : at + 1, :]
            done.append(row * lax.rsqrt(pivot))
            work = work - factor * row
            for later in range(j + 1, PANEL_STEP):
                columns[later] = columns[later] - factor * columns[later][at : at + 1, :]
        after = (first + PANEL_STEP) // 8 * 8
        if after > base:
            work = work[after - base :, :]
    return jnp.concatenate(done, axis=0)[:, width:]

WHOLE = pl.BlockSpec(memory_space=pltpu.VMEM)
SCALARS = pl.BlockSpec(memory_space=pltpu.SMEM)
AWAY = pl.BlockSpec(memory_space=pl.ANY)


def call(body, name, in_specs, out_shape, scratch=(), flops=0, moved=0):
    many = isinstance(out_shape, (tuple, list))
    return pl.pallas_call(
        body,
        out_shape=out_shape,
        in_specs=in_specs,
        out_specs=[WHOLE] * len(out_shape) if many else WHOLE,
        scratch_shapes=scratch,
        compiler_params=pltpu.CompilerParams(vmem_limit_bytes=VMEM_BYTES),
        cost_estimate=pl.CostEstimate(flops=flops, bytes_accessed=moved, transcendentals=0),
        name=name,
    )


def f32(*shape):
    return jax.ShapeDtypeStruct(shape, jnp.float32)


def bf16(*shape):
    return jax.ShapeDtypeStruct(shape, jnp.bfloat16)


def put(held, owner, value, side):
    share = value.shape[1]
    if share >= side:
        per = share // side
        for piece in range(per):
            held[owner * per + piece] = value[:, piece * side : (piece + 1) * side]
    else:
        per = side // share
        for at in range(per):

            @pl.when(owner % per == at)
            def _():
                held[owner // per, :, at * share : (at + 1) * share] = value


def get(total, owner, out_ref, side):
    share = out_ref.shape[1]
    if share >= side:
        per = share // side
        for piece in range(per):
            out_ref[:, piece * side : (piece + 1) * side] = total[owner * per + piece].astype(out_ref.dtype)
    else:
        per = side // share
        for at in range(per):

            @pl.when(owner % per == at)
            def _():
                out_ref[...] = total[owner // per, :, at * share : (at + 1) * share].astype(out_ref.dtype)


def emit(total, out_refs, me, side):
    count = len(out_refs)
    for step, out_ref in enumerate(out_refs):
        get(total, lax.rem(me + step, count), out_ref, side)


def collect(held, piece_refs, me, side):
    count = len(piece_refs)
    for step, piece_ref in enumerate(piece_refs):
        put(held, lax.rem(me + count - step, count), piece_ref[...], side)


def group_of(g, source, target, dims, count, ids, held, tile_ref, total):
    tiles, width, _ = total.shape
    for lane in range(GROUP):
        slot = g * GROUP + lane
        give = jnp.where(slot < count, ids[target, slot], tiles - 1)
        term = lax.dot_general(
            held[ids[source, slot]], tile_ref[slot], dims, preferred_element_type=jnp.float32
        )
        if term.shape[0] > width:
            term = term[:width] + term[width:]
        total[give] += term


def groups(source, target, dims, count, ids, held, tile_ref, total):
    def step(g, carry):
        group_of(g, source, target, dims, count, ids, held, tile_ref, total)
        return carry

    last = tile_ref.shape[0] // GROUP
    lax.fori_loop(0, jnp.minimum((count + GROUP - 1) // GROUP, last), step, 0)


def first_body(n_in, n_out, ids, live, place, *refs):
    pieces, tile_ref, outs = refs[:n_in], refs[n_in], refs[n_in + 1 : n_in + 1 + n_out]
    keep, held, total, sems = refs[n_in + 1 + n_out :]
    slots, side, _ = tile_ref.shape
    loads = []
    for g in range(slots // GROUP):
        span = pl.ds(g * GROUP, GROUP)
        loads.append(pltpu.make_async_copy(tile_ref.at[span], keep.at[span], sems.at[g]))
        loads[-1].start()
    collect(held, pieces, place[0], side)
    total[...] = jnp.zeros_like(total)
    count = live[0]
    for g in range(slots // GROUP):
        loads[g].wait()

        @pl.when(g * GROUP < count)
        def _():
            group_of(g, 1, 0, NT, count, ids, held, keep, total)

    emit(total, outs, place[1], side)


def back_body(n_in, ids, live, place, *refs):
    pieces, tile_ref, outs, (held, total) = refs[:n_in], refs[n_in], refs[n_in + 1 : -2], refs[-2:]
    side = tile_ref.shape[1]
    collect(held, pieces, place[1], side)
    total[...] = jnp.zeros_like(total)
    groups(0, 1, NN, live[0], ids, held, tile_ref, total)
    emit(total, outs, place[0], side)


def next_body(n_in, ids, live, place, *refs):
    pieces, (scale_ref, tile_ref, out_ref, spread, held, total) = refs[:n_in], refs[n_in:]
    tiles, width, side = out_ref.shape
    collect(spread, pieces, place[0], side)
    for tile in range(spread.shape[0]):
        value = spread[tile] * scale_ref[:, tile * side : (tile + 1) * side]
        high = value.astype(jnp.bfloat16)
        held[tile, :width] = high
        held[tile, width:] = (value - high.astype(jnp.float32)).astype(jnp.bfloat16)
    total[...] = jnp.zeros_like(total)
    groups(1, 0, NT, live[0], ids, held, tile_ref, total)
    out_ref[...] = total[:tiles]


def add(refs):
    total = refs[0][...].astype(jnp.float32)
    for ref in refs[1:]:
        total = total + ref[...].astype(jnp.float32)
    return total


def start_body(place, panel_ref, degree_ref, out_ref):
    share = panel_ref.shape[1]
    at = pl.multiple_of(place[0] * share, 128)
    scale = 1.0 / jnp.sqrt(degree_ref[:, pl.ds(at, share)].astype(jnp.float32))
    out_ref[...] = (panel_ref[...] * scale).astype(out_ref.dtype)


def query_body(*refs):
    part_refs, scale_ref, out_ref = refs[:-2], refs[-2], refs[-1]
    out_ref[...] = (add(part_refs) * scale_ref[...]).astype(out_ref.dtype)


def lift_body(*refs):
    part_refs, scale_ref, lifted_ref = refs[:-2], refs[-2], refs[-1]
    lifted_ref[...] = add(part_refs) * scale_ref[...]


def lift_gram_body(*refs):
    part_refs, scale_ref, lifted_ref, gram_ref = refs[:-3], refs[-3], refs[-2], refs[-1]
    lifted = add(part_refs) * scale_ref[...]
    lifted_ref[...] = lifted
    gram_ref[...] = lax.dot_general(lifted, lifted, NT, precision=HIGH, preferred_element_type=jnp.float32)


def gram_body(*refs):
    total = jnp.zeros(refs[-1].shape, jnp.float32)
    for ref in refs[:-1]:
        total = total + lax.dot_general(
            ref[...], ref[...], NT, precision=HIGH, preferred_element_type=jnp.float32
        )
    refs[-1][...] = total


def sum_body(*refs):
    refs[-1][...] = add(refs[:-1])


def apply_body(n_in, place, *refs):
    grams, total_ref, outs, done = refs[:n_in], refs[n_in], refs[n_in + 1 : -1], refs[-1]
    tiles, _, side = total_ref.shape
    inverse = inverse_factor(add(grams))
    for tile in range(tiles):
        done[tile] = lax.dot_general(
            inverse, total_ref[tile], NN, precision=HIGH, preferred_element_type=jnp.float32
        )
    emit(done, outs, place[1], side)


def finish_body(after, *refs):
    grams, lifted_ref, out_ref = refs[:-2], refs[-2], refs[-1]
    out_ref[...] = (
        lax.dot_general(
            inverse_factor(add(grams)), lifted_ref[...], NN, precision=HIGH, preferred_element_type=jnp.float32
        )
        * after
    )


def permute(value, axis, step):
    count = lax.axis_size(axis)
    return lax.ppermute(value, axis, [(i, (i + step) % count) for i in range(count)])


def spread_to(value, axis):
    return [value] + [permute(value, axis, step) for step in range(1, lax.axis_size(axis))]


def deal(values, axis):
    return [values[0]] + [permute(value, axis, step) for step, value in enumerate(values[1:], 1)]


def shards(tiles, tile_ids, tile_count, query_degree, product_degree, panel):
    tile_set = tiles[0, 0]
    ids = tile_ids[0, 0]
    live = tile_count[0]
    slots, side, _ = tile_set.shape
    width, share = panel.shape
    queries, products = query_degree.shape[0], product_degree.shape[0]
    query_tiles, product_tiles = queries // side, products // side
    n_row, n_col = lax.axis_size("row"), lax.axis_size("col")
    row_at, col_at = lax.axis_index("row"), lax.axis_index("col")
    place = jnp.stack([row_at, col_at]).astype(jnp.int32)
    columns = queries // n_col
    work = dict(flops=2 * slots * width * side * side, moved=2 * slots * side * side)
    scaled = call(start_body, "start", [SCALARS, WHOLE, WHOLE], bf16(width, share))(
        place, panel, product_degree[None, :]
    )
    pieces = spread_to(scaled, "row")
    my_pscale = 1.0 / jnp.sqrt(
        lax.dynamic_slice_in_dim(product_degree, row_at * share, share).astype(jnp.float32)
    )[None, :]
    my_qscale = 1.0 / jnp.sqrt(
        lax.dynamic_slice_in_dim(query_degree, col_at * columns, columns).astype(jnp.float32)
    )[None, :]
    pscale = 1.0 / jnp.sqrt(product_degree.astype(jnp.float32))[None, :]
    root_count = math.sqrt(products * n_col)
    sum_shapes = [f32(width, columns)] + [bf16(width, columns)] * (n_col - 1)
    query_scratch = pltpu.VMEM((query_tiles + 1, width, side), jnp.float32)
    product_scratch = pltpu.VMEM((product_tiles + 1, width, side), jnp.float32)
    for iteration in range(ITERS):
        if iteration == 0:
            *sums, tile_set = call(
                functools.partial(first_body, n_row, n_col),
                "forward",
                [SCALARS] * 3 + [WHOLE] * n_row + [AWAY],
                [*sum_shapes, bf16(slots, side, side)],
                [
                    pltpu.VMEM((product_tiles, width, side), jnp.bfloat16),
                    query_scratch,
                    pltpu.SemaphoreType.DMA((slots // GROUP,)),
                ],
                **work,
            )(ids, live, place, *pieces, tile_set)
        else:
            pieces = spread_to(lifted, "row")
            gram = call(gram_body, "gram", [WHOLE] * n_row, f32(width, width))(*pieces)
            grams = spread_to(gram, "col")
            total = call(
                functools.partial(next_body, n_row),
                "forward",
                [SCALARS] * 3 + [WHOLE] * (n_row + 2),
                f32(query_tiles, width, side),
                [
                    pltpu.VMEM((product_tiles, width, side), jnp.float32),
                    pltpu.VMEM((product_tiles, 2 * width, side), jnp.bfloat16),
                    query_scratch,
                ],
                **work,
            )(ids, live, place, *pieces, pscale, tile_set)
            sums = call(
                functools.partial(apply_body, n_col),
                "apply",
                [SCALARS] + [WHOLE] * (n_col + 1),
                sum_shapes,
                [pltpu.VMEM((query_tiles, width, side), jnp.float32)],
            )(place, *grams, total)
        parts = deal(sums, "col")
        rounded = call(query_body, "query", [WHOLE] * (n_col + 1), bf16(width, columns))(*parts, my_qscale)
        pieces = spread_to(rounded, "col")
        sums = call(
            functools.partial(back_body, n_col),
            "backward",
            [SCALARS] * 3 + [WHOLE] * (n_col + 1),
            [f32(width, share)] * n_row,
            [pltpu.VMEM((query_tiles, width, side), jnp.bfloat16), product_scratch],
            **work,
        )(ids, live, place, *pieces, tile_set)
        parts = deal(sums, "row")
        if iteration < ITERS - 1:
            lifted = call(lift_body, "lift", [WHOLE] * (n_row + 1), f32(width, share))(*parts, my_pscale)
    lifted, gram = call(
        lift_gram_body, "lift", [WHOLE] * (n_row + 1), [f32(width, share), f32(width, width)]
    )(*parts, my_pscale)
    gram = call(sum_body, "sum", [WHOLE] * n_row, f32(width, width))(*spread_to(gram, "row"))
    return call(
        functools.partial(finish_body, root_count), "finish", [WHOLE] * (n_col + 1), f32(width, share)
    )(*spread_to(gram, "col"), lifted)


def solution(mesh):
    in_specs = (
        P("row", "col", None, None, None),
        P("row", "col", None, None),
        P("row", "col"),
        P("row"),
        P("col"),
        P(None, ("col", "row")),
    )
    out_specs = P(None, ("col", "row"))
    return jax.shard_map(shards, mesh=mesh, in_specs=in_specs, out_specs=out_specs, check_vma=False)
```

```python
import functools
import math

import jax
import jax.numpy as jnp
from jax import lax
from jax.experimental import pallas as pl
from jax.experimental.pallas import tpu as pltpu
from jax.sharding import PartitionSpec as P

ITERS = 2
GROUP = 8
PANEL_STEP = 4
HIGH = lax.Precision.HIGHEST
VMEM_BYTES = 12 * 1024 * 1024
NT = (((1,), (1,)), ((), ()))
NN = (((1,), (0,)), ((), ()))

def inverse_factor(gram):
    width = gram.shape[0]
    rows = lax.broadcasted_iota(jnp.int32, (width, width), 0)
    cols = lax.broadcasted_iota(jnp.int32, (width, width), 1)
    work = jnp.concatenate([gram, (rows == cols).astype(jnp.float32)], axis=1)
    done = []
    for first in range(0, width, PANEL_STEP):
        base = first // 8 * 8
        height = width - base
        ids = lax.broadcasted_iota(jnp.int32, (height, 2 * width), 0) + base
        columns = [
            jnp.broadcast_to(work[:, first + j : first + j + 1], (height, 2 * width))
            for j in range(PANEL_STEP)
        ]
        for j in range(PANEL_STEP):
            k = first + j
            at = k - base
            pivot = columns[j][at : at + 1, :]
            factor = jnp.where(ids > k, columns[j] * (1.0 / pivot), 0.0)
            row = work[at : at + 1, :]
            done.append(row * lax.rsqrt(pivot))
            work = work - factor * row
            for later in range(j + 1, PANEL_STEP):
                columns[later] = columns[later] - factor * columns[later][at : at + 1, :]
        after = (first + PANEL_STEP) // 8 * 8
        if after > base:
            work = work[after - base :, :]
    return jnp.concatenate(done, axis=0)[:, width:]

WHOLE = pl.BlockSpec(memory_space=pltpu.VMEM)
SCALARS = pl.BlockSpec(memory_space=pltpu.SMEM)
AWAY = pl.BlockSpec(memory_space=pltpu.MemorySpace.HBM)


def call(body, name, in_specs, out_shape, scratch=(), flops=0, moved=0):
    many = isinstance(out_shape, (tuple, list))
    return pl.pallas_call(
        body,
        out_shape=out_shape,
        in_specs=in_specs,
        out_specs=[WHOLE] * len(out_shape) if many else WHOLE,
        scratch_shapes=scratch,
        compiler_params=pltpu.CompilerParams(vmem_limit_bytes=VMEM_BYTES),
        cost_estimate=pl.CostEstimate(flops=flops, bytes_accessed=moved, transcendentals=0),
        name=name,
    )


def in_hbm(value):
    return pltpu.with_memory_space_constraint(value, pltpu.MemorySpace.HBM)


def f32(*shape):
    return jax.ShapeDtypeStruct(shape, jnp.float32)


def bf16(*shape):
    return jax.ShapeDtypeStruct(shape, jnp.bfloat16)


def put(held, owner, value, side):
    share = value.shape[1]
    if share >= side:
        per = share // side
        for piece in range(per):
            held[owner * per + piece] = value[:, piece * side : (piece + 1) * side]
    else:
        per = side // share
        for at in range(per):

            @pl.when(owner % per == at)
            def _():
                held[owner // per, :, at * share : (at + 1) * share] = value


def get(total, owner, out_ref, side):
    share = out_ref.shape[1]
    if share >= side:
        per = share // side
        for piece in range(per):
            out_ref[:, piece * side : (piece + 1) * side] = total[owner * per + piece].astype(out_ref.dtype)
    else:
        per = side // share
        for at in range(per):

            @pl.when(owner % per == at)
            def _():
                out_ref[...] = total[owner // per, :, at * share : (at + 1) * share].astype(out_ref.dtype)


def emit(total, out_refs, me, side):
    for step, out_ref in enumerate(out_refs):
        get(total, lax.rem(me + step, len(out_refs)), out_ref, side)


def emit_pairs(total, mine_ref, other_ref, me, side):
    chips = mine_ref.shape[0]
    for step in range(chips):
        chip = lax.rem(me // 2 + step, chips)
        get(total, 2 * chip + me % 2, mine_ref.at[step], side)
        get(total, 2 * chip + 1 - me % 2, other_ref.at[step], side)


def collect(held, piece_refs, me, side):
    count = len(piece_refs)
    for step, piece_ref in enumerate(piece_refs):
        put(held, lax.rem(me + count - step, count), piece_ref[...], side)


def collect_pairs(held, mine_ref, other_ref, me, side):
    chips = mine_ref.shape[0]
    for step in range(chips):
        chip = lax.rem(me // 2 + chips - step, chips)
        put(held, 2 * chip + me % 2, mine_ref[step], side)
        put(held, 2 * chip + 1 - me % 2, other_ref[step], side)


def group_of(g, source, target, dims, count, ids, held, tile_ref, total):
    tiles, width, _ = total.shape
    for lane in range(GROUP):
        slot = g * GROUP + lane
        give = jnp.where(slot < count, ids[target, slot], tiles - 1)
        term = lax.dot_general(
            held[ids[source, slot]], tile_ref[slot], dims, preferred_element_type=jnp.float32
        )
        if term.shape[0] > width:
            term = term[:width] + term[width:]
        total[give] += term


def groups(source, target, dims, count, ids, held, tile_ref, total):
    def step(g, carry):
        group_of(g, source, target, dims, count, ids, held, tile_ref, total)
        return carry

    last = tile_ref.shape[0] // GROUP
    lax.fori_loop(0, jnp.minimum((count + GROUP - 1) // GROUP, last), step, 0)


def first_body(n_in, ids, live, place, *refs):
    pieces, (tile_ref, mine_ref, other_ref, keep, held, total, sems) = refs[:n_in], refs[n_in:]
    slots, side, _ = tile_ref.shape
    loads = []
    for g in range(slots // GROUP):
        span = pl.ds(g * GROUP, GROUP)
        loads.append(pltpu.make_async_copy(tile_ref.at[span], keep.at[span], sems.at[g]))
        loads[-1].start()
    collect(held, pieces, place[0], side)
    total[...] = jnp.zeros_like(total)
    count = live[0]
    for g in range(slots // GROUP):
        loads[g].wait()

        @pl.when(g * GROUP < count)
        def _():
            group_of(g, 1, 0, NT, count, ids, held, keep, total)

    emit_pairs(total, mine_ref, other_ref, place[1], side)


def back_body(ids, live, place, here_ref, there_ref, tile_ref, *refs):
    out_refs, (held, total) = refs[:-2], refs[-2:]
    side = tile_ref.shape[1]
    collect_pairs(held, here_ref, there_ref, place[1], side)
    total[...] = jnp.zeros_like(total)
    groups(0, 1, NN, live[0], ids, held, tile_ref, total)
    emit(total, out_refs, place[0], side)


def next_body(n_in, ids, live, place, *refs):
    pieces, (scale_ref, tile_ref, out_ref, spread, held, total) = refs[:n_in], refs[n_in:]
    tiles, width, side = out_ref.shape
    collect(spread, pieces, place[0], side)
    for tile in range(spread.shape[0]):
        value = spread[tile] * scale_ref[:, tile * side : (tile + 1) * side]
        high = value.astype(jnp.bfloat16)
        held[tile, :width] = high
        held[tile, width:] = (value - high.astype(jnp.float32)).astype(jnp.bfloat16)
    total[...] = jnp.zeros_like(total)
    groups(1, 0, NT, live[0], ids, held, tile_ref, total)
    out_ref[...] = total[:tiles]


def add(refs):
    total = refs[0][...].astype(jnp.float32)
    for ref in refs[1:]:
        total = total + ref[...].astype(jnp.float32)
    return total


def start_body(place, panel_ref, degree_ref, out_ref, held, degrees, sems):
    share = panel_ref.shape[1]
    at = pl.multiple_of(place[0] * share, 128)
    loads = [
        pltpu.make_async_copy(degree_ref, degrees, sems.at[0]),
        pltpu.make_async_copy(panel_ref, held, sems.at[1]),
    ]
    for load in loads:
        load.start()
    for load in loads:
        load.wait()
    scale = 1.0 / jnp.sqrt(degrees[:, pl.ds(at, share)].astype(jnp.float32))
    out_ref[...] = (held[...] * scale).astype(out_ref.dtype)


def scales_body(place, product_ref, query_ref, my_product_ref, product_out, my_query_ref):
    product_out[...] = 1.0 / jnp.sqrt(product_ref[...].astype(jnp.float32))
    share = my_product_ref.shape[1]
    at = pl.multiple_of(place[0] * share, 128)
    my_product_ref[...] = product_out[:, pl.ds(at, share)]
    columns = my_query_ref.shape[1]
    if columns % 128 == 0:
        at = pl.multiple_of(place[1] * columns, 128)
        my_query_ref[...] = 1.0 / jnp.sqrt(query_ref[:, pl.ds(at, columns)].astype(jnp.float32))
    else:
        for step in range(query_ref.shape[1] // columns):

            @pl.when(place[1] == step)
            def _():
                degree = query_ref[:, step * columns : (step + 1) * columns]
                my_query_ref[...] = 1.0 / jnp.sqrt(degree.astype(jnp.float32))


def pair_body(mine_ref, got_ref, *outs):
    for step, out_ref in enumerate(outs):
        out_ref[...] = (mine_ref[step] + got_ref[step]).astype(out_ref.dtype)


def join_body(*refs):
    for step, ref in enumerate(refs[:-1]):
        refs[-1][step] = ref[...]


def query_body(*refs):
    part_refs, scale_ref, out_ref = refs[:-2], refs[-2], refs[-1]
    out_ref[...] = (add(part_refs) * scale_ref[...]).astype(out_ref.dtype)


def lift_body(*refs):
    part_refs, scale_ref, lifted_ref = refs[:-2], refs[-2], refs[-1]
    lifted_ref[...] = add(part_refs) * scale_ref[...]


def lift_gram_body(*refs):
    part_refs, scale_ref, lifted_ref, gram_ref = refs[:-3], refs[-3], refs[-2], refs[-1]
    lifted = add(part_refs) * scale_ref[...]
    lifted_ref[...] = lifted
    gram_ref[...] = lax.dot_general(lifted, lifted, NT, precision=HIGH, preferred_element_type=jnp.float32)


def gram_body(*refs):
    total = jnp.zeros(refs[-1].shape, jnp.float32)
    for ref in refs[:-1]:
        total = total + lax.dot_general(
            ref[...], ref[...], NT, precision=HIGH, preferred_element_type=jnp.float32
        )
    refs[-1][...] = total


def sum_body(*refs):
    refs[-1][...] = add(refs[:-1])


def apply_body(n_in, place, *refs):
    grams, (total_ref, mine_ref, other_ref, done) = refs[:n_in], refs[n_in:]
    tiles, _, side = total_ref.shape
    inverse = inverse_factor(add(grams))
    for tile in range(tiles):
        done[tile] = lax.dot_general(
            inverse, total_ref[tile], NN, precision=HIGH, preferred_element_type=jnp.float32
        )
    emit_pairs(done, mine_ref, other_ref, place[1], side)


def finish_body(after, *refs):
    grams, lifted_ref, out_ref = refs[:-2], refs[-2], refs[-1]
    out_ref[...] = (
        lax.dot_general(
            inverse_factor(add(grams)), lifted_ref[...], NN, precision=HIGH, preferred_element_type=jnp.float32
        )
        * after
    )


def permute(value, axis, step):
    count = lax.axis_size(axis)
    return lax.ppermute(value, axis, [(i, (i + step) % count) for i in range(count)])


def swap(value):
    return lax.ppermute(value, "col", [(i, i ^ 1) for i in range(lax.axis_size("col"))])


def spread_to(value, axis, stride=1):
    return [value] + [permute(value, axis, step) for step in range(stride, lax.axis_size(axis), stride)]


def deal(values, axis, stride=1):
    return [values[0]] + [permute(value, axis, step * stride) for step, value in enumerate(values[1:], 1)]


def gram_over_col(gram):
    return spread_to(add_up(gram, swap(gram)), "col", 2)


def add_up(*values):
    return call(sum_body, "sum", [WHOLE] * len(values), f32(*values[0].shape))(*values)


def shards(tiles, tile_ids, tile_count, query_degree, product_degree, panel):
    tile_set = tiles[0, 0]
    ids = tile_ids[0, 0]
    live = tile_count[0]
    slots, side, _ = tile_set.shape
    width, share = panel.shape
    queries, products = query_degree.shape[0], product_degree.shape[0]
    query_tiles, product_tiles = queries // side, products // side
    n_row, n_col = lax.axis_size("row"), lax.axis_size("col")
    chips = n_col // 2
    place = jnp.stack([lax.axis_index("row"), lax.axis_index("col")]).astype(jnp.int32)
    columns = queries // n_col
    work = dict(flops=2 * slots * width * side * side, moved=2 * slots * side * side)
    scaled = call(
        start_body,
        "start",
        [SCALARS, AWAY, AWAY],
        bf16(width, share),
        [
            pltpu.VMEM((width, share), jnp.float32),
            pltpu.VMEM((1, products), jnp.int32),
            pltpu.SemaphoreType.DMA((2,)),
        ],
    )(place, in_hbm(panel), in_hbm(product_degree[None, :]))
    pieces = spread_to(scaled, "row")
    my_pscale, pscale, my_qscale = call(
        scales_body, "scales", [SCALARS, WHOLE, WHOLE], [f32(1, share), f32(1, products), f32(1, columns)]
    )(place, product_degree[None, :], query_degree[None, :])
    root_count = math.sqrt(products * n_col)
    half_shapes = [f32(chips, width, columns)] * 2
    query_scratch = pltpu.VMEM((query_tiles + 1, width, side), jnp.float32)
    product_scratch = pltpu.VMEM((product_tiles + 1, width, side), jnp.float32)
    for iteration in range(ITERS):
        if iteration == 0:
            mine, other, tile_set = call(
                functools.partial(first_body, n_row),
                "forward",
                [SCALARS] * 3 + [WHOLE] * n_row + [AWAY],
                [*half_shapes, pltpu.VMEM((slots, side, side), jnp.bfloat16)],
                [
                    pltpu.VMEM((product_tiles, width, side), jnp.bfloat16),
                    query_scratch,
                    pltpu.SemaphoreType.DMA((slots // GROUP,)),
                ],
                **work,
            )(ids, live, place, *pieces, in_hbm(tile_set))
            tile_set = pltpu.with_memory_space_constraint(tile_set, pltpu.VMEM)
        else:
            pieces = spread_to(lifted, "row")
            gram = call(gram_body, "gram", [WHOLE] * n_row, f32(width, width))(*pieces)
            grams = gram_over_col(gram)
            total = call(
                functools.partial(next_body, n_row),
                "forward",
                [SCALARS] * 3 + [WHOLE] * (n_row + 2),
                f32(query_tiles, width, side),
                [
                    pltpu.VMEM((product_tiles, width, side), jnp.float32),
                    pltpu.VMEM((product_tiles, 2 * width, side), jnp.bfloat16),
                    query_scratch,
                ],
                **work,
            )(ids, live, place, *pieces, pscale, tile_set)
            mine, other = call(
                functools.partial(apply_body, chips),
                "apply",
                [SCALARS] + [WHOLE] * (chips + 1),
                half_shapes,
                [pltpu.VMEM((query_tiles, width, side), jnp.float32)],
            )(place, *grams, total)
        sums = call(
            pair_body, "pair", [WHOLE] * 2, [f32(width, columns)] + [bf16(width, columns)] * (chips - 1)
        )(mine, swap(other))
        parts = deal(sums, "col", 2)
        rounded = call(query_body, "query", [WHOLE] * (chips + 1), bf16(width, columns))(*parts, my_qscale)
        here = call(join_body, "join", [WHOLE] * chips, bf16(chips, width, columns))(
            *spread_to(rounded, "col", 2)
        )
        sums = call(
            back_body,
            "backward",
            [SCALARS] * 3 + [WHOLE] * 3,
            [f32(width, share)] * n_row,
            [pltpu.VMEM((query_tiles, width, side), jnp.bfloat16), product_scratch],
            **work,
        )(ids, live, place, here, swap(here), tile_set)
        parts = deal(sums, "row")
        if iteration < ITERS - 1:
            lifted = call(lift_body, "lift", [WHOLE] * (n_row + 1), f32(width, share))(*parts, my_pscale)
    lifted, gram = call(
        lift_gram_body, "lift", [WHOLE] * (n_row + 1), [f32(width, share), f32(width, width)]
    )(*parts, my_pscale)
    grams = gram_over_col(add_up(*spread_to(gram, "row")))
    return call(
        functools.partial(finish_body, root_count), "finish", [WHOLE] * (chips + 1), f32(width, share)
    )(*grams, lifted)


def solution(mesh):
    in_specs = (
        P("row", "col", None, None, None),
        P("row", "col", None, None),
        P("row", "col"),
        P("row"),
        P("col"),
        P(None, ("col", "row")),
    )
    out_specs = P(None, ("col", "row"))
    return jax.shard_map(shards, mesh=mesh, in_specs=in_specs, out_specs=out_specs, check_vma=False)
```

```python
import functools
import math

import jax
import jax.numpy as jnp
from jax import lax
from jax.experimental import pallas as pl
from jax.experimental.pallas import tpu as pltpu
from jax.sharding import PartitionSpec as P

ITERS = 2
GROUP = 8
PANEL_STEP = 8
HIGH = lax.Precision.HIGHEST
VMEM_BYTES = 12 * 1024 * 1024
NT = (((1,), (1,)), ((), ()))
NN = (((1,), (0,)), ((), ()))

def inverse_factor(gram):
    width = gram.shape[0]
    rows = lax.broadcasted_iota(jnp.int32, (width, width), 0)
    cols = lax.broadcasted_iota(jnp.int32, (width, width), 1)
    work = jnp.concatenate([gram, (rows == cols).astype(jnp.float32)], axis=1)
    done = []
    for first in range(0, width, PANEL_STEP):
        base = first // 8 * 8
        height = width - base
        ids = lax.broadcasted_iota(jnp.int32, (height, 2 * width), 0) + base
        columns = [
            jnp.broadcast_to(work[:, first + j : first + j + 1], (height, 2 * width))
            for j in range(PANEL_STEP)
        ]
        for j in range(PANEL_STEP):
            k = first + j
            at = k - base
            pivot = columns[j][at : at + 1, :]
            factor = jnp.where(ids > k, columns[j] * (1.0 / pivot), 0.0)
            row = work[at : at + 1, :]
            done.append(row * lax.rsqrt(pivot))
            work = work - factor * row
            for later in range(j + 1, PANEL_STEP):
                columns[later] = columns[later] - factor * columns[later][at : at + 1, :]
        after = (first + PANEL_STEP) // 8 * 8
        if after > base:
            work = work[after - base :, :]
    return jnp.concatenate(done, axis=0)[:, width:]

WHOLE = pl.BlockSpec(memory_space=pltpu.VMEM)
SCALARS = pl.BlockSpec(memory_space=pltpu.SMEM)
AWAY = pl.BlockSpec(memory_space=pltpu.MemorySpace.HBM)


def call(body, name, in_specs, out_shape, scratch=(), flops=0, moved=0):
    many = isinstance(out_shape, (tuple, list))
    return pl.pallas_call(
        body,
        out_shape=out_shape,
        in_specs=in_specs,
        out_specs=[WHOLE] * len(out_shape) if many else WHOLE,
        scratch_shapes=scratch,
        compiler_params=pltpu.CompilerParams(vmem_limit_bytes=VMEM_BYTES),
        cost_estimate=pl.CostEstimate(flops=flops, bytes_accessed=moved, transcendentals=0),
        name=name,
    )


def in_hbm(value):
    return pltpu.with_memory_space_constraint(value, pltpu.MemorySpace.HBM)


def f32(*shape):
    return jax.ShapeDtypeStruct(shape, jnp.float32)


def bf16(*shape):
    return jax.ShapeDtypeStruct(shape, jnp.bfloat16)


def put(held, owner, value, side):
    share = value.shape[1]
    if share >= side:
        per = share // side
        for piece in range(per):
            held[owner * per + piece] = value[:, piece * side : (piece + 1) * side]
    else:
        per = side // share
        for at in range(per):

            @pl.when(owner % per == at)
            def _():
                held[owner // per, :, at * share : (at + 1) * share] = value


def get(total, owner, out_ref, side):
    share = out_ref.shape[1]
    if share >= side:
        per = share // side
        for piece in range(per):
            out_ref[:, piece * side : (piece + 1) * side] = total[owner * per + piece].astype(out_ref.dtype)
    else:
        per = side // share
        for at in range(per):

            @pl.when(owner % per == at)
            def _():
                out_ref[...] = total[owner // per, :, at * share : (at + 1) * share].astype(out_ref.dtype)


def emit(total, out_refs, me, side):
    for step, out_ref in enumerate(out_refs):
        get(total, me ^ step, out_ref, side)


def emit_pairs(total, mine_ref, other_ref, me, side):
    for step in range(mine_ref.shape[0]):
        get(total, me ^ (2 * step), mine_ref.at[step], side)
        get(total, me ^ (2 * step + 1), other_ref.at[step], side)


def collect(held, piece_refs, me, side):
    for step, piece_ref in enumerate(piece_refs):
        put(held, me ^ step, piece_ref[...], side)


def collect_pairs(held, mine_ref, other_ref, me, side):
    for step in range(mine_ref.shape[0]):
        put(held, me ^ (2 * step), mine_ref[step], side)
        put(held, me ^ (2 * step + 1), other_ref[step], side)


def group_of(g, source, target, dims, count, ids, held, tile_ref, total):
    tiles, width, _ = total.shape
    for lane in range(GROUP):
        slot = g * GROUP + lane
        give = jnp.where(slot < count, ids[target, slot], tiles - 1)
        term = lax.dot_general(
            held[ids[source, slot]], tile_ref[slot], dims, preferred_element_type=jnp.float32
        )
        if term.shape[0] > width:
            term = term[:width] + term[width:]
        total[give] += term


def groups(source, target, dims, count, ids, held, tile_ref, total):
    def step(g, carry):
        group_of(g, source, target, dims, count, ids, held, tile_ref, total)
        return carry

    last = tile_ref.shape[0] // GROUP
    lax.fori_loop(0, jnp.minimum((count + GROUP - 1) // GROUP, last), step, 0)


def first_body(n_in, ids, live, place, *refs):
    pieces, (tile_ref, mine_ref, other_ref, held, total) = refs[:n_in], refs[n_in:]
    side = tile_ref.shape[1]
    collect(held, pieces, place[0], side)
    total[...] = jnp.zeros_like(total)
    groups(1, 0, NT, live[0], ids, held, tile_ref, total)
    emit_pairs(total, mine_ref, other_ref, place[1], side)


def back_body(ids, live, place, here_ref, there_ref, tile_ref, *refs):
    out_refs, (held, total) = refs[:-2], refs[-2:]
    side = tile_ref.shape[1]
    collect_pairs(held, here_ref, there_ref, place[1], side)
    total[...] = jnp.zeros_like(total)
    groups(0, 1, NN, live[0], ids, held, tile_ref, total)
    emit(total, out_refs, place[0], side)


def next_body(n_in, ids, live, place, *refs):
    pieces, (scale_ref, tile_ref, out_ref, spread, held, total) = refs[:n_in], refs[n_in:]
    tiles, width, side = out_ref.shape
    collect(spread, pieces, place[0], side)
    for tile in range(spread.shape[0]):
        value = spread[tile] * scale_ref[:, tile * side : (tile + 1) * side]
        high = value.astype(jnp.bfloat16)
        held[tile, :width] = high
        held[tile, width:] = (value - high.astype(jnp.float32)).astype(jnp.bfloat16)
    total[...] = jnp.zeros_like(total)
    groups(1, 0, NT, live[0], ids, held, tile_ref, total)
    out_ref[...] = total[:tiles]


def add(refs):
    total = refs[0][...].astype(jnp.float32)
    for ref in refs[1:]:
        total = total + ref[...].astype(jnp.float32)
    return total


def start_body(place, panel_ref, degree_ref, out_ref, held, degrees, sems):
    share = panel_ref.shape[1]
    at = pl.multiple_of(place[0] * share, 128)
    loads = [
        pltpu.make_async_copy(degree_ref, degrees, sems.at[0]),
        pltpu.make_async_copy(panel_ref, held, sems.at[1]),
    ]
    for load in loads:
        load.start()
    for load in loads:
        load.wait()
    scale = 1.0 / jnp.sqrt(degrees[:, pl.ds(at, share)].astype(jnp.float32))
    out_ref[...] = (held[...] * scale).astype(out_ref.dtype)


def load_body(place, after_ref, tile_ref, product_ref, query_ref, keep, my_product_ref, product_out, my_query_ref, sem):
    load = pltpu.make_async_copy(tile_ref, keep, sem)
    load.start()
    product_out[...] = 1.0 / jnp.sqrt(product_ref[...].astype(jnp.float32))
    share = my_product_ref.shape[1]
    at = pl.multiple_of(place[0] * share, 128)
    my_product_ref[...] = product_out[:, pl.ds(at, share)]
    columns = my_query_ref.shape[1]
    if columns % 128 == 0:
        at = pl.multiple_of(place[1] * columns, 128)
        my_query_ref[...] = 1.0 / jnp.sqrt(query_ref[:, pl.ds(at, columns)].astype(jnp.float32))
    else:
        for step in range(query_ref.shape[1] // columns):

            @pl.when(place[1] == step)
            def _():
                degree = query_ref[:, step * columns : (step + 1) * columns]
                my_query_ref[...] = 1.0 / jnp.sqrt(degree.astype(jnp.float32))
    load.wait()


def pair_body(mine_ref, got_ref, *outs):
    for step, out_ref in enumerate(outs):
        out_ref[...] = (mine_ref[step] + got_ref[step]).astype(out_ref.dtype)


def join_body(*refs):
    for step, ref in enumerate(refs[:-1]):
        refs[-1][step] = ref[...]


def query_body(*refs):
    part_refs, scale_ref, out_ref = refs[:-2], refs[-2], refs[-1]
    out_ref[...] = (add(part_refs) * scale_ref[...]).astype(out_ref.dtype)


def lift_body(*refs):
    part_refs, scale_ref, lifted_ref, gram_ref = refs[:-3], refs[-3], refs[-2], refs[-1]
    lifted = add(part_refs) * scale_ref[...]
    lifted_ref[...] = lifted
    gram_ref[...] = lax.dot_general(lifted, lifted, NT, precision=HIGH, preferred_element_type=jnp.float32)


def sum_body(*refs):
    refs[-1][...] = add(refs[:-1])


def apply_body(place, gram_ref, total_ref, mine_ref, other_ref, done):
    tiles, _, side = total_ref.shape
    inverse = inverse_factor(gram_ref[...])
    for tile in range(tiles):
        done[tile] = lax.dot_general(
            inverse, total_ref[tile], NN, precision=HIGH, preferred_element_type=jnp.float32
        )
    emit_pairs(done, mine_ref, other_ref, place[1], side)


def finish_body(after, gram_ref, lifted_ref, out_ref):
    out_ref[...] = (
        lax.dot_general(
            inverse_factor(gram_ref[...]), lifted_ref[...], NN, precision=HIGH, preferred_element_type=jnp.float32
        )
        * after
    )


def swap(value, axis, step):
    return lax.ppermute(value, axis, [(i, i ^ step) for i in range(lax.axis_size(axis))])


def spread_to(value, axis, stride=1):
    return [value] + [swap(value, axis, step) for step in range(stride, lax.axis_size(axis), stride)]


def deal(values, axis, stride=1):
    return [values[0]] + [swap(value, axis, step * stride) for step, value in enumerate(values[1:], 1)]


def sum_everywhere(value):
    for axis in ("col", "row"):
        step = 1
        while step < lax.axis_size(axis):
            value = call(sum_body, "sum", [WHOLE] * 2, f32(*value.shape))(value, swap(value, axis, step))
            step *= 2
    return value


def shards(tiles, tile_ids, tile_count, query_degree, product_degree, panel):
    tile_set = tiles[0, 0]
    ids = tile_ids[0, 0]
    live = tile_count[0]
    slots, side, _ = tile_set.shape
    width, share = panel.shape
    queries, products = query_degree.shape[0], product_degree.shape[0]
    query_tiles, product_tiles = queries // side, products // side
    n_row, n_col = lax.axis_size("row"), lax.axis_size("col")
    chips = n_col // 2
    place = jnp.stack([lax.axis_index("row"), lax.axis_index("col")]).astype(jnp.int32)
    columns = queries // n_col
    work = dict(flops=2 * slots * width * side * side, moved=2 * slots * side * side)
    scaled = call(
        start_body,
        "start",
        [SCALARS, AWAY, AWAY],
        bf16(width, share),
        [
            pltpu.VMEM((width, share), jnp.float32),
            pltpu.VMEM((1, products), jnp.int32),
            pltpu.SemaphoreType.DMA((2,)),
        ],
    )(place, in_hbm(panel), in_hbm(product_degree[None, :]))
    pieces = spread_to(scaled, "row")
    tile_set, my_pscale, pscale, my_qscale = call(
        load_body,
        "load",
        [SCALARS, WHOLE, AWAY, WHOLE, WHOLE],
        [pltpu.VMEM((slots, side, side), jnp.bfloat16), f32(1, share), f32(1, products), f32(1, columns)],
        [pltpu.SemaphoreType.DMA],
        moved=4 * slots * side * side,
    )(place, scaled, in_hbm(tile_set), product_degree[None, :], query_degree[None, :])
    tile_set = pltpu.with_memory_space_constraint(tile_set, pltpu.VMEM)
    root_count = math.sqrt(products * n_col)
    half_shapes = [f32(chips, width, columns)] * 2
    query_scratch = pltpu.VMEM((query_tiles + 1, width, side), jnp.float32)
    product_scratch = pltpu.VMEM((product_tiles + 1, width, side), jnp.float32)
    for iteration in range(ITERS):
        if iteration == 0:
            mine, other = call(
                functools.partial(first_body, n_row),
                "forward",
                [SCALARS] * 3 + [WHOLE] * (n_row + 1),
                half_shapes,
                [pltpu.VMEM((product_tiles, width, side), jnp.bfloat16), query_scratch],
                **work,
            )(ids, live, place, *pieces, tile_set)
        else:
            pieces = spread_to(lifted, "row")
            total = call(
                functools.partial(next_body, n_row),
                "forward",
                [SCALARS] * 3 + [WHOLE] * (n_row + 2),
                f32(query_tiles, width, side),
                [
                    pltpu.VMEM((product_tiles, width, side), jnp.float32),
                    pltpu.VMEM((product_tiles, 2 * width, side), jnp.bfloat16),
                    query_scratch,
                ],
                **work,
            )(ids, live, place, *pieces, pscale, tile_set)
            mine, other = call(
                apply_body,
                "apply",
                [SCALARS] + [WHOLE] * 2,
                half_shapes,
                [pltpu.VMEM((query_tiles, width, side), jnp.float32)],
            )(place, sum_everywhere(gram), total)
        sums = call(
            pair_body, "pair", [WHOLE] * 2, [f32(width, columns)] + [bf16(width, columns)] * (chips - 1)
        )(mine, swap(other, "col", 1))
        parts = deal(sums, "col", 2)
        rounded = call(query_body, "query", [WHOLE] * (chips + 1), bf16(width, columns))(*parts, my_qscale)
        here = call(join_body, "join", [WHOLE] * chips, bf16(chips, width, columns))(
            *spread_to(rounded, "col", 2)
        )
        sums = call(
            back_body,
            "backward",
            [SCALARS] * 3 + [WHOLE] * 3,
            [f32(width, share)] * n_row,
            [pltpu.VMEM((query_tiles, width, side), jnp.bfloat16), product_scratch],
            **work,
        )(ids, live, place, here, swap(here, "col", 1), tile_set)
        lifted, gram = call(
            lift_body, "lift", [WHOLE] * (n_row + 1), [f32(width, share), f32(width, width)]
        )(*deal(sums, "row"), my_pscale)
    return call(
        functools.partial(finish_body, root_count), "finish", [WHOLE] * 2, f32(width, share)
    )(sum_everywhere(gram), lifted)


def solution(mesh):
    in_specs = (
        P("row", "col", None, None, None),
        P("row", "col", None, None),
        P("row", "col"),
        P("row"),
        P("col"),
        P(None, ("col", "row")),
    )
    out_specs = P(None, ("col", "row"))
    return jax.shard_map(shards, mesh=mesh, in_specs=in_specs, out_specs=out_specs, check_vma=False)
```

```python
import functools
import math

import jax
import jax.numpy as jnp
from jax import lax
from jax.experimental import pallas as pl
from jax.experimental.pallas import tpu as pltpu
from jax.sharding import PartitionSpec as P

ITERS = 2
GROUP = 8
PANEL_STEP = 8
HIGH = lax.Precision.HIGHEST
VMEM_BYTES = 12 * 1024 * 1024
NT = (((1,), (1,)), ((), ()))
NN = (((1,), (0,)), ((), ()))

def inverse_factor(gram):
    width = gram.shape[0]
    rows = lax.broadcasted_iota(jnp.int32, (width, width), 0)
    cols = lax.broadcasted_iota(jnp.int32, (width, width), 1)
    work = jnp.concatenate([gram, (rows == cols).astype(jnp.float32)], axis=1)
    done = []
    for first in range(0, width, PANEL_STEP):
        height = width - first
        columns = [
            jnp.broadcast_to(work[:, first + j : first + j + 1], (height, 2 * width))
            for j in range(PANEL_STEP)
        ]
        for j in range(PANEL_STEP):
            scale = lax.rsqrt(columns[j][j : j + 1, :])
            row = work[j : j + 1, :] * scale
            factor = columns[j] * scale
            done.append(row)
            for later in range(j + 1, PANEL_STEP):
                columns[later] = columns[later] - factor * (columns[later][j : j + 1, :] * scale)
            work = work - factor * row
        work = work[PANEL_STEP:, :]
    return jnp.concatenate(done, axis=0)[:, width:]


WHOLE = pl.BlockSpec(memory_space=pltpu.VMEM)
SCALARS = pl.BlockSpec(memory_space=pltpu.SMEM)
AWAY = pl.BlockSpec(memory_space=pltpu.MemorySpace.HBM)


def call(body, name, in_specs, out_shape, scratch=(), flops=0, moved=0):
    many = isinstance(out_shape, (tuple, list))
    return pl.pallas_call(
        body,
        out_shape=out_shape,
        in_specs=in_specs,
        out_specs=[WHOLE] * len(out_shape) if many else WHOLE,
        scratch_shapes=scratch,
        compiler_params=pltpu.CompilerParams(vmem_limit_bytes=VMEM_BYTES),
        cost_estimate=pl.CostEstimate(flops=flops, bytes_accessed=moved, transcendentals=0),
        name=name,
    )


def in_hbm(value):
    return pltpu.with_memory_space_constraint(value, pltpu.MemorySpace.HBM)


def f32(*shape):
    return jax.ShapeDtypeStruct(shape, jnp.float32)


def bf16(*shape):
    return jax.ShapeDtypeStruct(shape, jnp.bfloat16)


def put(held, owner, value, side):
    share = value.shape[1]
    if share >= side:
        per = share // side
        for piece in range(per):
            held[owner * per + piece] = value[:, piece * side : (piece + 1) * side]
    else:
        per = side // share
        for at in range(per):

            @pl.when(owner % per == at)
            def _():
                held[owner // per, :, at * share : (at + 1) * share] = value


def get(total, owner, out_ref, side):
    share = out_ref.shape[1]
    if share >= side:
        per = share // side
        for piece in range(per):
            out_ref[:, piece * side : (piece + 1) * side] = total[owner * per + piece].astype(out_ref.dtype)
    else:
        per = side // share
        for at in range(per):

            @pl.when(owner % per == at)
            def _():
                out_ref[...] = total[owner // per, :, at * share : (at + 1) * share].astype(out_ref.dtype)


def emit(total, out_refs, me, side):
    for step, out_ref in enumerate(out_refs):
        get(total, me ^ step, out_ref, side)


def emit_pairs(total, mine_ref, other_ref, me, side):
    for step in range(mine_ref.shape[0]):
        get(total, me ^ (2 * step), mine_ref.at[step], side)
        get(total, me ^ (2 * step + 1), other_ref.at[step], side)


def collect(held, piece_refs, me, side):
    for step, piece_ref in enumerate(piece_refs):
        put(held, me ^ step, piece_ref[...], side)


def collect_pairs(held, mine_ref, other_ref, me, side):
    for step in range(mine_ref.shape[0]):
        put(held, me ^ (2 * step), mine_ref[step], side)
        put(held, me ^ (2 * step + 1), other_ref[step], side)


def group_of(g, source, target, dims, count, ids, held, tile_ref, total):
    tiles, width, _ = total.shape
    for lane in range(GROUP):
        slot = g * GROUP + lane
        give = jnp.where(slot < count, ids[target, slot], tiles - 1)
        term = lax.dot_general(
            held[ids[source, slot]], tile_ref[slot], dims, preferred_element_type=jnp.float32
        )
        if term.shape[0] > width:
            term = term[:width] + term[width:]
        total[give] += term


def groups(source, target, dims, count, ids, held, tile_ref, total):
    def step(g, carry):
        group_of(g, source, target, dims, count, ids, held, tile_ref, total)
        return carry

    last = tile_ref.shape[0] // GROUP
    lax.fori_loop(0, jnp.minimum((count + GROUP - 1) // GROUP, last), step, 0)


def first_body(n_in, ids, live, place, *refs):
    pieces, (tile_ref, mine_ref, other_ref, held, total) = refs[:n_in], refs[n_in:]
    side = tile_ref.shape[1]
    collect(held, pieces, place[0], side)
    total[...] = jnp.zeros_like(total)
    groups(1, 0, NT, live[0], ids, held, tile_ref, total)
    emit_pairs(total, mine_ref, other_ref, place[1], side)


def back_body(ids, live, place, here_ref, there_ref, tile_ref, *refs):
    out_refs, (held, total) = refs[:-2], refs[-2:]
    side = tile_ref.shape[1]
    collect_pairs(held, here_ref, there_ref, place[1], side)
    total[...] = jnp.zeros_like(total)
    groups(0, 1, NN, live[0], ids, held, tile_ref, total)
    emit(total, out_refs, place[0], side)


def next_body(n_in, ids, live, place, *refs):
    pieces, (scale_ref, tile_ref, out_ref, spread, held, total) = refs[:n_in], refs[n_in:]
    tiles, width, side = out_ref.shape
    collect(spread, pieces, place[0], side)
    for tile in range(spread.shape[0]):
        value = spread[tile] * scale_ref[:, tile * side : (tile + 1) * side]
        high = value.astype(jnp.bfloat16)
        held[tile, :width] = high
        held[tile, width:] = (value - high.astype(jnp.float32)).astype(jnp.bfloat16)
    total[...] = jnp.zeros_like(total)
    groups(1, 0, NT, live[0], ids, held, tile_ref, total)
    out_ref[...] = total[:tiles]


def add(refs):
    total = refs[0][...].astype(jnp.float32)
    for ref in refs[1:]:
        total = total + ref[...].astype(jnp.float32)
    return total


def start_body(place, panel_ref, degree_ref, out_ref, held, degrees, sems):
    share = panel_ref.shape[1]
    at = pl.multiple_of(place[0] * share, 128)
    loads = [
        pltpu.make_async_copy(degree_ref, degrees, sems.at[0]),
        pltpu.make_async_copy(panel_ref, held, sems.at[1]),
    ]
    for load in loads:
        load.start()
    for load in loads:
        load.wait()
    scale = 1.0 / jnp.sqrt(degrees[:, pl.ds(at, share)].astype(jnp.float32))
    out_ref[...] = (held[...] * scale).astype(out_ref.dtype)


def load_body(place, after_ref, tile_ref, product_ref, query_ref, *refs):
    keep, my_product_ref, product_out, my_query_ref, degrees, counts, sems = refs
    loads = [
        pltpu.make_async_copy(product_ref, degrees, sems.at[0]),
        pltpu.make_async_copy(query_ref, counts, sems.at[1]),
        pltpu.make_async_copy(tile_ref, keep, sems.at[2]),
    ]
    for load in loads:
        load.start()
    loads[0].wait()
    product_out[...] = 1.0 / jnp.sqrt(degrees[...].astype(jnp.float32))
    share = my_product_ref.shape[1]
    at = pl.multiple_of(place[0] * share, 128)
    my_product_ref[...] = product_out[:, pl.ds(at, share)]
    loads[1].wait()
    columns = my_query_ref.shape[1]
    if columns % 128 == 0:
        at = pl.multiple_of(place[1] * columns, 128)
        my_query_ref[...] = 1.0 / jnp.sqrt(counts[:, pl.ds(at, columns)].astype(jnp.float32))
    else:
        for step in range(counts.shape[1] // columns):

            @pl.when(place[1] == step)
            def _():
                degree = counts[:, step * columns : (step + 1) * columns]
                my_query_ref[...] = 1.0 / jnp.sqrt(degree.astype(jnp.float32))
    loads[2].wait()


def pair_body(mine_ref, got_ref, *outs):
    for step, out_ref in enumerate(outs):
        out_ref[...] = (mine_ref[step] + got_ref[step]).astype(out_ref.dtype)


def join_body(*refs):
    for step, ref in enumerate(refs[:-1]):
        refs[-1][step] = ref[...]


def query_body(*refs):
    part_refs, scale_ref, out_ref = refs[:-2], refs[-2], refs[-1]
    out_ref[...] = (add(part_refs) * scale_ref[...]).astype(out_ref.dtype)


def lift_body(*refs):
    part_refs, scale_ref, lifted_ref, gram_ref = refs[:-3], refs[-3], refs[-2], refs[-1]
    lifted = add(part_refs) * scale_ref[...]
    lifted_ref[...] = lifted
    gram_ref[...] = lax.dot_general(lifted, lifted, NT, precision=HIGH, preferred_element_type=jnp.float32)


def gram_body(*refs):
    total = jnp.zeros(refs[-1].shape, jnp.float32)
    for ref in refs[:-1]:
        total = total + lax.dot_general(
            ref[...], ref[...], NT, precision=HIGH, preferred_element_type=jnp.float32
        )
    refs[-1][...] = total


def sum_body(*refs):
    refs[-1][...] = add(refs[:-1])


def apply_body(n_in, place, *refs):
    grams, (total_ref, mine_ref, other_ref, done) = refs[:n_in], refs[n_in:]
    tiles, _, side = total_ref.shape
    inverse = inverse_factor(add(grams))
    for tile in range(tiles):
        done[tile] = lax.dot_general(
            inverse, total_ref[tile], NN, precision=HIGH, preferred_element_type=jnp.float32
        )
    emit_pairs(done, mine_ref, other_ref, place[1], side)


def finish_body(after, *refs):
    grams, lifted_ref, out_ref = refs[:-2], refs[-2], refs[-1]
    out_ref[...] = (
        lax.dot_general(
            inverse_factor(add(grams)), lifted_ref[...], NN, precision=HIGH, preferred_element_type=jnp.float32
        )
        * after
    )


def swap(value, axis, step):
    return lax.ppermute(value, axis, [(i, i ^ step) for i in range(lax.axis_size(axis))])


def spread_to(value, axis, stride=1):
    return [value] + [swap(value, axis, step) for step in range(stride, lax.axis_size(axis), stride)]


def deal(values, axis, stride=1):
    return [values[0]] + [swap(value, axis, step * stride) for step, value in enumerate(values[1:], 1)]


def add_up(*values):
    return call(sum_body, "sum", [WHOLE] * len(values), f32(*values[0].shape))(*values)


def terms_over_col(gram):
    return spread_to(add_up(gram, swap(gram, "col", 1)), "col", 2)


def shards(tiles, tile_ids, tile_count, query_degree, product_degree, panel):
    tile_set = tiles[0, 0]
    ids = tile_ids[0, 0]
    live = tile_count[0]
    slots, side, _ = tile_set.shape
    width, share = panel.shape
    queries, products = query_degree.shape[0], product_degree.shape[0]
    query_tiles, product_tiles = queries // side, products // side
    n_row, n_col = lax.axis_size("row"), lax.axis_size("col")
    chips = n_col // 2
    place = jnp.stack([lax.axis_index("row"), lax.axis_index("col")]).astype(jnp.int32)
    columns = queries // n_col
    work = dict(flops=2 * slots * width * side * side, moved=2 * slots * side * side)
    scaled = call(
        start_body,
        "start",
        [SCALARS, AWAY, AWAY],
        bf16(width, share),
        [
            pltpu.VMEM((width, share), jnp.float32),
            pltpu.VMEM((1, products), jnp.int32),
            pltpu.SemaphoreType.DMA((2,)),
        ],
    )(place, in_hbm(panel), in_hbm(product_degree[None, :]))
    pieces = spread_to(scaled, "row")
    tile_set, my_pscale, pscale, my_qscale = call(
        load_body,
        "load",
        [SCALARS, WHOLE, AWAY, AWAY, AWAY],
        [pltpu.VMEM((slots, side, side), jnp.bfloat16), f32(1, share), f32(1, products), f32(1, columns)],
        [
            pltpu.VMEM((1, products), jnp.int32),
            pltpu.VMEM((1, queries), jnp.int32),
            pltpu.SemaphoreType.DMA((3,)),
        ],
        moved=4 * slots * side * side,
    )(place, scaled, in_hbm(tile_set), in_hbm(product_degree[None, :]), in_hbm(query_degree[None, :]))
    tile_set = pltpu.with_memory_space_constraint(tile_set, pltpu.VMEM)
    root_count = math.sqrt(products * n_col)
    half_shapes = [f32(chips, width, columns)] * 2
    query_scratch = pltpu.VMEM((query_tiles + 1, width, side), jnp.float32)
    product_scratch = pltpu.VMEM((product_tiles + 1, width, side), jnp.float32)
    for iteration in range(ITERS):
        if iteration == 0:
            mine, other = call(
                functools.partial(first_body, n_row),
                "forward",
                [SCALARS] * 3 + [WHOLE] * (n_row + 1),
                half_shapes,
                [pltpu.VMEM((product_tiles, width, side), jnp.bfloat16), query_scratch],
                **work,
            )(ids, live, place, *pieces, tile_set)
        else:
            pieces = spread_to(lifted, "row")
            gram = call(gram_body, "gram", [WHOLE] * n_row, f32(width, width))(*pieces)
            grams = terms_over_col(gram)
            total = call(
                functools.partial(next_body, n_row),
                "forward",
                [SCALARS] * 3 + [WHOLE] * (n_row + 2),
                f32(query_tiles, width, side),
                [
                    pltpu.VMEM((product_tiles, width, side), jnp.float32),
                    pltpu.VMEM((product_tiles, 2 * width, side), jnp.bfloat16),
                    query_scratch,
                ],
                **work,
            )(ids, live, place, *pieces, pscale, tile_set)
            mine, other = call(
                functools.partial(apply_body, chips),
                "apply",
                [SCALARS] + [WHOLE] * (chips + 1),
                half_shapes,
                [pltpu.VMEM((query_tiles, width, side), jnp.float32)],
            )(place, *grams, total)
        sums = call(
            pair_body, "pair", [WHOLE] * 2, [f32(width, columns)] + [bf16(width, columns)] * (chips - 1)
        )(mine, swap(other, "col", 1))
        parts = deal(sums, "col", 2)
        rounded = call(query_body, "query", [WHOLE] * (chips + 1), bf16(width, columns))(*parts, my_qscale)
        here = call(join_body, "join", [WHOLE] * chips, bf16(chips, width, columns))(
            *spread_to(rounded, "col", 2)
        )
        sums = call(
            back_body,
            "backward",
            [SCALARS] * 3 + [WHOLE] * 3,
            [f32(width, share)] * n_row,
            [pltpu.VMEM((query_tiles, width, side), jnp.bfloat16), product_scratch],
            **work,
        )(ids, live, place, here, swap(here, "col", 1), tile_set)
        lifted, gram = call(
            lift_body, "lift", [WHOLE] * (n_row + 1), [f32(width, share), f32(width, width)]
        )(*deal(sums, "row"), my_pscale)
    return call(
        functools.partial(finish_body, root_count), "finish", [WHOLE] * (chips + 1), f32(width, share)
    )(*terms_over_col(add_up(*spread_to(gram, "row"))), lifted)


def solution(mesh):
    in_specs = (
        P("row", "col", None, None, None),
        P("row", "col", None, None),
        P("row", "col"),
        P("row"),
        P("col"),
        P(None, ("col", "row")),
    )
    out_specs = P(None, ("col", "row"))
    return jax.shard_map(shards, mesh=mesh, in_specs=in_specs, out_specs=out_specs, check_vma=False)
```

```python
import functools
import math

import jax
import jax.numpy as jnp
from jax import lax
from jax.experimental import pallas as pl
from jax.experimental.pallas import tpu as pltpu
from jax.sharding import PartitionSpec as P

ITERS = 2
GROUP = 16
LOADS = 8
PANEL_STEP = 8
HIGH = lax.Precision.HIGHEST
VMEM_BYTES = 12 * 1024 * 1024
NT = (((1,), (1,)), ((), ()))
NN = (((1,), (0,)), ((), ()))

def inverse_factor(gram):
    width = gram.shape[0]
    rows = lax.broadcasted_iota(jnp.int32, (width, width), 0)
    cols = lax.broadcasted_iota(jnp.int32, (width, width), 1)
    work = jnp.concatenate([gram, (rows == cols).astype(jnp.float32)], axis=1)
    done = []
    for first in range(0, width, PANEL_STEP):
        height = width - first
        columns = [
            jnp.broadcast_to(work[:, first + j : first + j + 1], (height, 2 * width))
            for j in range(PANEL_STEP)
        ]
        for j in range(PANEL_STEP):
            scale = lax.rsqrt(columns[j][j : j + 1, :])
            row = work[j : j + 1, :] * scale
            factor = columns[j] * scale
            done.append(row)
            for later in range(j + 1, PANEL_STEP):
                columns[later] = columns[later] - factor * (columns[later][j : j + 1, :] * scale)
            work = work - factor * row
        work = work[PANEL_STEP:, :]
    return jnp.concatenate(done, axis=0)[:, width:]


WHOLE = pl.BlockSpec(memory_space=pltpu.VMEM)
SCALARS = pl.BlockSpec(memory_space=pltpu.SMEM)
AWAY = pl.BlockSpec(memory_space=pltpu.MemorySpace.HBM)


def call(body, name, in_specs, out_shape, scratch=(), flops=0, moved=0):
    many = isinstance(out_shape, (tuple, list))
    return pl.pallas_call(
        body,
        out_shape=out_shape,
        in_specs=in_specs,
        out_specs=[WHOLE] * len(out_shape) if many else WHOLE,
        scratch_shapes=scratch,
        compiler_params=pltpu.CompilerParams(vmem_limit_bytes=VMEM_BYTES),
        cost_estimate=pl.CostEstimate(flops=flops, bytes_accessed=moved, transcendentals=0),
        name=name,
    )


def in_hbm(value):
    return pltpu.with_memory_space_constraint(value, pltpu.MemorySpace.HBM)


def f32(*shape):
    return jax.ShapeDtypeStruct(shape, jnp.float32)


def bf16(*shape):
    return jax.ShapeDtypeStruct(shape, jnp.bfloat16)


def put(held, owner, value, side):
    share = value.shape[1]
    if share >= side:
        per = share // side
        for piece in range(per):
            held[owner * per + piece] = value[:, piece * side : (piece + 1) * side]
    else:
        per = side // share
        for at in range(per):

            @pl.when(owner % per == at)
            def _():
                held[owner // per, :, at * share : (at + 1) * share] = value


def get(total, owner, out_ref, side):
    share = out_ref.shape[1]
    if share >= side:
        per = share // side
        for piece in range(per):
            out_ref[:, piece * side : (piece + 1) * side] = total[owner * per + piece].astype(out_ref.dtype)
    else:
        per = side // share
        for at in range(per):

            @pl.when(owner % per == at)
            def _():
                out_ref[...] = total[owner // per, :, at * share : (at + 1) * share].astype(out_ref.dtype)


def emit(total, out_refs, me, side):
    count = len(out_refs)
    for at, out_ref in enumerate(out_refs):
        get(total, me ^ ((count - at) % count), out_ref, side)


def emit_pairs(total, mine_ref, other_ref, me, side):
    for step in range(mine_ref.shape[0]):
        get(total, me ^ (2 * step), mine_ref.at[step], side)
        get(total, me ^ (2 * step + 1), other_ref.at[step], side)


def collect(held, piece_refs, me, side):
    for step, piece_ref in enumerate(piece_refs):
        put(held, me ^ step, piece_ref[...], side)


def collect_pairs(held, mine_ref, other_ref, me, side):
    for step in range(mine_ref.shape[0]):
        put(held, me ^ (2 * step), mine_ref[step], side)
        put(held, me ^ (2 * step + 1), other_ref[step], side)


def group_of(g, source, target, dims, count, ids, held, tile_ref, total):
    tiles, width, _ = total.shape
    for lane in range(GROUP):
        slot = g * GROUP + lane
        give = jnp.where(slot < count, ids[target, slot], tiles - 1)
        term = lax.dot_general(
            held[ids[source, slot]], tile_ref[slot], dims, preferred_element_type=jnp.float32
        )
        if term.shape[0] > width:
            term = term[:width] + term[width:]
        total[give] += term


def groups(source, target, dims, count, ids, held, tile_ref, total):
    def step(g, carry):
        group_of(g, source, target, dims, count, ids, held, tile_ref, total)
        return carry

    last = tile_ref.shape[0] // GROUP
    lax.fori_loop(0, jnp.minimum((count + GROUP - 1) // GROUP, last), step, 0)


def first_body(n_in, ids, live, place, *refs):
    pieces, (tile_ref, mine_ref, other_ref, held, total) = refs[:n_in], refs[n_in:]
    side = tile_ref.shape[1]
    collect(held, pieces, place[0], side)
    total[...] = jnp.zeros_like(total)
    groups(1, 0, NT, live[0], ids, held, tile_ref, total)
    emit_pairs(total, mine_ref, other_ref, place[1], side)


def back_body(ids, live, place, here_ref, there_ref, tile_ref, *refs):
    out_refs, (held, total) = refs[:-2], refs[-2:]
    side = tile_ref.shape[1]
    collect_pairs(held, here_ref, there_ref, place[1], side)
    total[...] = jnp.zeros_like(total)
    groups(0, 1, NN, live[0], ids, held, tile_ref, total)
    emit(total, out_refs, place[0], side)


def next_body(n_in, ids, live, place, *refs):
    pieces, (scale_ref, tile_ref, out_ref, spread, held, total) = refs[:n_in], refs[n_in:]
    tiles, width, side = out_ref.shape
    collect(spread, pieces, place[0], side)
    for tile in range(spread.shape[0]):
        value = spread[tile] * scale_ref[:, tile * side : (tile + 1) * side]
        high = value.astype(jnp.bfloat16)
        held[tile, :width] = high
        held[tile, width:] = (value - high.astype(jnp.float32)).astype(jnp.bfloat16)
    total[...] = jnp.zeros_like(total)
    groups(1, 0, NT, live[0], ids, held, tile_ref, total)
    out_ref[...] = total[:tiles]


def add(refs):
    total = refs[0][...].astype(jnp.float32)
    for ref in refs[1:]:
        total = total + ref[...].astype(jnp.float32)
    return total


def start_body(place, panel_ref, degree_ref, out_ref, held, degrees, sems):
    share = panel_ref.shape[1]
    at = pl.multiple_of(place[0] * share, 128)
    loads = [
        pltpu.make_async_copy(degree_ref, degrees, sems.at[0]),
        pltpu.make_async_copy(panel_ref, held, sems.at[1]),
    ]
    for load in loads:
        load.start()
    for load in loads:
        load.wait()
    scale = 1.0 / jnp.sqrt(degrees[:, pl.ds(at, share)].astype(jnp.float32))
    out_ref[...] = (held[...] * scale).astype(out_ref.dtype)


def load_body(place, after_ref, tile_ref, product_ref, query_ref, *refs):
    keep, my_product_ref, product_out, my_query_ref, degrees, counts, sems = refs
    loads = [
        pltpu.make_async_copy(product_ref, degrees, sems.at[0]),
        pltpu.make_async_copy(query_ref, counts, sems.at[1]),
    ]
    part = tile_ref.shape[0] // LOADS
    for step in range(LOADS):
        span = pl.ds(step * part, part)
        loads.append(pltpu.make_async_copy(tile_ref.at[span], keep.at[span], sems.at[2 + step]))
    for load in loads:
        load.start()
    loads[0].wait()
    product_out[...] = 1.0 / jnp.sqrt(degrees[...].astype(jnp.float32))
    share = my_product_ref.shape[1]
    at = pl.multiple_of(place[0] * share, 128)
    my_product_ref[...] = product_out[:, pl.ds(at, share)]
    loads[1].wait()
    columns = my_query_ref.shape[1]
    if columns % 128 == 0:
        at = pl.multiple_of(place[1] * columns, 128)
        my_query_ref[...] = 1.0 / jnp.sqrt(counts[:, pl.ds(at, columns)].astype(jnp.float32))
    else:
        for step in range(counts.shape[1] // columns):

            @pl.when(place[1] == step)
            def _():
                degree = counts[:, step * columns : (step + 1) * columns]
                my_query_ref[...] = 1.0 / jnp.sqrt(degree.astype(jnp.float32))
    for load in loads[2:]:
        load.wait()


def pair_body(mine_ref, got_ref, *outs):
    count = len(outs)
    for at, out_ref in enumerate(outs):
        step = (count - at) % count
        out_ref[...] = (mine_ref[step] + got_ref[step]).astype(out_ref.dtype)


def join_body(*refs):
    for step, ref in enumerate(refs[:-1]):
        refs[-1][step] = ref[...]


def query_body(*refs):
    part_refs, scale_ref, out_ref = refs[:-2], refs[-2], refs[-1]
    out_ref[...] = (add(part_refs) * scale_ref[...]).astype(out_ref.dtype)


def lift_body(*refs):
    part_refs, scale_ref, lifted_ref, gram_ref = refs[:-3], refs[-3], refs[-2], refs[-1]
    lifted = add(part_refs) * scale_ref[...]
    lifted_ref[...] = lifted
    gram_ref[...] = lax.dot_general(lifted, lifted, NT, precision=HIGH, preferred_element_type=jnp.float32)


def gram_body(*refs):
    total = jnp.zeros(refs[-1].shape, jnp.float32)
    for ref in refs[:-1]:
        total = total + lax.dot_general(
            ref[...], ref[...], NT, precision=HIGH, preferred_element_type=jnp.float32
        )
    refs[-1][...] = total


def sum_body(*refs):
    refs[-1][...] = add(refs[:-1])


def apply_body(n_in, place, *refs):
    grams, (total_ref, mine_ref, other_ref, done) = refs[:n_in], refs[n_in:]
    tiles, _, side = total_ref.shape
    inverse = inverse_factor(add(grams))
    for tile in range(tiles):
        done[tile] = lax.dot_general(
            inverse, total_ref[tile], NN, precision=HIGH, preferred_element_type=jnp.float32
        )
    emit_pairs(done, mine_ref, other_ref, place[1], side)


def finish_body(after, *refs):
    grams, lifted_ref, out_ref = refs[:-2], refs[-2], refs[-1]
    out_ref[...] = (
        lax.dot_general(
            inverse_factor(add(grams)), lifted_ref[...], NN, precision=HIGH, preferred_element_type=jnp.float32
        )
        * after
    )


def swap(value, axis, step):
    return lax.ppermute(value, axis, [(i, i ^ step) for i in range(lax.axis_size(axis))])


def spread_to(value, axis, stride=1):
    return [value] + [swap(value, axis, step) for step in range(stride, lax.axis_size(axis), stride)]


def deal(values, axis, stride=1):
    count = len(values)
    return [values[0]] + [swap(value, axis, (count - at) * stride) for at, value in enumerate(values[1:], 1)]


def add_up(*values):
    return call(sum_body, "sum", [WHOLE] * len(values), f32(*values[0].shape))(*values)


def terms_over_col(gram):
    return spread_to(add_up(gram, swap(gram, "col", 1)), "col", 2)


def shards(tiles, tile_ids, tile_count, query_degree, product_degree, panel):
    tile_set = tiles[0, 0]
    ids = tile_ids[0, 0]
    live = tile_count[0]
    slots, side, _ = tile_set.shape
    width, share = panel.shape
    queries, products = query_degree.shape[0], product_degree.shape[0]
    query_tiles, product_tiles = queries // side, products // side
    n_row, n_col = lax.axis_size("row"), lax.axis_size("col")
    chips = n_col // 2
    place = jnp.stack([lax.axis_index("row"), lax.axis_index("col")]).astype(jnp.int32)
    columns = queries // n_col
    work = dict(flops=2 * slots * width * side * side, moved=2 * slots * side * side)
    scaled = call(
        start_body,
        "start",
        [SCALARS, AWAY, AWAY],
        bf16(width, share),
        [
            pltpu.VMEM((width, share), jnp.float32),
            pltpu.VMEM((1, products), jnp.int32),
            pltpu.SemaphoreType.DMA((2,)),
        ],
    )(place, in_hbm(panel), in_hbm(product_degree[None, :]))
    pieces = spread_to(scaled, "row")
    tile_set, my_pscale, pscale, my_qscale = call(
        load_body,
        "load",
        [SCALARS, WHOLE, AWAY, AWAY, AWAY],
        [pltpu.VMEM((slots, side, side), jnp.bfloat16), f32(1, share), f32(1, products), f32(1, columns)],
        [
            pltpu.VMEM((1, products), jnp.int32),
            pltpu.VMEM((1, queries), jnp.int32),
            pltpu.SemaphoreType.DMA((2 + LOADS,)),
        ],
        moved=4 * slots * side * side,
    )(place, scaled, in_hbm(tile_set), in_hbm(product_degree[None, :]), in_hbm(query_degree[None, :]))
    tile_set = pltpu.with_memory_space_constraint(tile_set, pltpu.VMEM)
    root_count = math.sqrt(products * n_col)
    half_shapes = [f32(chips, width, columns)] * 2
    query_scratch = pltpu.VMEM((query_tiles + 1, width, side), jnp.float32)
    product_scratch = pltpu.VMEM((product_tiles + 1, width, side), jnp.float32)
    for iteration in range(ITERS):
        if iteration == 0:
            mine, other = call(
                functools.partial(first_body, n_row),
                "forward",
                [SCALARS] * 3 + [WHOLE] * (n_row + 1),
                half_shapes,
                [pltpu.VMEM((product_tiles, width, side), jnp.bfloat16), query_scratch],
                **work,
            )(ids, live, place, *pieces, tile_set)
        else:
            pieces = spread_to(lifted, "row")
            gram = call(gram_body, "gram", [WHOLE] * n_row, f32(width, width))(*pieces)
            grams = terms_over_col(gram)
            total = call(
                functools.partial(next_body, n_row),
                "forward",
                [SCALARS] * 3 + [WHOLE] * (n_row + 2),
                f32(query_tiles, width, side),
                [
                    pltpu.VMEM((product_tiles, width, side), jnp.float32),
                    pltpu.VMEM((product_tiles, 2 * width, side), jnp.bfloat16),
                    query_scratch,
                ],
                **work,
            )(ids, live, place, *pieces, pscale, tile_set)
            mine, other = call(
                functools.partial(apply_body, chips),
                "apply",
                [SCALARS] + [WHOLE] * (chips + 1),
                half_shapes,
                [pltpu.VMEM((query_tiles, width, side), jnp.float32)],
            )(place, *grams, total)
        sums = call(
            pair_body, "pair", [WHOLE] * 2, [f32(width, columns)] + [bf16(width, columns)] * (chips - 1)
        )(mine, swap(other, "col", 1))
        parts = deal(sums, "col", 2)
        rounded = call(query_body, "query", [WHOLE] * (chips + 1), bf16(width, columns))(*parts, my_qscale)
        here = call(join_body, "join", [WHOLE] * chips, bf16(chips, width, columns))(
            *spread_to(rounded, "col", 2)
        )
        sums = call(
            back_body,
            "backward",
            [SCALARS] * 3 + [WHOLE] * 3,
            [f32(width, share)] * n_row,
            [pltpu.VMEM((query_tiles, width, side), jnp.bfloat16), product_scratch],
            **work,
        )(ids, live, place, here, swap(here, "col", 1), tile_set)
        lifted, gram = call(
            lift_body, "lift", [WHOLE] * (n_row + 1), [f32(width, share), f32(width, width)]
        )(*deal(sums, "row"), my_pscale)
    return call(
        functools.partial(finish_body, root_count), "finish", [WHOLE] * (chips + 1), f32(width, share)
    )(*terms_over_col(add_up(*spread_to(gram, "row"))), lifted)


def solution(mesh):
    in_specs = (
        P("row", "col", None, None, None),
        P("row", "col", None, None),
        P("row", "col"),
        P("row"),
        P("col"),
        P(None, ("col", "row")),
    )
    out_specs = P(None, ("col", "row"))
    return jax.shard_map(shards, mesh=mesh, in_specs=in_specs, out_specs=out_specs, check_vma=False)
```

```python
import functools
import math

import jax
import jax.numpy as jnp
from jax import lax
from jax.experimental import pallas as pl
from jax.experimental.pallas import tpu as pltpu
from jax.sharding import PartitionSpec as P

ITERS = 2
GROUP = 16
HALF_GROUP = 8
LOADS = 8
PANEL_STEP = 8
HIGH = lax.Precision.HIGHEST
VMEM_BYTES = 12 * 1024 * 1024
NT = (((1,), (1,)), ((), ()))
NN = (((1,), (0,)), ((), ()))

def inverse_factor(gram):
    width = gram.shape[0]
    rows = lax.broadcasted_iota(jnp.int32, (width, width), 0)
    cols = lax.broadcasted_iota(jnp.int32, (width, width), 1)
    work = jnp.concatenate([gram, (rows == cols).astype(jnp.float32)], axis=1)
    done = []
    for first in range(0, width, PANEL_STEP):
        height = width - first
        columns = [
            jnp.broadcast_to(work[:, first + j : first + j + 1], (height, 2 * width))
            for j in range(PANEL_STEP)
        ]
        for j in range(PANEL_STEP):
            scale = lax.rsqrt(columns[j][j : j + 1, :])
            row = work[j : j + 1, :] * scale
            factor = columns[j] * scale
            done.append(row)
            for later in range(j + 1, PANEL_STEP):
                columns[later] = columns[later] - factor * (columns[later][j : j + 1, :] * scale)
            work = work - factor * row
        work = work[PANEL_STEP:, :]
    return jnp.concatenate(done, axis=0)[:, width:]


WHOLE = pl.BlockSpec(memory_space=pltpu.VMEM)
SCALARS = pl.BlockSpec(memory_space=pltpu.SMEM)
AWAY = pl.BlockSpec(memory_space=pltpu.MemorySpace.HBM)


def call(body, name, in_specs, out_shape, scratch=(), flops=0, moved=0, out_specs=None):
    many = isinstance(out_shape, (tuple, list))
    return pl.pallas_call(
        body,
        out_shape=out_shape,
        in_specs=in_specs,
        out_specs=out_specs or ([WHOLE] * len(out_shape) if many else WHOLE),
        scratch_shapes=scratch,
        compiler_params=pltpu.CompilerParams(vmem_limit_bytes=VMEM_BYTES),
        cost_estimate=pl.CostEstimate(flops=flops, bytes_accessed=moved, transcendentals=0),
        name=name,
    )


def in_hbm(value):
    return pltpu.with_memory_space_constraint(value, pltpu.MemorySpace.HBM)


def f32(*shape):
    return jax.ShapeDtypeStruct(shape, jnp.float32)


def bf16(*shape):
    return jax.ShapeDtypeStruct(shape, jnp.bfloat16)


def put(held, owner, value, side):
    share = value.shape[1]
    if share >= side:
        per = share // side
        for piece in range(per):
            held[owner * per + piece] = value[:, piece * side : (piece + 1) * side]
    else:
        per = side // share
        for at in range(per):

            @pl.when(owner % per == at)
            def _():
                held[owner // per, :, at * share : (at + 1) * share] = value


def get(total, owner, out_ref, side):
    share = out_ref.shape[1]
    if share >= side:
        per = share // side
        for piece in range(per):
            out_ref[:, piece * side : (piece + 1) * side] = total[owner * per + piece].astype(out_ref.dtype)
    else:
        per = side // share
        for at in range(per):

            @pl.when(owner % per == at)
            def _():
                out_ref[...] = total[owner // per, :, at * share : (at + 1) * share].astype(out_ref.dtype)


def emit(total, out_refs, me, side):
    count = len(out_refs)
    for at, out_ref in enumerate(out_refs):
        get(total, me ^ ((count - at) % count), out_ref, side)


def emit_pairs(total, mine_ref, other_ref, me, side):
    for step in range(mine_ref.shape[0]):
        get(total, me ^ (2 * step), mine_ref.at[step], side)
        get(total, me ^ (2 * step + 1), other_ref.at[step], side)


def collect(held, piece_refs, me, side):
    for step, piece_ref in enumerate(piece_refs):
        put(held, me ^ step, piece_ref[...], side)


def collect_pairs(held, mine_ref, other_ref, me, side):
    for step in range(mine_ref.shape[0]):
        put(held, me ^ (2 * step), mine_ref[step], side)
        put(held, me ^ (2 * step + 1), other_ref[step], side)


def group_of(g, source, target, dims, count, ids, held, tile_ref, total):
    tiles, width, _ = total.shape
    for lane in range(GROUP):
        slot = g * GROUP + lane
        give = jnp.where(slot < count, ids[target, slot], tiles - 1)
        term = lax.dot_general(
            held[ids[source, slot]], tile_ref[slot], dims, preferred_element_type=jnp.float32
        )
        if term.shape[0] > width:
            term = term[:width] + term[width:]
        total[give] += term


def groups(source, target, dims, count, ids, held, tile_ref, total):
    def step(g, carry):
        group_of(g, source, target, dims, count, ids, held, tile_ref, total)
        return carry

    last = tile_ref.shape[0] // GROUP
    lax.fori_loop(0, jnp.minimum((count + GROUP - 1) // GROUP, last), step, 0)


def first_body(n_in, ids, live, place, *refs):
    pieces, (tile_ref, mine_ref, other_ref, held, total) = refs[:n_in], refs[n_in:]
    side = tile_ref.shape[1]
    collect(held, pieces, place[0], side)
    total[...] = jnp.zeros_like(total)
    groups(1, 0, NT, live[0], ids, held, tile_ref, total)
    emit_pairs(total, mine_ref, other_ref, place[1], side)


def back_body(ids, live, place, here_ref, there_ref, tile_ref, *refs):
    out_refs, (held, total) = refs[:-2], refs[-2:]
    side = tile_ref.shape[1]
    collect_pairs(held, here_ref, there_ref, place[1], side)
    total[...] = jnp.zeros_like(total)
    groups(0, 1, NN, live[0], ids, held, tile_ref, total)
    emit(total, out_refs, place[0], side)


def listed(source, target, dims, side_of, ids, order, held, tile_ref, total):
    tiles = total.shape[0]
    slots = tile_ref.shape[0]
    count = order[2, side_of]

    def step(g, carry):
        for lane in range(HALF_GROUP):
            at = g * HALF_GROUP + lane
            slot = order[side_of, at]
            give = jnp.where(at < count, ids[target, slot], tiles - 1)
            total[give] += lax.dot_general(
                held[ids[source, slot]], tile_ref[slot], dims, preferred_element_type=jnp.float32
            )
        return carry

    lax.fori_loop(0, jnp.minimum((count + HALF_GROUP - 1) // HALF_GROUP, slots // HALF_GROUP), step, 0)


def emit_half(total, out_ref, me, side, flip):
    for step in range(out_ref.shape[0]):
        get(total, me ^ (2 * step + flip), out_ref.at[step], side)


def collect_half(held, piece_refs, me, side, flip):
    for step, piece_ref in enumerate(piece_refs):
        put(held, me ^ (2 * step + flip), piece_ref[...], side)


def forward_other_body(n_in, ids, order, place, *refs):
    pieces, (tile_ref, held, other_ref, total) = refs[:n_in], refs[n_in:]
    side = tile_ref.shape[1]
    collect(held, pieces, place[0], side)
    total[...] = jnp.zeros_like(total)
    listed(1, 0, NT, 1 - place[1] % 2, ids, order, held, tile_ref, total)
    emit_half(total, other_ref, place[1], side, 1)


def forward_mine_body(ids, order, place, held, tile_ref, mine_ref, total):
    side = tile_ref.shape[1]
    total[...] = jnp.zeros_like(total)
    listed(1, 0, NT, place[1] % 2, ids, order, held, tile_ref, total)
    emit_half(total, mine_ref, place[1], side, 0)


def back_mine_body(n_in, ids, order, place, *refs):
    pieces, (tile_ref, total, held) = refs[:n_in], refs[n_in:]
    collect_half(held, pieces, place[1], tile_ref.shape[1], 0)
    total[...] = jnp.zeros_like(total)
    listed(0, 1, NN, place[1] % 2, ids, order, held, tile_ref, total)


def back_other_body(ids, order, place, there_ref, begun_ref, tile_ref, *refs):
    out_refs, (held, total) = refs[:-2], refs[-2:]
    side = tile_ref.shape[1]
    collect_half(held, [there_ref.at[step] for step in range(there_ref.shape[0])], place[1], side, 1)
    total[...] = begun_ref[...]
    listed(0, 1, NN, 1 - place[1] % 2, ids, order, held, tile_ref, total)
    emit(total, out_refs, place[0], side)


def next_body(n_in, ids, live, place, *refs):
    pieces, (scale_ref, tile_ref, out_ref, spread, held, total) = refs[:n_in], refs[n_in:]
    tiles, width, side = out_ref.shape
    collect(spread, pieces, place[0], side)
    for tile in range(spread.shape[0]):
        value = spread[tile] * scale_ref[:, tile * side : (tile + 1) * side]
        high = value.astype(jnp.bfloat16)
        held[tile, :width] = high
        held[tile, width:] = (value - high.astype(jnp.float32)).astype(jnp.bfloat16)
    total[...] = jnp.zeros_like(total)
    groups(1, 0, NT, live[0], ids, held, tile_ref, total)
    out_ref[...] = total[:tiles]


def add(refs):
    total = refs[0][...].astype(jnp.float32)
    for ref in refs[1:]:
        total = total + ref[...].astype(jnp.float32)
    return total


def start_body(place, panel_ref, degree_ref, out_ref, held, degrees, sems):
    share = panel_ref.shape[1]
    at = pl.multiple_of(place[0] * share, 128)
    loads = [
        pltpu.make_async_copy(degree_ref, degrees, sems.at[0]),
        pltpu.make_async_copy(panel_ref, held, sems.at[1]),
    ]
    for load in loads:
        load.start()
    for load in loads:
        load.wait()
    scale = 1.0 / jnp.sqrt(degrees[:, pl.ds(at, share)].astype(jnp.float32))
    out_ref[...] = (held[...] * scale).astype(out_ref.dtype)


def load_body(per, ids, live, place, after_ref, tile_ref, product_ref, query_ref, *refs):
    keep, my_product_ref, product_out, my_query_ref, order, degrees, counts, sems = refs
    loads = [
        pltpu.make_async_copy(product_ref, degrees, sems.at[0]),
        pltpu.make_async_copy(query_ref, counts, sems.at[1]),
    ]
    part = tile_ref.shape[0] // LOADS
    for step in range(LOADS):
        span = pl.ds(step * part, part)
        loads.append(pltpu.make_async_copy(tile_ref.at[span], keep.at[span], sems.at[2 + step]))
    for load in loads:
        load.start()
    order[2, 0] = 0
    order[2, 1] = 0
    for slot in range(tile_ref.shape[0]):
        order[0, slot] = 0
        order[1, slot] = 0
    for slot in range(tile_ref.shape[0]):

        @pl.when(slot < live[0])
        def _():
            core = ids[0, slot] // per % 2
            at = order[2, core]
            order[core, at] = slot
            order[2, core] = at + 1

    loads[0].wait()
    product_out[...] = 1.0 / jnp.sqrt(degrees[...].astype(jnp.float32))
    share = my_product_ref.shape[1]
    at = pl.multiple_of(place[0] * share, 128)
    my_product_ref[...] = product_out[:, pl.ds(at, share)]
    loads[1].wait()
    columns = my_query_ref.shape[1]
    if columns % 128 == 0:
        at = pl.multiple_of(place[1] * columns, 128)
        my_query_ref[...] = 1.0 / jnp.sqrt(counts[:, pl.ds(at, columns)].astype(jnp.float32))
    else:
        for step in range(counts.shape[1] // columns):

            @pl.when(place[1] == step)
            def _():
                degree = counts[:, step * columns : (step + 1) * columns]
                my_query_ref[...] = 1.0 / jnp.sqrt(degree.astype(jnp.float32))
    for load in loads[2:]:
        load.wait()


def pair_body(mine_ref, got_ref, *outs):
    count = len(outs)
    for at, out_ref in enumerate(outs):
        step = (count - at) % count
        out_ref[...] = (mine_ref[step] + got_ref[step]).astype(out_ref.dtype)


def join_body(*refs):
    for step, ref in enumerate(refs[:-1]):
        refs[-1][step] = ref[...]


def query_body(*refs):
    part_refs, scale_ref, out_ref = refs[:-2], refs[-2], refs[-1]
    out_ref[...] = (add(part_refs) * scale_ref[...]).astype(out_ref.dtype)


def lift_only_body(*refs):
    part_refs, scale_ref, lifted_ref = refs[:-2], refs[-2], refs[-1]
    lifted_ref[...] = add(part_refs) * scale_ref[...]


def lift_body(*refs):
    part_refs, scale_ref, lifted_ref, gram_ref = refs[:-3], refs[-3], refs[-2], refs[-1]
    lifted = add(part_refs) * scale_ref[...]
    lifted_ref[...] = lifted
    gram_ref[...] = lax.dot_general(lifted, lifted, NT, precision=HIGH, preferred_element_type=jnp.float32)


def gram_body(*refs):
    total = jnp.zeros(refs[-1].shape, jnp.float32)
    for ref in refs[:-1]:
        total = total + lax.dot_general(
            ref[...], ref[...], NT, precision=HIGH, preferred_element_type=jnp.float32
        )
    refs[-1][...] = total


def sum_body(*refs):
    refs[-1][...] = add(refs[:-1])


def apply_tile(inverse, total_ref, owner, out_ref):
    width, share = out_ref.shape
    side = total_ref.shape[2]
    if share >= side:
        for piece in range(share // side):
            out_ref[:, piece * side : (piece + 1) * side] = lax.dot_general(
                inverse,
                total_ref[owner * (share // side) + piece],
                NN,
                precision=HIGH,
                preferred_element_type=jnp.float32,
            )
    else:
        per = side // share
        for at in range(per):

            @pl.when(owner % per == at)
            def _():
                out_ref[...] = lax.dot_general(
                    inverse,
                    total_ref[owner // per],
                    NN,
                    precision=HIGH,
                    preferred_element_type=jnp.float32,
                )[:, at * share : (at + 1) * share]


def apply_other_body(n_in, place, *refs):
    grams, (total_ref, inverse_ref, other_ref) = refs[:n_in], refs[n_in:]
    inverse = inverse_factor(add(grams))
    inverse_ref[...] = inverse
    for step in range(other_ref.shape[0]):
        apply_tile(inverse, total_ref, place[1] ^ (2 * step + 1), other_ref.at[step])


def apply_mine_body(place, inverse_ref, total_ref, mine_ref):
    for step in range(mine_ref.shape[0]):
        apply_tile(inverse_ref[...], total_ref, place[1] ^ (2 * step), mine_ref.at[step])


def finish_body(after, *refs):
    grams, lifted_ref, out_ref = refs[:-2], refs[-2], refs[-1]
    out_ref[...] = (
        lax.dot_general(
            inverse_factor(add(grams)), lifted_ref[...], NN, precision=HIGH, preferred_element_type=jnp.float32
        )
        * after
    )


def swap(value, axis, step):
    return lax.ppermute(value, axis, [(i, i ^ step) for i in range(lax.axis_size(axis))])


def spread_to(value, axis, stride=1):
    return [value] + [swap(value, axis, step) for step in range(stride, lax.axis_size(axis), stride)]


def deal(values, axis, stride=1):
    count = len(values)
    return [values[0]] + [swap(value, axis, (count - at) * stride) for at, value in enumerate(values[1:], 1)]


def add_up(*values):
    return call(sum_body, "sum", [WHOLE] * len(values), f32(*values[0].shape))(*values)


def terms_over_col(gram):
    return spread_to(add_up(gram, swap(gram, "col", 1)), "col", 2)


def shards(tiles, tile_ids, tile_count, query_degree, product_degree, panel):
    tile_set = tiles[0, 0]
    ids = tile_ids[0, 0]
    live = tile_count[0]
    slots, side, _ = tile_set.shape
    width, share = panel.shape
    queries, products = query_degree.shape[0], product_degree.shape[0]
    query_tiles, product_tiles = queries // side, products // side
    n_row, n_col = lax.axis_size("row"), lax.axis_size("col")
    chips = n_col // 2
    place = jnp.stack([lax.axis_index("row"), lax.axis_index("col")]).astype(jnp.int32)
    columns = queries // n_col
    work = dict(flops=2 * slots * width * side * side, moved=2 * slots * side * side)
    scaled = call(
        start_body,
        "start",
        [SCALARS, AWAY, AWAY],
        bf16(width, share),
        [
            pltpu.VMEM((width, share), jnp.float32),
            pltpu.VMEM((1, products), jnp.int32),
            pltpu.SemaphoreType.DMA((2,)),
        ],
    )(place, in_hbm(panel), in_hbm(product_degree[None, :]))
    pieces = spread_to(scaled, "row")
    split = columns % side == 0
    tile_set, my_pscale, pscale, my_qscale, order = call(
        functools.partial(load_body, max(columns // side, 1)),
        "load",
        [SCALARS] * 3 + [WHOLE, AWAY, AWAY, AWAY],
        [
            pltpu.VMEM((slots, side, side), jnp.bfloat16),
            f32(1, share),
            f32(1, products),
            f32(1, columns),
            jax.ShapeDtypeStruct((3, slots), jnp.int32),
        ],
        [
            pltpu.VMEM((1, products), jnp.int32),
            pltpu.VMEM((1, queries), jnp.int32),
            pltpu.SemaphoreType.DMA((2 + LOADS,)),
        ],
        moved=4 * slots * side * side,
        out_specs=[WHOLE] * 4 + [SCALARS],
    )(ids, live, place, scaled, in_hbm(tile_set), in_hbm(product_degree[None, :]), in_hbm(query_degree[None, :]))
    tile_set = pltpu.with_memory_space_constraint(tile_set, pltpu.VMEM)
    root_count = math.sqrt(products * n_col)
    half = f32(chips, width, columns)
    half_work = dict(flops=slots * width * side * side, moved=slots * side * side)
    query_scratch = pltpu.VMEM((query_tiles + 1, width, side), jnp.float32)
    product_scratch = pltpu.VMEM((product_tiles + 1, width, side), jnp.float32)
    query_held = pltpu.VMEM((query_tiles, width, side), jnp.bfloat16)
    for iteration in range(ITERS):
        if iteration > 0:
            pieces = spread_to(lifted, "row")
            gram = call(gram_body, "gram", [WHOLE] * n_row, f32(width, width))(*pieces)
            grams = terms_over_col(gram)
            total = call(
                functools.partial(next_body, n_row),
                "forward",
                [SCALARS] * 3 + [WHOLE] * (n_row + 2),
                f32(query_tiles, width, side),
                [
                    pltpu.VMEM((product_tiles, width, side), jnp.float32),
                    pltpu.VMEM((product_tiles, 2 * width, side), jnp.bfloat16),
                    query_scratch,
                ],
                **work,
            )(ids, live, place, *pieces, pscale, tile_set)
            inverse, other = call(
                functools.partial(apply_other_body, chips),
                "apply",
                [SCALARS] + [WHOLE] * (chips + 1),
                [f32(width, width), half],
            )(place, *grams, total)
            got = swap(other, "col", 1)
            mine = call(apply_mine_body, "apply_rest", [SCALARS] + [WHOLE] * 2, half, **half_work)(
                place, inverse, total
            )
        elif split:
            held, other = call(
                functools.partial(forward_other_body, n_row),
                "forward",
                [SCALARS] * 3 + [WHOLE] * (n_row + 1),
                [bf16(product_tiles, width, side), half],
                [query_scratch],
                **half_work,
            )(ids, order, place, *pieces, tile_set)
            got = swap(other, "col", 1)
            mine = call(
                forward_mine_body,
                "forward_rest",
                [SCALARS] * 3 + [WHOLE] * 2,
                half,
                [query_scratch],
                **half_work,
            )(ids, order, place, held, tile_set)
        else:
            mine, other = call(
                functools.partial(first_body, n_row),
                "forward",
                [SCALARS] * 3 + [WHOLE] * (n_row + 1),
                [half] * 2,
                [pltpu.VMEM((product_tiles, width, side), jnp.bfloat16), query_scratch],
                **work,
            )(ids, live, place, *pieces, tile_set)
            got = swap(other, "col", 1)
        sums = call(
            pair_body, "pair", [WHOLE] * 2, [f32(width, columns)] + [bf16(width, columns)] * (chips - 1)
        )(mine, got)
        parts = deal(sums, "col", 2)
        rounded = call(query_body, "query", [WHOLE] * (chips + 1), bf16(width, columns))(*parts, my_qscale)
        pieces = spread_to(rounded, "col", 2)
        here = call(join_body, "join", [WHOLE] * chips, bf16(chips, width, columns))(*pieces)
        there = swap(here, "col", 1)
        if split:
            begun = call(
                functools.partial(back_mine_body, chips),
                "backward",
                [SCALARS] * 3 + [WHOLE] * (chips + 1),
                f32(product_tiles + 1, width, side),
                [query_held],
                **half_work,
            )(ids, order, place, *pieces, tile_set)
            sums = call(
                back_other_body,
                "backward_rest",
                [SCALARS] * 3 + [WHOLE] * 3,
                [f32(width, share)] * n_row,
                [query_held, product_scratch],
                **half_work,
            )(ids, order, place, there, begun, tile_set)
        else:
            sums = call(
                back_body,
                "backward",
                [SCALARS] * 3 + [WHOLE] * 3,
                [f32(width, share)] * n_row,
                [query_held, product_scratch],
                **work,
            )(ids, live, place, here, there, tile_set)
        parts = deal(sums, "row")
        if iteration < ITERS - 1:
            lifted = call(lift_only_body, "lift", [WHOLE] * (n_row + 1), f32(width, share))(*parts, my_pscale)
    lifted, gram = call(
        lift_body, "lift", [WHOLE] * (n_row + 1), [f32(width, share), f32(width, width)]
    )(*parts, my_pscale)
    return call(
        functools.partial(finish_body, root_count), "finish", [WHOLE] * (chips + 1), f32(width, share)
    )(*terms_over_col(add_up(*spread_to(gram, "row"))), lifted)


def solution(mesh):
    in_specs = (
        P("row", "col", None, None, None),
        P("row", "col", None, None),
        P("row", "col"),
        P("row"),
        P("col"),
        P(None, ("col", "row")),
    )
    out_specs = P(None, ("col", "row"))
    return jax.shard_map(shards, mesh=mesh, in_specs=in_specs, out_specs=out_specs, check_vma=False)
```

```python
import functools
import math

import jax
import jax.numpy as jnp
from jax import lax
from jax.experimental import pallas as pl
from jax.experimental.pallas import tpu as pltpu
from jax.sharding import PartitionSpec as P

ITERS = 2
GROUP = 8
LOADS = 8
PANEL_STEP = 8
HIGH = lax.Precision.HIGHEST
VMEM_BYTES = 12 * 1024 * 1024
NT = (((1,), (1,)), ((), ()))
NN = (((1,), (0,)), ((), ()))

def inverse_factor(gram):
    width = gram.shape[0]
    rows = lax.broadcasted_iota(jnp.int32, (width, width), 0)
    cols = lax.broadcasted_iota(jnp.int32, (width, width), 1)
    work = jnp.concatenate([gram, (rows == cols).astype(jnp.float32)], axis=1)
    done = []
    for first in range(0, width, PANEL_STEP):
        height = width - first
        columns = [
            jnp.broadcast_to(work[:, first + j : first + j + 1], (height, 2 * width))
            for j in range(PANEL_STEP)
        ]
        for j in range(PANEL_STEP):
            scale = lax.rsqrt(columns[j][j : j + 1, :])
            row = work[j : j + 1, :] * scale
            factor = columns[j] * scale
            done.append(row)
            for later in range(j + 1, PANEL_STEP):
                columns[later] = columns[later] - factor * (columns[later][j : j + 1, :] * scale)
            work = work - factor * row
        work = work[PANEL_STEP:, :]
    return jnp.concatenate(done, axis=0)[:, width:]


SLOT, QUERY_GIVE, PRODUCT_TAKE, QUERY_TAKE, PRODUCT_GIVE = range(5)
FIELDS, LISTS, ALL = 5, 3, 2
SINGLES = FIELDS * LISTS
ROW_AT, COL_AT = 3, 4
WHOLE = pl.BlockSpec(memory_space=pltpu.VMEM)
SCALARS = pl.BlockSpec(memory_space=pltpu.SMEM)
AWAY = pl.BlockSpec(memory_space=pltpu.MemorySpace.HBM)


def call(body, name, in_specs, out_shape, scratch=(), flops=0, moved=0, out_specs=None):
    many = isinstance(out_shape, (tuple, list))
    return pl.pallas_call(
        body,
        out_shape=out_shape,
        in_specs=in_specs,
        out_specs=out_specs or ([WHOLE] * len(out_shape) if many else WHOLE),
        scratch_shapes=scratch,
        compiler_params=pltpu.CompilerParams(vmem_limit_bytes=VMEM_BYTES),
        cost_estimate=pl.CostEstimate(flops=flops, bytes_accessed=moved, transcendentals=0),
        name=name,
    )


def in_hbm(value):
    return pltpu.with_memory_space_constraint(value, pltpu.MemorySpace.HBM)


def f32(*shape):
    return jax.ShapeDtypeStruct(shape, jnp.float32)


def bf16(*shape):
    return jax.ShapeDtypeStruct(shape, jnp.bfloat16)


def put(held, owner, value, side):
    share = value.shape[1]
    if share >= side:
        per = share // side
        for piece in range(per):
            held[owner * per + piece] = value[:, piece * side : (piece + 1) * side]
    else:
        per = side // share
        for at in range(per):

            @pl.when(owner % per == at)
            def _():
                held[owner // per, :, at * share : (at + 1) * share] = value


def get(total, owner, out_ref, side):
    share = out_ref.shape[1]
    if share >= side:
        per = share // side
        for piece in range(per):
            out_ref[:, piece * side : (piece + 1) * side] = total[owner * per + piece].astype(out_ref.dtype)
    else:
        per = side // share
        for at in range(per):

            @pl.when(owner % per == at)
            def _():
                out_ref[...] = total[owner // per, :, at * share : (at + 1) * share].astype(out_ref.dtype)


def emit(total, out_refs, me, side):
    count = len(out_refs)
    for at, out_ref in enumerate(out_refs):
        get(total, me ^ ((count - at) % count), out_ref, side)


def collect(held, piece_refs, me, side):
    for step, piece_ref in enumerate(piece_refs):
        put(held, me ^ step, piece_ref[...], side)


def products(which, take, give, dims, table, held, tile_ref, total):
    width = total.shape[1]
    count = table[SINGLES, which]

    def step(g, carry):
        for lane in range(GROUP):
            at = g * GROUP + lane
            term = lax.dot_general(
                held[table[which * FIELDS + take, at]],
                tile_ref[table[which * FIELDS + SLOT, at]],
                dims,
                preferred_element_type=jnp.float32,
            )
            if term.shape[0] > width:
                term = term[:width] + term[width:]
            total[table[which * FIELDS + give, at]] += term
        return carry

    last = tile_ref.shape[0] // GROUP
    lax.fori_loop(0, jnp.minimum((count + GROUP - 1) // GROUP, last), step, 0)


forward = functools.partial(products, take=PRODUCT_TAKE, give=QUERY_GIVE, dims=NT)
backward = functools.partial(products, take=QUERY_TAKE, give=PRODUCT_GIVE, dims=NN)


def emit_half(total, out_ref, me, side, flip):
    for step in range(out_ref.shape[0]):
        get(total, me ^ (2 * step + flip), out_ref.at[step], side)


def collect_half(held, piece_refs, me, side, flip):
    for step, piece_ref in enumerate(piece_refs):
        put(held, me ^ (2 * step + flip), piece_ref[...], side)


def forward_body(n_in, table, *refs):
    pieces, (tile_ref, mine_ref, other_ref, held, total) = refs[:n_in], refs[n_in:]
    side = tile_ref.shape[1]
    collect(held, pieces, table[SINGLES, ROW_AT], side)
    total[...] = jnp.zeros_like(total)
    forward(ALL, table=table, held=held, tile_ref=tile_ref, total=total)
    emit_half(total, mine_ref, table[SINGLES, COL_AT], side, 0)
    emit_half(total, other_ref, table[SINGLES, COL_AT], side, 1)


def forward_other_body(n_in, table, *refs):
    pieces, (tile_ref, held, other_ref, total) = refs[:n_in], refs[n_in:]
    side, me = tile_ref.shape[1], table[SINGLES, COL_AT]
    collect(held, pieces, table[SINGLES, ROW_AT], side)
    total[...] = jnp.zeros_like(total)
    forward(1 - me % 2, table=table, held=held, tile_ref=tile_ref, total=total)
    emit_half(total, other_ref, me, side, 1)


def forward_mine_body(table, held, tile_ref, mine_ref, total):
    side, me = tile_ref.shape[1], table[SINGLES, COL_AT]
    total[...] = jnp.zeros_like(total)
    forward(me % 2, table=table, held=held, tile_ref=tile_ref, total=total)
    emit_half(total, mine_ref, me, side, 0)


def back_body(table, here_ref, there_ref, tile_ref, *refs):
    out_refs, (held, total) = refs[:-2], refs[-2:]
    side = tile_ref.shape[1]
    for flip, ref in enumerate((here_ref, there_ref)):
        collect_half(held, [ref.at[step] for step in range(ref.shape[0])], table[SINGLES, COL_AT], side, flip)
    total[...] = jnp.zeros_like(total)
    backward(ALL, table=table, held=held, tile_ref=tile_ref, total=total)
    emit(total, out_refs, table[SINGLES, ROW_AT], side)


def back_mine_body(n_in, table, *refs):
    pieces, (tile_ref, total, held) = refs[:n_in], refs[n_in:]
    me = table[SINGLES, COL_AT]
    collect_half(held, pieces, me, tile_ref.shape[1], 0)
    total[...] = jnp.zeros_like(total)
    backward(me % 2, table=table, held=held, tile_ref=tile_ref, total=total)


def back_other_body(table, there_ref, begun_ref, tile_ref, *refs):
    out_refs, (held, total) = refs[:-2], refs[-2:]
    side, me = tile_ref.shape[1], table[SINGLES, COL_AT]
    collect_half(held, [there_ref.at[step] for step in range(there_ref.shape[0])], me, side, 1)
    total[...] = begun_ref[...]
    backward(1 - me % 2, table=table, held=held, tile_ref=tile_ref, total=total)
    emit(total, out_refs, table[SINGLES, ROW_AT], side)


def next_body(n_in, table, *refs):
    pieces, (scale_ref, tile_ref, out_ref, spread, held, total) = refs[:n_in], refs[n_in:]
    tiles, width, side = out_ref.shape
    collect(spread, pieces, table[SINGLES, ROW_AT], side)
    for tile in range(spread.shape[0]):
        value = spread[tile] * scale_ref[:, tile * side : (tile + 1) * side]
        high = value.astype(jnp.bfloat16)
        held[tile, :width] = high
        held[tile, width:] = (value - high.astype(jnp.float32)).astype(jnp.bfloat16)
    total[...] = jnp.zeros_like(total)
    forward(ALL, table=table, held=held, tile_ref=tile_ref, total=total)
    out_ref[...] = total[:tiles]


def add(refs):
    total = refs[0][...].astype(jnp.float32)
    for ref in refs[1:]:
        total = total + ref[...].astype(jnp.float32)
    return total


def start_body(place, panel_ref, degree_ref, out_ref, held, degrees, sems):
    share = panel_ref.shape[1]
    at = pl.multiple_of(place[0] * share, 128)
    loads = [
        pltpu.make_async_copy(degree_ref, degrees, sems.at[0]),
        pltpu.make_async_copy(panel_ref, held, sems.at[1]),
    ]
    for load in loads:
        load.start()
    for load in loads:
        load.wait()
    scale = 1.0 / jnp.sqrt(degrees[:, pl.ds(at, share)].astype(jnp.float32))
    out_ref[...] = (held[...] * scale).astype(out_ref.dtype)


def write_table(table, ids, place, per, query_tiles, product_tiles):
    slots = ids.shape[1]
    for which in range(LISTS):
        table[SINGLES, which] = 0
        for at in range(slots):
            table[which * FIELDS + SLOT, at] = 0
            table[which * FIELDS + QUERY_GIVE, at] = query_tiles
            table[which * FIELDS + PRODUCT_TAKE, at] = 0
            table[which * FIELDS + QUERY_TAKE, at] = 0
            table[which * FIELDS + PRODUCT_GIVE, at] = product_tiles
    table[SINGLES, ROW_AT] = place[0]
    table[SINGLES, COL_AT] = place[1]

    def step(slot, carry):
        query, product = ids[0, slot], ids[1, slot]
        for which in (query // per % 2, ALL):
            at = table[SINGLES, which]
            table[which * FIELDS + SLOT, at] = slot
            table[which * FIELDS + QUERY_GIVE, at] = query
            table[which * FIELDS + PRODUCT_TAKE, at] = product
            table[which * FIELDS + QUERY_TAKE, at] = query
            table[which * FIELDS + PRODUCT_GIVE, at] = product
            table[SINGLES, which] = at + 1
        return carry

    lax.fori_loop(0, jnp.minimum(place[2], slots), step, 0)


def load_body(per, place, after_ref, tile_ref, id_ref, product_ref, query_ref, *refs):
    keep, my_product_ref, product_out, my_query_ref, table, ids, degrees, counts, sems = refs
    loads = [
        pltpu.make_async_copy(id_ref, ids, sems.at[0]),
        pltpu.make_async_copy(product_ref, degrees, sems.at[1]),
        pltpu.make_async_copy(query_ref, counts, sems.at[2]),
    ]
    part = tile_ref.shape[0] // LOADS
    for step in range(LOADS):
        span = pl.ds(step * part, part)
        loads.append(pltpu.make_async_copy(tile_ref.at[span], keep.at[span], sems.at[3 + step]))
    for load in loads:
        load.start()
    loads[0].wait()
    side = tile_ref.shape[1]
    write_table(table, ids, place, per, query_ref.shape[1] // side, product_ref.shape[1] // side)
    loads[1].wait()
    product_out[...] = 1.0 / jnp.sqrt(degrees[...].astype(jnp.float32))
    share = my_product_ref.shape[1]
    at = pl.multiple_of(place[0] * share, 128)
    my_product_ref[...] = product_out[:, pl.ds(at, share)]
    loads[2].wait()
    columns = my_query_ref.shape[1]
    if columns % 128 == 0:
        at = pl.multiple_of(place[1] * columns, 128)
        my_query_ref[...] = 1.0 / jnp.sqrt(counts[:, pl.ds(at, columns)].astype(jnp.float32))
    else:
        for step in range(counts.shape[1] // columns):

            @pl.when(place[1] == step)
            def _():
                degree = counts[:, step * columns : (step + 1) * columns]
                my_query_ref[...] = 1.0 / jnp.sqrt(degree.astype(jnp.float32))
    for load in loads[3:]:
        load.wait()


def pair_body(mine_ref, got_ref, *outs):
    count = len(outs)
    for at, out_ref in enumerate(outs):
        step = (count - at) % count
        out_ref[...] = (mine_ref[step] + got_ref[step]).astype(out_ref.dtype)


def join_body(*refs):
    for step, ref in enumerate(refs[:-1]):
        refs[-1][step] = ref[...]


def query_body(*refs):
    part_refs, scale_ref, out_ref = refs[:-2], refs[-2], refs[-1]
    out_ref[...] = (add(part_refs) * scale_ref[...]).astype(out_ref.dtype)


def lift_only_body(*refs):
    part_refs, scale_ref, lifted_ref = refs[:-2], refs[-2], refs[-1]
    lifted_ref[...] = add(part_refs) * scale_ref[...]


def lift_body(*refs):
    part_refs, scale_ref, lifted_ref, gram_ref = refs[:-3], refs[-3], refs[-2], refs[-1]
    lifted = add(part_refs) * scale_ref[...]
    lifted_ref[...] = lifted
    gram_ref[...] = lax.dot_general(lifted, lifted, NT, precision=HIGH, preferred_element_type=jnp.float32)


def gram_body(*refs):
    total = jnp.zeros(refs[-1].shape, jnp.float32)
    for ref in refs[:-1]:
        total = total + lax.dot_general(
            ref[...], ref[...], NT, precision=HIGH, preferred_element_type=jnp.float32
        )
    refs[-1][...] = total


def sum_body(*refs):
    refs[-1][...] = add(refs[:-1])


def apply_tile(inverse, total_ref, owner, out_ref):
    width, share = out_ref.shape
    side = total_ref.shape[2]
    if share >= side:
        for piece in range(share // side):
            out_ref[:, piece * side : (piece + 1) * side] = lax.dot_general(
                inverse,
                total_ref[owner * (share // side) + piece],
                NN,
                precision=HIGH,
                preferred_element_type=jnp.float32,
            )
    else:
        per = side // share
        for at in range(per):

            @pl.when(owner % per == at)
            def _():
                out_ref[...] = lax.dot_general(
                    inverse,
                    total_ref[owner // per],
                    NN,
                    precision=HIGH,
                    preferred_element_type=jnp.float32,
                )[:, at * share : (at + 1) * share]


def apply_other_body(n_in, table, *refs):
    grams, (total_ref, inverse_ref, other_ref) = refs[:n_in], refs[n_in:]
    inverse = inverse_factor(add(grams))
    inverse_ref[...] = inverse
    for step in range(other_ref.shape[0]):
        apply_tile(inverse, total_ref, table[SINGLES, COL_AT] ^ (2 * step + 1), other_ref.at[step])


def apply_mine_body(table, inverse_ref, total_ref, mine_ref):
    for step in range(mine_ref.shape[0]):
        apply_tile(inverse_ref[...], total_ref, table[SINGLES, COL_AT] ^ (2 * step), mine_ref.at[step])


def finish_body(after, *refs):
    grams, lifted_ref, out_ref = refs[:-2], refs[-2], refs[-1]
    out_ref[...] = (
        lax.dot_general(
            inverse_factor(add(grams)), lifted_ref[...], NN, precision=HIGH, preferred_element_type=jnp.float32
        )
        * after
    )


def swap(value, axis, step):
    return lax.ppermute(value, axis, [(i, i ^ step) for i in range(lax.axis_size(axis))])


def spread_to(value, axis, stride=1):
    return [value] + [swap(value, axis, step) for step in range(stride, lax.axis_size(axis), stride)]


def deal(values, axis, stride=1):
    count = len(values)
    return [values[0]] + [swap(value, axis, (count - at) * stride) for at, value in enumerate(values[1:], 1)]


def add_up(*values):
    return call(sum_body, "sum", [WHOLE] * len(values), f32(*values[0].shape))(*values)


def terms_over_col(gram):
    return spread_to(add_up(gram, swap(gram, "col", 1)), "col", 2)


def shards(tiles, tile_ids, tile_count, query_degree, product_degree, panel):
    tile_set = tiles[0, 0]
    ids = tile_ids[0, 0]
    slots, side, _ = tile_set.shape
    width, share = panel.shape
    queries, products = query_degree.shape[0], product_degree.shape[0]
    query_tiles, product_tiles = queries // side, products // side
    n_row, n_col = lax.axis_size("row"), lax.axis_size("col")
    chips = n_col // 2
    row_at, col_at = lax.axis_index("row").astype(jnp.int32), lax.axis_index("col").astype(jnp.int32)
    columns = queries // n_col
    work = dict(flops=2 * slots * width * side * side, moved=2 * slots * side * side)
    scaled = call(
        start_body,
        "start",
        [SCALARS, AWAY, AWAY],
        bf16(width, share),
        [
            pltpu.VMEM((width, share), jnp.float32),
            pltpu.VMEM((1, products), jnp.int32),
            pltpu.SemaphoreType.DMA((2,)),
        ],
    )(row_at[None], in_hbm(panel), in_hbm(product_degree[None, :]))
    pieces = spread_to(scaled, "row")
    split = columns % side == 0
    tile_set, my_pscale, pscale, my_qscale, table = call(
        functools.partial(load_body, max(columns // side, 1)),
        "load",
        [SCALARS, WHOLE] + [AWAY] * 4,
        [
            pltpu.VMEM((slots, side, side), jnp.bfloat16),
            f32(1, share),
            f32(1, products),
            f32(1, columns),
            jax.ShapeDtypeStruct((SINGLES + 1, slots), jnp.int32),
        ],
        [
            pltpu.SMEM(ids.shape, jnp.int32),
            pltpu.VMEM((1, products), jnp.int32),
            pltpu.VMEM((1, queries), jnp.int32),
            pltpu.SemaphoreType.DMA((3 + LOADS,)),
        ],
        moved=4 * slots * side * side,
        out_specs=[WHOLE] * 4 + [SCALARS],
    )(
        jnp.stack([row_at, col_at, tile_count[0, 0]]),
        scaled,
        in_hbm(tile_set),
        in_hbm(ids),
        in_hbm(product_degree[None, :]),
        in_hbm(query_degree[None, :]),
    )
    tile_set = pltpu.with_memory_space_constraint(tile_set, pltpu.VMEM)
    root_count = math.sqrt(products * n_col)
    half = f32(chips, width, columns)
    half_work = dict(flops=slots * width * side * side, moved=slots * side * side)
    query_scratch = pltpu.VMEM((query_tiles + 1, width, side), jnp.float32)
    product_scratch = pltpu.VMEM((product_tiles + 1, width, side), jnp.float32)
    query_held = pltpu.VMEM((query_tiles, width, side), jnp.bfloat16)
    for iteration in range(ITERS):
        if iteration > 0:
            pieces = spread_to(lifted, "row")
            gram = call(gram_body, "gram", [WHOLE] * n_row, f32(width, width))(*pieces)
            grams = terms_over_col(gram)
            total = call(
                functools.partial(next_body, n_row),
                "forward",
                [SCALARS] + [WHOLE] * (n_row + 2),
                f32(query_tiles, width, side),
                [
                    pltpu.VMEM((product_tiles, width, side), jnp.float32),
                    pltpu.VMEM((product_tiles, 2 * width, side), jnp.bfloat16),
                    query_scratch,
                ],
                **work,
            )(table, *pieces, pscale, tile_set)
            inverse, other = call(
                functools.partial(apply_other_body, chips),
                "apply",
                [SCALARS] + [WHOLE] * (chips + 1),
                [f32(width, width), half],
            )(table, *grams, total)
            got = swap(other, "col", 1)
            mine = call(apply_mine_body, "apply_rest", [SCALARS] + [WHOLE] * 2, half, **half_work)(
                table, inverse, total
            )
        elif split:
            held, other = call(
                functools.partial(forward_other_body, n_row),
                "forward",
                [SCALARS] + [WHOLE] * (n_row + 1),
                [bf16(product_tiles, width, side), half],
                [query_scratch],
                **half_work,
            )(table, *pieces, tile_set)
            got = swap(other, "col", 1)
            mine = call(
                forward_mine_body,
                "forward_rest",
                [SCALARS] + [WHOLE] * 2,
                half,
                [query_scratch],
                **half_work,
            )(table, held, tile_set)
        else:
            mine, other = call(
                functools.partial(forward_body, n_row),
                "forward",
                [SCALARS] + [WHOLE] * (n_row + 1),
                [half] * 2,
                [pltpu.VMEM((product_tiles, width, side), jnp.bfloat16), query_scratch],
                **work,
            )(table, *pieces, tile_set)
            got = swap(other, "col", 1)
        sums = call(
            pair_body, "pair", [WHOLE] * 2, [f32(width, columns)] + [bf16(width, columns)] * (chips - 1)
        )(mine, got)
        parts = deal(sums, "col", 2)
        rounded = call(query_body, "query", [WHOLE] * (chips + 1), bf16(width, columns))(*parts, my_qscale)
        pieces = spread_to(rounded, "col", 2)
        here = call(join_body, "join", [WHOLE] * chips, bf16(chips, width, columns))(*pieces)
        there = swap(here, "col", 1)
        if split:
            begun = call(
                functools.partial(back_mine_body, chips),
                "backward",
                [SCALARS] + [WHOLE] * (chips + 1),
                f32(product_tiles + 1, width, side),
                [query_held],
                **half_work,
            )(table, *pieces, tile_set)
            sums = call(
                back_other_body,
                "backward_rest",
                [SCALARS] + [WHOLE] * 3,
                [f32(width, share)] * n_row,
                [query_held, product_scratch],
                **half_work,
            )(table, there, begun, tile_set)
        else:
            sums = call(
                back_body,
                "backward",
                [SCALARS] + [WHOLE] * 3,
                [f32(width, share)] * n_row,
                [query_held, product_scratch],
                **work,
            )(table, here, there, tile_set)
        parts = deal(sums, "row")
        if iteration < ITERS - 1:
            lifted = call(lift_only_body, "lift", [WHOLE] * (n_row + 1), f32(width, share))(*parts, my_pscale)
    lifted, gram = call(
        lift_body, "lift", [WHOLE] * (n_row + 1), [f32(width, share), f32(width, width)]
    )(*parts, my_pscale)
    return call(
        functools.partial(finish_body, root_count), "finish", [WHOLE] * (chips + 1), f32(width, share)
    )(*terms_over_col(add_up(*spread_to(gram, "row"))), lifted)


def solution(mesh):
    in_specs = (
        P("row", "col", None, None, None),
        P("row", "col", None, None),
        P("row", "col"),
        P("row"),
        P("col"),
        P(None, ("col", "row")),
    )
    out_specs = P(None, ("col", "row"))
    return jax.shard_map(shards, mesh=mesh, in_specs=in_specs, out_specs=out_specs, check_vma=False)
```

```python
import functools
import math

import jax
import jax.numpy as jnp
from jax import lax
from jax.experimental import pallas as pl
from jax.experimental.pallas import tpu as pltpu
from jax.sharding import PartitionSpec as P

ITERS = 2
GROUP = 8
LOADS = 8
PANEL_STEP = 8
HIGH = lax.Precision.HIGHEST
VMEM_BYTES = 12 * 1024 * 1024
NT = (((1,), (1,)), ((), ()))
NN = (((1,), (0,)), ((), ()))

def inverse_factor(gram):
    width = gram.shape[0]
    rows = lax.broadcasted_iota(jnp.int32, (width, width), 0)
    cols = lax.broadcasted_iota(jnp.int32, (width, width), 1)
    work = jnp.concatenate([gram, (rows == cols).astype(jnp.float32)], axis=1)
    done = []
    for first in range(0, width, PANEL_STEP):
        height = width - first
        columns = [
            jnp.broadcast_to(work[:, first + j : first + j + 1], (height, 2 * width))
            for j in range(PANEL_STEP)
        ]
        for j in range(PANEL_STEP):
            scale = lax.rsqrt(columns[j][j : j + 1, :])
            row = work[j : j + 1, :] * scale
            factor = columns[j] * scale
            done.append(row)
            for later in range(j + 1, PANEL_STEP):
                columns[later] = columns[later] - factor * (columns[later][j : j + 1, :] * scale)
            work = work - factor * row
        work = work[PANEL_STEP:, :]
    return jnp.concatenate(done, axis=0)[:, width:]


SLOT, QUERY_GIVE, PRODUCT_TAKE, QUERY_TAKE, PRODUCT_GIVE = range(5)
FIELDS, LISTS, ALL = 5, 3, 2
SINGLES = FIELDS * LISTS
ROW_AT, COL_AT = 3, 4
WHOLE = pl.BlockSpec(memory_space=pltpu.VMEM)
SCALARS = pl.BlockSpec(memory_space=pltpu.SMEM)
AWAY = pl.BlockSpec(memory_space=pltpu.MemorySpace.HBM)


def call(body, name, in_specs, out_shape, scratch=(), flops=0, moved=0, out_specs=None):
    many = isinstance(out_shape, (tuple, list))
    return pl.pallas_call(
        body,
        out_shape=out_shape,
        in_specs=in_specs,
        out_specs=out_specs or ([WHOLE] * len(out_shape) if many else WHOLE),
        scratch_shapes=scratch,
        compiler_params=pltpu.CompilerParams(vmem_limit_bytes=VMEM_BYTES),
        cost_estimate=pl.CostEstimate(flops=flops, bytes_accessed=moved, transcendentals=0),
        name=name,
    )


def in_hbm(value):
    return pltpu.with_memory_space_constraint(value, pltpu.MemorySpace.HBM)


def f32(*shape):
    return jax.ShapeDtypeStruct(shape, jnp.float32)


def bf16(*shape):
    return jax.ShapeDtypeStruct(shape, jnp.bfloat16)


def put(held, owner, value, side):
    share = value.shape[1]
    if share >= side:
        per = share // side
        for piece in range(per):
            held[owner * per + piece] = value[:, piece * side : (piece + 1) * side]
    else:
        per = side // share
        for at in range(per):

            @pl.when(owner % per == at)
            def _():
                held[owner // per, :, at * share : (at + 1) * share] = value


def get(total, owner, out_ref, side):
    share = out_ref.shape[1]
    if share >= side:
        per = share // side
        for piece in range(per):
            out_ref[:, piece * side : (piece + 1) * side] = total[owner * per + piece].astype(out_ref.dtype)
    else:
        per = side // share
        for at in range(per):

            @pl.when(owner % per == at)
            def _():
                out_ref[...] = total[owner // per, :, at * share : (at + 1) * share].astype(out_ref.dtype)


def emit(total, out_refs, me, side):
    count = len(out_refs)
    for at, out_ref in enumerate(out_refs):
        get(total, me ^ ((count - at) % count), out_ref, side)


def collect(held, piece_refs, me, side):
    for step, piece_ref in enumerate(piece_refs):
        put(held, me ^ step, piece_ref[...], side)


def products(which, take, give, dims, table, held, tile_ref, total):
    width = total.shape[1]
    slots = tile_ref.shape[0]

    def run(first, length):
        for lane in range(length):
            at = first + lane
            term = lax.dot_general(
                held[table[which * FIELDS + take, at]],
                tile_ref[table[which * FIELDS + SLOT, at]],
                dims,
                preferred_element_type=jnp.float32,
            )
            if term.shape[0] > width:
                term = term[:width] + term[width:]
            total[table[which * FIELDS + give, at]] += term

    if isinstance(which, int):
        run(0, slots)
        return

    def step(g, carry):
        run(slots // 2 + g * GROUP, GROUP)
        return carry

    run(0, slots // 2)
    rest = jnp.maximum(table[SINGLES, which] - slots // 2, 0)
    lax.fori_loop(0, jnp.minimum((rest + GROUP - 1) // GROUP, slots // 2 // GROUP), step, 0)


forward = functools.partial(products, take=PRODUCT_TAKE, give=QUERY_GIVE, dims=NT)
backward = functools.partial(products, take=QUERY_TAKE, give=PRODUCT_GIVE, dims=NN)


def emit_half(total, out_ref, me, side, flip):
    for step in range(out_ref.shape[0]):
        get(total, me ^ (2 * step + flip), out_ref.at[step], side)


def collect_half(held, piece_refs, me, side, flip):
    for step, piece_ref in enumerate(piece_refs):
        put(held, me ^ (2 * step + flip), piece_ref[...], side)


def forward_body(n_in, table, *refs):
    pieces, (tile_ref, mine_ref, other_ref, held, total) = refs[:n_in], refs[n_in:]
    side = tile_ref.shape[1]
    collect(held, pieces, table[SINGLES, ROW_AT], side)
    total[...] = jnp.zeros_like(total)
    forward(ALL, table=table, held=held, tile_ref=tile_ref, total=total)
    emit_half(total, mine_ref, table[SINGLES, COL_AT], side, 0)
    emit_half(total, other_ref, table[SINGLES, COL_AT], side, 1)


def forward_other_body(n_in, table, *refs):
    pieces, (tile_ref, held, other_ref, total) = refs[:n_in], refs[n_in:]
    side, me = tile_ref.shape[1], table[SINGLES, COL_AT]
    collect(held, pieces, table[SINGLES, ROW_AT], side)
    total[...] = jnp.zeros_like(total)
    forward(1 - me % 2, table=table, held=held, tile_ref=tile_ref, total=total)
    emit_half(total, other_ref, me, side, 1)


def forward_mine_body(table, held, tile_ref, mine_ref, total):
    side, me = tile_ref.shape[1], table[SINGLES, COL_AT]
    total[...] = jnp.zeros_like(total)
    forward(me % 2, table=table, held=held, tile_ref=tile_ref, total=total)
    emit_half(total, mine_ref, me, side, 0)


def back_body(table, here_ref, there_ref, tile_ref, *refs):
    out_refs, (held, total) = refs[:-2], refs[-2:]
    side = tile_ref.shape[1]
    for flip, ref in enumerate((here_ref, there_ref)):
        collect_half(held, [ref.at[step] for step in range(ref.shape[0])], table[SINGLES, COL_AT], side, flip)
    total[...] = jnp.zeros_like(total)
    backward(ALL, table=table, held=held, tile_ref=tile_ref, total=total)
    emit(total, out_refs, table[SINGLES, ROW_AT], side)


def back_mine_body(n_in, table, *refs):
    pieces, (tile_ref, total, held) = refs[:n_in], refs[n_in:]
    me = table[SINGLES, COL_AT]
    collect_half(held, pieces, me, tile_ref.shape[1], 0)
    total[...] = jnp.zeros_like(total)
    backward(me % 2, table=table, held=held, tile_ref=tile_ref, total=total)


def back_other_body(table, there_ref, begun_ref, tile_ref, *refs):
    out_refs, (held, total) = refs[:-2], refs[-2:]
    side, me = tile_ref.shape[1], table[SINGLES, COL_AT]
    collect_half(held, [there_ref.at[step] for step in range(there_ref.shape[0])], me, side, 1)
    total[...] = begun_ref[...]
    backward(1 - me % 2, table=table, held=held, tile_ref=tile_ref, total=total)
    emit(total, out_refs, table[SINGLES, ROW_AT], side)


def next_body(n_in, table, *refs):
    pieces, (scale_ref, tile_ref, out_ref, spread, held, total) = refs[:n_in], refs[n_in:]
    tiles, width, side = out_ref.shape
    collect(spread, pieces, table[SINGLES, ROW_AT], side)
    for tile in range(spread.shape[0]):
        value = spread[tile] * scale_ref[:, tile * side : (tile + 1) * side]
        high = value.astype(jnp.bfloat16)
        held[tile, :width] = high
        held[tile, width:] = (value - high.astype(jnp.float32)).astype(jnp.bfloat16)
    total[...] = jnp.zeros_like(total)
    forward(ALL, table=table, held=held, tile_ref=tile_ref, total=total)
    out_ref[...] = total[:tiles]


def add(refs):
    total = refs[0][...].astype(jnp.float32)
    for ref in refs[1:]:
        total = total + ref[...].astype(jnp.float32)
    return total


def start_body(place, panel_ref, degree_ref, out_ref, held, degrees, sems):
    share = panel_ref.shape[1]
    at = pl.multiple_of(place[0] * share, 128)
    loads = [
        pltpu.make_async_copy(degree_ref, degrees, sems.at[0]),
        pltpu.make_async_copy(panel_ref, held, sems.at[1]),
    ]
    for load in loads:
        load.start()
    for load in loads:
        load.wait()
    scale = 1.0 / jnp.sqrt(degrees[:, pl.ds(at, share)].astype(jnp.float32))
    out_ref[...] = (held[...] * scale).astype(out_ref.dtype)


def write_table(table, ids, place, per, query_tiles, product_tiles):
    slots = ids.shape[1]
    for which in range(LISTS):
        table[SINGLES, which] = 0
        for at in range(slots):
            table[which * FIELDS + SLOT, at] = 0
            table[which * FIELDS + QUERY_GIVE, at] = query_tiles
            table[which * FIELDS + PRODUCT_TAKE, at] = 0
            table[which * FIELDS + QUERY_TAKE, at] = 0
            table[which * FIELDS + PRODUCT_GIVE, at] = product_tiles
    table[SINGLES, ROW_AT] = place[0]
    table[SINGLES, COL_AT] = place[1]

    def step(slot, carry):
        query, product = ids[0, slot], ids[1, slot]
        for which in (query // per % 2, ALL):
            at = table[SINGLES, which]
            table[which * FIELDS + SLOT, at] = slot
            table[which * FIELDS + QUERY_GIVE, at] = query
            table[which * FIELDS + PRODUCT_TAKE, at] = product
            table[which * FIELDS + QUERY_TAKE, at] = query
            table[which * FIELDS + PRODUCT_GIVE, at] = product
            table[SINGLES, which] = at + 1
        return carry

    lax.fori_loop(0, jnp.minimum(place[2], slots), step, 0)


def load_body(per, place, after_ref, tile_ref, id_ref, product_ref, query_ref, *refs):
    keep, my_product_ref, product_out, my_query_ref, table, ids, degrees, counts, sems = refs
    loads = [
        pltpu.make_async_copy(id_ref, ids, sems.at[0]),
        pltpu.make_async_copy(product_ref, degrees, sems.at[1]),
        pltpu.make_async_copy(query_ref, counts, sems.at[2]),
    ]
    part = tile_ref.shape[0] // LOADS
    for step in range(LOADS):
        span = pl.ds(step * part, part)
        loads.append(pltpu.make_async_copy(tile_ref.at[span], keep.at[span], sems.at[3 + step]))
    for load in loads:
        load.start()
    loads[0].wait()
    side = tile_ref.shape[1]
    write_table(table, ids, place, per, query_ref.shape[1] // side, product_ref.shape[1] // side)
    loads[1].wait()
    product_out[...] = 1.0 / jnp.sqrt(degrees[...].astype(jnp.float32))
    share = my_product_ref.shape[1]
    at = pl.multiple_of(place[0] * share, 128)
    my_product_ref[...] = product_out[:, pl.ds(at, share)]
    loads[2].wait()
    columns = my_query_ref.shape[1]
    if columns % 128 == 0:
        at = pl.multiple_of(place[1] * columns, 128)
        my_query_ref[...] = 1.0 / jnp.sqrt(counts[:, pl.ds(at, columns)].astype(jnp.float32))
    else:
        for step in range(counts.shape[1] // columns):

            @pl.when(place[1] == step)
            def _():
                degree = counts[:, step * columns : (step + 1) * columns]
                my_query_ref[...] = 1.0 / jnp.sqrt(degree.astype(jnp.float32))
    for load in loads[3:]:
        load.wait()


def pair_body(mine_ref, got_ref, *outs):
    count = len(outs)
    for at, out_ref in enumerate(outs):
        step = (count - at) % count
        out_ref[...] = (mine_ref[step] + got_ref[step]).astype(out_ref.dtype)


def join_body(*refs):
    for step, ref in enumerate(refs[:-1]):
        refs[-1][step] = ref[...]


def query_body(*refs):
    part_refs, scale_ref, out_ref = refs[:-2], refs[-2], refs[-1]
    out_ref[...] = (add(part_refs) * scale_ref[...]).astype(out_ref.dtype)


def lift_only_body(*refs):
    part_refs, scale_ref, lifted_ref = refs[:-2], refs[-2], refs[-1]
    lifted_ref[...] = add(part_refs) * scale_ref[...]


def lift_body(*refs):
    part_refs, scale_ref, lifted_ref, gram_ref = refs[:-3], refs[-3], refs[-2], refs[-1]
    lifted = add(part_refs) * scale_ref[...]
    lifted_ref[...] = lifted
    gram_ref[...] = lax.dot_general(lifted, lifted, NT, precision=HIGH, preferred_element_type=jnp.float32)


def gram_body(*refs):
    total = jnp.zeros(refs[-1].shape, jnp.float32)
    for ref in refs[:-1]:
        total = total + lax.dot_general(
            ref[...], ref[...], NT, precision=HIGH, preferred_element_type=jnp.float32
        )
    refs[-1][...] = total


def sum_body(*refs):
    refs[-1][...] = add(refs[:-1])


def apply_tile(inverse, total_ref, owner, out_ref):
    width, share = out_ref.shape
    side = total_ref.shape[2]
    if share >= side:
        for piece in range(share // side):
            out_ref[:, piece * side : (piece + 1) * side] = lax.dot_general(
                inverse,
                total_ref[owner * (share // side) + piece],
                NN,
                precision=HIGH,
                preferred_element_type=jnp.float32,
            )
    else:
        per = side // share
        for at in range(per):

            @pl.when(owner % per == at)
            def _():
                out_ref[...] = lax.dot_general(
                    inverse,
                    total_ref[owner // per],
                    NN,
                    precision=HIGH,
                    preferred_element_type=jnp.float32,
                )[:, at * share : (at + 1) * share]


def apply_other_body(n_in, table, *refs):
    grams, (total_ref, inverse_ref, other_ref) = refs[:n_in], refs[n_in:]
    inverse = inverse_factor(add(grams))
    inverse_ref[...] = inverse
    for step in range(other_ref.shape[0]):
        apply_tile(inverse, total_ref, table[SINGLES, COL_AT] ^ (2 * step + 1), other_ref.at[step])


def apply_mine_body(table, inverse_ref, total_ref, mine_ref):
    for step in range(mine_ref.shape[0]):
        apply_tile(inverse_ref[...], total_ref, table[SINGLES, COL_AT] ^ (2 * step), mine_ref.at[step])


def finish_body(after, *refs):
    grams, lifted_ref, out_ref = refs[:-2], refs[-2], refs[-1]
    out_ref[...] = (
        lax.dot_general(
            inverse_factor(add(grams)), lifted_ref[...], NN, precision=HIGH, preferred_element_type=jnp.float32
        )
        * after
    )


def swap(value, axis, step):
    return lax.ppermute(value, axis, [(i, i ^ step) for i in range(lax.axis_size(axis))])


def spread_to(value, axis, stride=1):
    return [value] + [swap(value, axis, step) for step in range(stride, lax.axis_size(axis), stride)]


def deal(values, axis, stride=1):
    count = len(values)
    return [values[0]] + [swap(value, axis, (count - at) * stride) for at, value in enumerate(values[1:], 1)]


def add_up(*values):
    return call(sum_body, "sum", [WHOLE] * len(values), f32(*values[0].shape))(*values)


def terms_over_col(gram):
    return spread_to(add_up(gram, swap(gram, "col", 1)), "col", 2)


def shards(tiles, tile_ids, tile_count, query_degree, product_degree, panel):
    tile_set = tiles[0, 0]
    ids = tile_ids[0, 0]
    slots, side, _ = tile_set.shape
    width, share = panel.shape
    queries, products = query_degree.shape[0], product_degree.shape[0]
    query_tiles, product_tiles = queries // side, products // side
    n_row, n_col = lax.axis_size("row"), lax.axis_size("col")
    chips = n_col // 2
    row_at, col_at = lax.axis_index("row").astype(jnp.int32), lax.axis_index("col").astype(jnp.int32)
    columns = queries // n_col
    work = dict(flops=2 * slots * width * side * side, moved=2 * slots * side * side)
    scaled = call(
        start_body,
        "start",
        [SCALARS, AWAY, AWAY],
        bf16(width, share),
        [
            pltpu.VMEM((width, share), jnp.float32),
            pltpu.VMEM((1, products), jnp.int32),
            pltpu.SemaphoreType.DMA((2,)),
        ],
    )(row_at[None], in_hbm(panel), in_hbm(product_degree[None, :]))
    pieces = spread_to(scaled, "row")
    split = columns % side == 0
    tile_set, my_pscale, pscale, my_qscale, table = call(
        functools.partial(load_body, max(columns // side, 1)),
        "load",
        [SCALARS, WHOLE] + [AWAY] * 4,
        [
            pltpu.VMEM((slots, side, side), jnp.bfloat16),
            f32(1, share),
            f32(1, products),
            f32(1, columns),
            jax.ShapeDtypeStruct((SINGLES + 1, slots), jnp.int32),
        ],
        [
            pltpu.SMEM(ids.shape, jnp.int32),
            pltpu.VMEM((1, products), jnp.int32),
            pltpu.VMEM((1, queries), jnp.int32),
            pltpu.SemaphoreType.DMA((3 + LOADS,)),
        ],
        moved=4 * slots * side * side,
        out_specs=[WHOLE] * 4 + [SCALARS],
    )(
        jnp.stack([row_at, col_at, tile_count[0, 0]]),
        scaled,
        in_hbm(tile_set),
        in_hbm(ids),
        in_hbm(product_degree[None, :]),
        in_hbm(query_degree[None, :]),
    )
    tile_set = pltpu.with_memory_space_constraint(tile_set, pltpu.VMEM)
    root_count = math.sqrt(products * n_col)
    half = f32(chips, width, columns)
    half_work = dict(flops=slots * width * side * side, moved=slots * side * side)
    query_scratch = pltpu.VMEM((query_tiles + 1, width, side), jnp.float32)
    product_scratch = pltpu.VMEM((product_tiles + 1, width, side), jnp.float32)
    query_held = pltpu.VMEM((query_tiles, width, side), jnp.bfloat16)
    for iteration in range(ITERS):
        if iteration > 0:
            pieces = spread_to(lifted, "row")
            gram = call(gram_body, "gram", [WHOLE] * n_row, f32(width, width))(*pieces)
            grams = terms_over_col(gram)
            total = call(
                functools.partial(next_body, n_row),
                "forward",
                [SCALARS] + [WHOLE] * (n_row + 2),
                f32(query_tiles, width, side),
                [
                    pltpu.VMEM((product_tiles, width, side), jnp.float32),
                    pltpu.VMEM((product_tiles, 2 * width, side), jnp.bfloat16),
                    query_scratch,
                ],
                **work,
            )(table, *pieces, pscale, tile_set)
            inverse, other = call(
                functools.partial(apply_other_body, chips),
                "apply",
                [SCALARS] + [WHOLE] * (chips + 1),
                [f32(width, width), half],
            )(table, *grams, total)
            got = swap(other, "col", 1)
            mine = call(apply_mine_body, "apply_rest", [SCALARS] + [WHOLE] * 2, half, **half_work)(
                table, inverse, total
            )
        elif split:
            held, other = call(
                functools.partial(forward_other_body, n_row),
                "forward",
                [SCALARS] + [WHOLE] * (n_row + 1),
                [bf16(product_tiles, width, side), half],
                [query_scratch],
                **half_work,
            )(table, *pieces, tile_set)
            got = swap(other, "col", 1)
            mine = call(
                forward_mine_body,
                "forward_rest",
                [SCALARS] + [WHOLE] * 2,
                half,
                [query_scratch],
                **half_work,
            )(table, held, tile_set)
        else:
            mine, other = call(
                functools.partial(forward_body, n_row),
                "forward",
                [SCALARS] + [WHOLE] * (n_row + 1),
                [half] * 2,
                [pltpu.VMEM((product_tiles, width, side), jnp.bfloat16), query_scratch],
                **work,
            )(table, *pieces, tile_set)
            got = swap(other, "col", 1)
        sums = call(
            pair_body, "pair", [WHOLE] * 2, [f32(width, columns)] + [bf16(width, columns)] * (chips - 1)
        )(mine, got)
        parts = deal(sums, "col", 2)
        rounded = call(query_body, "query", [WHOLE] * (chips + 1), bf16(width, columns))(*parts, my_qscale)
        pieces = spread_to(rounded, "col", 2)
        here = call(join_body, "join", [WHOLE] * chips, bf16(chips, width, columns))(*pieces)
        there = swap(here, "col", 1)
        if split:
            begun = call(
                functools.partial(back_mine_body, chips),
                "backward",
                [SCALARS] + [WHOLE] * (chips + 1),
                f32(product_tiles + 1, width, side),
                [query_held],
                **half_work,
            )(table, *pieces, tile_set)
            sums = call(
                back_other_body,
                "backward_rest",
                [SCALARS] + [WHOLE] * 3,
                [f32(width, share)] * n_row,
                [query_held, product_scratch],
                **half_work,
            )(table, there, begun, tile_set)
        else:
            sums = call(
                back_body,
                "backward",
                [SCALARS] + [WHOLE] * 3,
                [f32(width, share)] * n_row,
                [query_held, product_scratch],
                **work,
            )(table, here, there, tile_set)
        parts = deal(sums, "row")
        if iteration < ITERS - 1:
            lifted = call(lift_only_body, "lift", [WHOLE] * (n_row + 1), f32(width, share))(*parts, my_pscale)
    lifted, gram = call(
        lift_body, "lift", [WHOLE] * (n_row + 1), [f32(width, share), f32(width, width)]
    )(*parts, my_pscale)
    return call(
        functools.partial(finish_body, root_count), "finish", [WHOLE] * (chips + 1), f32(width, share)
    )(*terms_over_col(add_up(*spread_to(gram, "row"))), lifted)


def solution(mesh):
    in_specs = (
        P("row", "col", None, None, None),
        P("row", "col", None, None),
        P("row", "col"),
        P("row"),
        P("col"),
        P(None, ("col", "row")),
    )
    out_specs = P(None, ("col", "row"))
    return jax.shard_map(shards, mesh=mesh, in_specs=in_specs, out_specs=out_specs, check_vma=False)
```

```python
import functools
import math

import jax
import jax.numpy as jnp
from jax import lax
from jax.experimental import pallas as pl
from jax.experimental.pallas import tpu as pltpu
from jax.sharding import PartitionSpec as P

ITERS = 2
GROUP = 8
LOADS = 8
PANEL_STEP = 8
HIGH = lax.Precision.HIGHEST
VMEM_BYTES = 12 * 1024 * 1024
NT = (((1,), (1,)), ((), ()))
NN = (((1,), (0,)), ((), ()))

def inverse_factor(gram):
    width = gram.shape[0]
    rows = lax.broadcasted_iota(jnp.int32, (width, width), 0)
    cols = lax.broadcasted_iota(jnp.int32, (width, width), 1)
    work = jnp.concatenate([gram, (rows == cols).astype(jnp.float32)], axis=1)
    done = []
    for first in range(0, width, PANEL_STEP):
        height = width - first
        columns = [
            jnp.broadcast_to(work[:, first + j : first + j + 1], (height, 2 * width))
            for j in range(PANEL_STEP)
        ]
        for j in range(PANEL_STEP):
            scale = lax.rsqrt(columns[j][j : j + 1, :])
            row = work[j : j + 1, :] * scale
            factor = columns[j] * scale
            done.append(row)
            for later in range(j + 1, PANEL_STEP):
                columns[later] = columns[later] - factor * (columns[later][j : j + 1, :] * scale)
            work = work - factor * row
        work = work[PANEL_STEP:, :]
    return jnp.concatenate(done, axis=0)[:, width:]


SLOT, QUERY_GIVE, PRODUCT_TAKE, QUERY_TAKE, PRODUCT_GIVE = range(5)
FIELDS, LISTS, ALL = 5, 3, 2
SINGLES = FIELDS * LISTS
ROW_AT, COL_AT = 3, 4
WHOLE = pl.BlockSpec(memory_space=pltpu.VMEM)
SCALARS = pl.BlockSpec(memory_space=pltpu.SMEM)
AWAY = pl.BlockSpec(memory_space=pltpu.MemorySpace.HBM)


def call(body, name, in_specs, out_shape, scratch=(), flops=0, moved=0, out_specs=None):
    many = isinstance(out_shape, (tuple, list))
    return pl.pallas_call(
        body,
        out_shape=out_shape,
        in_specs=in_specs,
        out_specs=out_specs or ([WHOLE] * len(out_shape) if many else WHOLE),
        scratch_shapes=scratch,
        compiler_params=pltpu.CompilerParams(vmem_limit_bytes=VMEM_BYTES),
        cost_estimate=pl.CostEstimate(flops=flops, bytes_accessed=moved, transcendentals=0),
        name=name,
    )


def in_hbm(value):
    return pltpu.with_memory_space_constraint(value, pltpu.MemorySpace.HBM)


def f32(*shape):
    return jax.ShapeDtypeStruct(shape, jnp.float32)


def bf16(*shape):
    return jax.ShapeDtypeStruct(shape, jnp.bfloat16)


def put(held, owner, value, side):
    share = value.shape[1]
    if share >= side:
        per = share // side
        for piece in range(per):
            held[owner * per + piece] = value[:, piece * side : (piece + 1) * side]
    else:
        per = side // share
        for at in range(per):

            @pl.when(owner % per == at)
            def _():
                held[owner // per, :, at * share : (at + 1) * share] = value


def get(total, owner, out_ref, side):
    share = out_ref.shape[1]
    if share >= side:
        per = share // side
        for piece in range(per):
            out_ref[:, piece * side : (piece + 1) * side] = total[owner * per + piece].astype(out_ref.dtype)
    else:
        per = side // share
        for at in range(per):

            @pl.when(owner % per == at)
            def _():
                out_ref[...] = total[owner // per, :, at * share : (at + 1) * share].astype(out_ref.dtype)


def emit(total, out_refs, me, side):
    count = len(out_refs)
    for at, out_ref in enumerate(out_refs):
        get(total, me ^ ((count - at) % count), out_ref, side)


def collect(held, piece_refs, me, side):
    for step, piece_ref in enumerate(piece_refs):
        put(held, me ^ step, piece_ref[...], side)


def products(which, take, give, dims, table, held, tile_ref, total):
    width = total.shape[1]
    slots = tile_ref.shape[0]

    def run(first, length):
        for lane in range(length):
            at = first + lane
            term = lax.dot_general(
                held[table[which * FIELDS + take, at]],
                tile_ref[table[which * FIELDS + SLOT, at]],
                dims,
                preferred_element_type=jnp.float32,
            )
            if term.shape[0] > width:
                term = term[:width] + term[width:]
            total[table[which * FIELDS + give, at]] += term

    if isinstance(which, int):
        run(0, slots)
        return

    def step(g, carry):
        run(slots // 2 + g * GROUP, GROUP)
        return carry

    run(0, slots // 2)
    rest = jnp.maximum(table[SINGLES, which] - slots // 2, 0)
    lax.fori_loop(0, jnp.minimum((rest + GROUP - 1) // GROUP, slots // 2 // GROUP), step, 0)


forward = functools.partial(products, take=PRODUCT_TAKE, give=QUERY_GIVE, dims=NT)
backward = functools.partial(products, take=QUERY_TAKE, give=PRODUCT_GIVE, dims=NN)


def emit_half(total, out_ref, me, side, flip):
    for step in range(out_ref.shape[0]):
        get(total, me ^ (2 * step + flip), out_ref.at[step], side)


def collect_half(held, piece_refs, me, side, flip):
    for step, piece_ref in enumerate(piece_refs):
        put(held, me ^ (2 * step + flip), piece_ref[...], side)


def forward_body(n_in, table, *refs):
    pieces, (tile_ref, mine_ref, other_ref, held, total) = refs[:n_in], refs[n_in:]
    side = tile_ref.shape[1]
    collect(held, pieces, table[SINGLES, ROW_AT], side)
    total[...] = jnp.zeros_like(total)
    forward(ALL, table=table, held=held, tile_ref=tile_ref, total=total)
    emit_half(total, mine_ref, table[SINGLES, COL_AT], side, 0)
    emit_half(total, other_ref, table[SINGLES, COL_AT], side, 1)


def forward_other_body(n_in, table, *refs):
    pieces, (tile_ref, held, other_ref, total) = refs[:n_in], refs[n_in:]
    side, me = tile_ref.shape[1], table[SINGLES, COL_AT]
    collect(held, pieces, table[SINGLES, ROW_AT], side)
    total[...] = jnp.zeros_like(total)
    forward(1 - me % 2, table=table, held=held, tile_ref=tile_ref, total=total)
    emit_half(total, other_ref, me, side, 1)


def forward_mine_body(table, held, tile_ref, mine_ref, total):
    side, me = tile_ref.shape[1], table[SINGLES, COL_AT]
    total[...] = jnp.zeros_like(total)
    forward(me % 2, table=table, held=held, tile_ref=tile_ref, total=total)
    emit_half(total, mine_ref, me, side, 0)


def back_body(table, here_ref, there_ref, tile_ref, *refs):
    out_refs, (held, total) = refs[:-2], refs[-2:]
    side = tile_ref.shape[1]
    for flip, ref in enumerate((here_ref, there_ref)):
        collect_half(held, [ref.at[step] for step in range(ref.shape[0])], table[SINGLES, COL_AT], side, flip)
    total[...] = jnp.zeros_like(total)
    backward(ALL, table=table, held=held, tile_ref=tile_ref, total=total)
    emit(total, out_refs, table[SINGLES, ROW_AT], side)


def back_mine_body(n_in, table, *refs):
    pieces, (tile_ref, total, held) = refs[:n_in], refs[n_in:]
    me = table[SINGLES, COL_AT]
    collect_half(held, pieces, me, tile_ref.shape[1], 0)
    total[...] = jnp.zeros_like(total)
    backward(me % 2, table=table, held=held, tile_ref=tile_ref, total=total)


def back_other_body(table, there_ref, begun_ref, tile_ref, *refs):
    out_refs, (held, total) = refs[:-2], refs[-2:]
    side, me = tile_ref.shape[1], table[SINGLES, COL_AT]
    collect_half(held, [there_ref.at[step] for step in range(there_ref.shape[0])], me, side, 1)
    total[...] = begun_ref[...]
    backward(1 - me % 2, table=table, held=held, tile_ref=tile_ref, total=total)
    emit(total, out_refs, table[SINGLES, ROW_AT], side)


def pack_gram(gram, columns):
    per = columns // gram.shape[0]
    rows = gram.shape[0] // per
    return jnp.concatenate([gram[at * rows : (at + 1) * rows] for at in range(per)], axis=1)


def unpack_gram(rows, width):
    return jnp.concatenate([rows[:, at : at + width] for at in range(0, rows.shape[1], width)], axis=0)


def split_panel(pieces, scale_ref, spread, held, me):
    width, side = spread.shape[1:]
    collect(spread, pieces, me, side)
    for tile in range(spread.shape[0]):
        value = spread[tile] * scale_ref[:, tile * side : (tile + 1) * side]
        high = value.astype(jnp.bfloat16)
        held[tile, :width] = high
        held[tile, width:] = (value - high.astype(jnp.float32)).astype(jnp.bfloat16)
    gram = jnp.zeros((width, width), jnp.float32)
    for piece in pieces:
        gram = gram + lax.dot_general(
            piece[...], piece[...], NT, precision=HIGH, preferred_element_type=jnp.float32
        )
    return gram


def emit_rows(total, out_ref, chips, me, side, flip):
    width = total.shape[1]
    for step in range(chips):
        get(total, me ^ (2 * step + flip), out_ref.at[step * width : (step + 1) * width], side)


def next_body(n_in, chips, table, *refs):
    pieces, (scale_ref, tile_ref, mine_ref, other_ref, gram_ref, spread, held, total) = refs[:n_in], refs[n_in:]
    side, me, width = tile_ref.shape[1], table[SINGLES, COL_AT], total.shape[1]
    rows = pack_gram(split_panel(pieces, scale_ref, spread, held, table[SINGLES, ROW_AT]), gram_ref.shape[1])
    gram_ref[...] = rows
    other_ref[chips * width :] = rows
    total[...] = jnp.zeros_like(total)
    forward(ALL, table=table, held=held, tile_ref=tile_ref, total=total)
    emit_rows(total, mine_ref, chips, me, side, 0)
    emit_rows(total, other_ref, chips, me, side, 1)


def next_other_body(n_in, chips, table, *refs):
    pieces, (scale_ref, tile_ref, held, other_ref, gram_ref, spread, total) = refs[:n_in], refs[n_in:]
    side, me, width = tile_ref.shape[1], table[SINGLES, COL_AT], total.shape[1]
    rows = pack_gram(split_panel(pieces, scale_ref, spread, held, table[SINGLES, ROW_AT]), gram_ref.shape[1])
    gram_ref[...] = rows
    other_ref[chips * width :] = rows
    total[...] = jnp.zeros_like(total)
    forward(1 - me % 2, table=table, held=held, tile_ref=tile_ref, total=total)
    emit_rows(total, other_ref, chips, me, side, 1)


def next_mine_body(chips, table, held, tile_ref, mine_ref, total):
    side, me = tile_ref.shape[1], table[SINGLES, COL_AT]
    total[...] = jnp.zeros_like(total)
    forward(me % 2, table=table, held=held, tile_ref=tile_ref, total=total)
    emit_rows(total, mine_ref, chips, me, side, 0)


def next_pair_body(width, mine_ref, got_ref, gram_ref, *outs):
    count = len(outs)
    gram = gram_ref[...] + got_ref[count * width :]
    for at, out_ref in enumerate(outs):
        step = (count - at) % count
        span = slice(step * width, (step + 1) * width)
        out_ref[:width] = mine_ref[span] + got_ref[span]
        out_ref[width:] = gram


def next_query_body(*refs):
    part_refs, scale_ref, out_ref = refs[:-2], refs[-2], refs[-1]
    width = out_ref.shape[0]
    total = add(part_refs)
    inverse = inverse_factor(unpack_gram(total[width:], width))
    current = lax.dot_general(inverse, total[:width], NN, precision=HIGH, preferred_element_type=jnp.float32)
    out_ref[...] = (current * scale_ref[...]).astype(out_ref.dtype)


def add(refs):
    total = refs[0][...].astype(jnp.float32)
    for ref in refs[1:]:
        total = total + ref[...].astype(jnp.float32)
    return total


def start_body(place, panel_ref, degree_ref, out_ref, held, degrees, sems):
    share = panel_ref.shape[1]
    at = pl.multiple_of(place[0] * share, 128)
    loads = [
        pltpu.make_async_copy(degree_ref, degrees, sems.at[0]),
        pltpu.make_async_copy(panel_ref, held, sems.at[1]),
    ]
    for load in loads:
        load.start()
    for load in loads:
        load.wait()
    scale = 1.0 / jnp.sqrt(degrees[:, pl.ds(at, share)].astype(jnp.float32))
    out_ref[...] = (held[...] * scale).astype(out_ref.dtype)


def write_table(table, ids, place, per, query_tiles, product_tiles):
    slots = ids.shape[1]
    for which in range(LISTS):
        table[SINGLES, which] = 0
        for at in range(slots):
            table[which * FIELDS + SLOT, at] = 0
            table[which * FIELDS + QUERY_GIVE, at] = query_tiles
            table[which * FIELDS + PRODUCT_TAKE, at] = 0
            table[which * FIELDS + QUERY_TAKE, at] = 0
            table[which * FIELDS + PRODUCT_GIVE, at] = product_tiles
    table[SINGLES, ROW_AT] = place[0]
    table[SINGLES, COL_AT] = place[1]

    def step(slot, carry):
        query, product = ids[0, slot], ids[1, slot]
        for which in (query // per % 2, ALL):
            at = table[SINGLES, which]
            table[which * FIELDS + SLOT, at] = slot
            table[which * FIELDS + QUERY_GIVE, at] = query
            table[which * FIELDS + PRODUCT_TAKE, at] = product
            table[which * FIELDS + QUERY_TAKE, at] = query
            table[which * FIELDS + PRODUCT_GIVE, at] = product
            table[SINGLES, which] = at + 1
        return carry

    lax.fori_loop(0, jnp.minimum(place[2], slots), step, 0)


def load_body(per, place, after_ref, tile_ref, id_ref, product_ref, query_ref, *refs):
    keep, my_product_ref, product_out, my_query_ref, table, ids, degrees, counts, sems = refs
    loads = [
        pltpu.make_async_copy(id_ref, ids, sems.at[0]),
        pltpu.make_async_copy(product_ref, degrees, sems.at[1]),
        pltpu.make_async_copy(query_ref, counts, sems.at[2]),
    ]
    part = tile_ref.shape[0] // LOADS
    for step in range(LOADS):
        span = pl.ds(step * part, part)
        loads.append(pltpu.make_async_copy(tile_ref.at[span], keep.at[span], sems.at[3 + step]))
    for load in loads:
        load.start()
    loads[0].wait()
    side = tile_ref.shape[1]
    write_table(table, ids, place, per, query_ref.shape[1] // side, product_ref.shape[1] // side)
    loads[1].wait()
    product_out[...] = 1.0 / jnp.sqrt(degrees[...].astype(jnp.float32))
    share = my_product_ref.shape[1]
    at = pl.multiple_of(place[0] * share, 128)
    my_product_ref[...] = product_out[:, pl.ds(at, share)]
    loads[2].wait()
    columns = my_query_ref.shape[1]
    if columns % 128 == 0:
        at = pl.multiple_of(place[1] * columns, 128)
        my_query_ref[...] = 1.0 / jnp.sqrt(counts[:, pl.ds(at, columns)].astype(jnp.float32))
    else:
        for step in range(counts.shape[1] // columns):

            @pl.when(place[1] == step)
            def _():
                degree = counts[:, step * columns : (step + 1) * columns]
                my_query_ref[...] = 1.0 / jnp.sqrt(degree.astype(jnp.float32))
    for load in loads[3:]:
        load.wait()


def pair_body(mine_ref, got_ref, *outs):
    count = len(outs)
    for at, out_ref in enumerate(outs):
        step = (count - at) % count
        out_ref[...] = (mine_ref[step] + got_ref[step]).astype(out_ref.dtype)


def join_body(*refs):
    for step, ref in enumerate(refs[:-1]):
        refs[-1][step] = ref[...]


def query_body(*refs):
    part_refs, scale_ref, out_ref = refs[:-2], refs[-2], refs[-1]
    out_ref[...] = (add(part_refs) * scale_ref[...]).astype(out_ref.dtype)


def lift_only_body(*refs):
    part_refs, scale_ref, lifted_ref = refs[:-2], refs[-2], refs[-1]
    lifted_ref[...] = add(part_refs) * scale_ref[...]


def lift_body(*refs):
    part_refs, scale_ref, lifted_ref, gram_ref = refs[:-3], refs[-3], refs[-2], refs[-1]
    lifted = add(part_refs) * scale_ref[...]
    lifted_ref[...] = lifted
    gram_ref[...] = lax.dot_general(lifted, lifted, NT, precision=HIGH, preferred_element_type=jnp.float32)


def sum_body(*refs):
    refs[-1][...] = add(refs[:-1])


def finish_body(after, *refs):
    grams, lifted_ref, out_ref = refs[:-2], refs[-2], refs[-1]
    out_ref[...] = (
        lax.dot_general(
            inverse_factor(add(grams)), lifted_ref[...], NN, precision=HIGH, preferred_element_type=jnp.float32
        )
        * after
    )


def swap(value, axis, step):
    return lax.ppermute(value, axis, [(i, i ^ step) for i in range(lax.axis_size(axis))])


def spread_to(value, axis, stride=1):
    return [value] + [swap(value, axis, step) for step in range(stride, lax.axis_size(axis), stride)]


def deal(values, axis, stride=1):
    count = len(values)
    return [values[0]] + [swap(value, axis, (count - at) * stride) for at, value in enumerate(values[1:], 1)]


def add_up(*values):
    return call(sum_body, "sum", [WHOLE] * len(values), f32(*values[0].shape))(*values)


def terms_over_col(gram):
    return spread_to(add_up(gram, swap(gram, "col", 1)), "col", 2)


def shards(tiles, tile_ids, tile_count, query_degree, product_degree, panel):
    tile_set = tiles[0, 0]
    ids = tile_ids[0, 0]
    slots, side, _ = tile_set.shape
    width, share = panel.shape
    queries, products = query_degree.shape[0], product_degree.shape[0]
    query_tiles, product_tiles = queries // side, products // side
    n_row, n_col = lax.axis_size("row"), lax.axis_size("col")
    chips = n_col // 2
    row_at, col_at = lax.axis_index("row").astype(jnp.int32), lax.axis_index("col").astype(jnp.int32)
    columns = queries // n_col
    work = dict(flops=2 * slots * width * side * side, moved=2 * slots * side * side)
    scaled = call(
        start_body,
        "start",
        [SCALARS, AWAY, AWAY],
        bf16(width, share),
        [
            pltpu.VMEM((width, share), jnp.float32),
            pltpu.VMEM((1, products), jnp.int32),
            pltpu.SemaphoreType.DMA((2,)),
        ],
    )(row_at[None], in_hbm(panel), in_hbm(product_degree[None, :]))
    pieces = spread_to(scaled, "row")
    split = columns % side == 0
    tile_set, my_pscale, pscale, my_qscale, table = call(
        functools.partial(load_body, max(columns // side, 1)),
        "load",
        [SCALARS, WHOLE] + [AWAY] * 4,
        [
            pltpu.VMEM((slots, side, side), jnp.bfloat16),
            f32(1, share),
            f32(1, products),
            f32(1, columns),
            jax.ShapeDtypeStruct((SINGLES + 1, slots), jnp.int32),
        ],
        [
            pltpu.SMEM(ids.shape, jnp.int32),
            pltpu.VMEM((1, products), jnp.int32),
            pltpu.VMEM((1, queries), jnp.int32),
            pltpu.SemaphoreType.DMA((3 + LOADS,)),
        ],
        moved=4 * slots * side * side,
        out_specs=[WHOLE] * 4 + [SCALARS],
    )(
        jnp.stack([row_at, col_at, tile_count[0, 0]]),
        scaled,
        in_hbm(tile_set),
        in_hbm(ids),
        in_hbm(product_degree[None, :]),
        in_hbm(query_degree[None, :]),
    )
    tile_set = pltpu.with_memory_space_constraint(tile_set, pltpu.VMEM)
    root_count = math.sqrt(products * n_col)
    half = f32(chips, width, columns)
    gram_rows = width * width // columns
    half_work = dict(flops=slots * width * side * side, moved=slots * side * side)
    query_scratch = pltpu.VMEM((query_tiles + 1, width, side), jnp.float32)
    product_scratch = pltpu.VMEM((product_tiles + 1, width, side), jnp.float32)
    query_held = pltpu.VMEM((query_tiles, width, side), jnp.bfloat16)
    for iteration in range(ITERS):
        if iteration > 0:
            pieces = spread_to(lifted, "row")
            arrays = [WHOLE] * (n_row + 2)
            message = f32(chips * width + gram_rows, columns)
            spread = pltpu.VMEM((product_tiles, width, side), jnp.float32)
            if split:
                held, other, gram = call(
                    functools.partial(next_other_body, n_row, chips),
                    "forward",
                    [SCALARS] + arrays,
                    [bf16(product_tiles, 2 * width, side), message, f32(gram_rows, columns)],
                    [spread, query_scratch],
                    **half_work,
                )(table, *pieces, pscale, tile_set)
                got = swap(other, "col", 1)
                mine = call(
                    functools.partial(next_mine_body, chips),
                    "forward_rest",
                    [SCALARS] + [WHOLE] * 2,
                    f32(chips * width, columns),
                    [query_scratch],
                    **half_work,
                )(table, held, tile_set)
            else:
                mine, other, gram = call(
                    functools.partial(next_body, n_row, chips),
                    "forward",
                    [SCALARS] + arrays,
                    [f32(chips * width, columns), message, f32(gram_rows, columns)],
                    [spread, pltpu.VMEM((product_tiles, 2 * width, side), jnp.bfloat16), query_scratch],
                    **work,
                )(table, *pieces, pscale, tile_set)
                got = swap(other, "col", 1)
            sums = call(
                functools.partial(next_pair_body, width),
                "pair",
                [WHOLE] * 3,
                [f32(width + gram_rows, columns)] * chips,
            )(mine, got, gram)
        elif split:
            held, other = call(
                functools.partial(forward_other_body, n_row),
                "forward",
                [SCALARS] + [WHOLE] * (n_row + 1),
                [bf16(product_tiles, width, side), half],
                [query_scratch],
                **half_work,
            )(table, *pieces, tile_set)
            got = swap(other, "col", 1)
            mine = call(
                forward_mine_body,
                "forward_rest",
                [SCALARS] + [WHOLE] * 2,
                half,
                [query_scratch],
                **half_work,
            )(table, held, tile_set)
        else:
            mine, other = call(
                functools.partial(forward_body, n_row),
                "forward",
                [SCALARS] + [WHOLE] * (n_row + 1),
                [half] * 2,
                [pltpu.VMEM((product_tiles, width, side), jnp.bfloat16), query_scratch],
                **work,
            )(table, *pieces, tile_set)
            got = swap(other, "col", 1)
        if iteration == 0:
            sums = call(
                pair_body, "pair", [WHOLE] * 2, [f32(width, columns)] + [bf16(width, columns)] * (chips - 1)
            )(mine, got)
        parts = deal(sums, "col", 2)
        rounded = call(next_query_body if iteration else query_body, "query", [WHOLE] * (chips + 1), bf16(width, columns))(*parts, my_qscale)
        pieces = spread_to(rounded, "col", 2)
        here = call(join_body, "join", [WHOLE] * chips, bf16(chips, width, columns))(*pieces)
        there = swap(here, "col", 1)
        if split:
            begun = call(
                functools.partial(back_mine_body, chips),
                "backward",
                [SCALARS] + [WHOLE] * (chips + 1),
                f32(product_tiles + 1, width, side),
                [query_held],
                **half_work,
            )(table, *pieces, tile_set)
            sums = call(
                back_other_body,
                "backward_rest",
                [SCALARS] + [WHOLE] * 3,
                [f32(width, share)] * n_row,
                [query_held, product_scratch],
                **half_work,
            )(table, there, begun, tile_set)
        else:
            sums = call(
                back_body,
                "backward",
                [SCALARS] + [WHOLE] * 3,
                [f32(width, share)] * n_row,
                [query_held, product_scratch],
                **work,
            )(table, here, there, tile_set)
        parts = deal(sums, "row")
        if iteration < ITERS - 1:
            lifted = call(lift_only_body, "lift", [WHOLE] * (n_row + 1), f32(width, share))(*parts, my_pscale)
    lifted, gram = call(
        lift_body, "lift", [WHOLE] * (n_row + 1), [f32(width, share), f32(width, width)]
    )(*parts, my_pscale)
    return call(
        functools.partial(finish_body, root_count), "finish", [WHOLE] * (chips + 1), f32(width, share)
    )(*terms_over_col(add_up(*spread_to(gram, "row"))), lifted)


def solution(mesh):
    in_specs = (
        P("row", "col", None, None, None),
        P("row", "col", None, None),
        P("row", "col"),
        P("row"),
        P("col"),
        P(None, ("col", "row")),
    )
    out_specs = P(None, ("col", "row"))
    return jax.shard_map(shards, mesh=mesh, in_specs=in_specs, out_specs=out_specs, check_vma=False)
```

```python
import functools
import math

import jax
import jax.numpy as jnp
from jax import lax
from jax.experimental import pallas as pl
from jax.experimental.pallas import tpu as pltpu
from jax.sharding import PartitionSpec as P

ITERS = 2
GROUP = 8
LOADS = 8
SETS = 2
PANEL_STEP = 8
HIGH = lax.Precision.HIGHEST
VMEM_BYTES = 12 * 1024 * 1024
NT = (((1,), (1,)), ((), ()))
NN = (((1,), (0,)), ((), ()))

def inverse_factor(gram):
    width = gram.shape[0]
    rows = lax.broadcasted_iota(jnp.int32, (width, width), 0)
    cols = lax.broadcasted_iota(jnp.int32, (width, width), 1)
    work = jnp.concatenate([gram, (rows == cols).astype(jnp.float32)], axis=1)
    done = []
    for first in range(0, width, PANEL_STEP):
        height = width - first
        columns = [
            jnp.broadcast_to(work[:, first + j : first + j + 1], (height, 2 * width))
            for j in range(PANEL_STEP)
        ]
        for j in range(PANEL_STEP):
            scale = lax.rsqrt(columns[j][j : j + 1, :])
            row = work[j : j + 1, :] * scale
            factor = columns[j] * scale
            done.append(row)
            for later in range(j + 1, PANEL_STEP):
                columns[later] = columns[later] - factor * (columns[later][j : j + 1, :] * scale)
            work = work - factor * row
        work = work[PANEL_STEP:, :]
    return jnp.concatenate(done, axis=0)[:, width:]


SLOT, QUERY_GIVE, PRODUCT_TAKE, QUERY_TAKE, PRODUCT_GIVE = range(5)
FIELDS, LISTS, ALL = 5, 3, 2
SINGLES = FIELDS * LISTS
ROW_AT, COL_AT = 3, 4
WHOLE = pl.BlockSpec(memory_space=pltpu.VMEM)
SCALARS = pl.BlockSpec(memory_space=pltpu.SMEM)
AWAY = pl.BlockSpec(memory_space=pltpu.MemorySpace.HBM)


def call(body, name, in_specs, out_shape, scratch=(), flops=0, moved=0, out_specs=None):
    many = isinstance(out_shape, (tuple, list))
    return pl.pallas_call(
        body,
        out_shape=out_shape,
        in_specs=in_specs,
        out_specs=out_specs or ([WHOLE] * len(out_shape) if many else WHOLE),
        scratch_shapes=scratch,
        compiler_params=pltpu.CompilerParams(vmem_limit_bytes=VMEM_BYTES),
        cost_estimate=pl.CostEstimate(flops=flops, bytes_accessed=moved, transcendentals=0),
        name=name,
    )


def in_hbm(value):
    return pltpu.with_memory_space_constraint(value, pltpu.MemorySpace.HBM)


def f32(*shape):
    return jax.ShapeDtypeStruct(shape, jnp.float32)


def bf16(*shape):
    return jax.ShapeDtypeStruct(shape, jnp.bfloat16)


def put(held, owner, value, side, row=0):
    span, share = slice(row, row + value.shape[0]), value.shape[1]
    if share >= side:
        per = share // side
        for piece in range(per):
            held[owner * per + piece, span] = value[:, piece * side : (piece + 1) * side]
    else:
        per = side // share
        for at in range(per):

            @pl.when(owner % per == at)
            def _():
                held[owner // per, span, at * share : (at + 1) * share] = value


def get(total, owner, out_ref, side, row=0):
    span, share = slice(row, row + out_ref.shape[0]), out_ref.shape[1]
    if share >= side:
        per = share // side
        for piece in range(per):
            out_ref[:, piece * side : (piece + 1) * side] = total[owner * per + piece, span].astype(out_ref.dtype)
    else:
        per = side // share
        for at in range(per):

            @pl.when(owner % per == at)
            def _():
                out_ref[...] = total[owner // per, span, at * share : (at + 1) * share].astype(out_ref.dtype)


def emit(total, out_refs, me, side):
    sets = total.shape[1] // out_refs[0].shape[0]
    count = len(out_refs) // sets
    for at, out_ref in enumerate(out_refs):
        part, at = divmod(at, count)
        get(total, me ^ ((count - at) % count), out_ref, side, part * out_ref.shape[0])


def collect(held, piece_refs, me, side):
    sets = held.shape[1] // piece_refs[0].shape[0]
    count = len(piece_refs) // sets
    for at, piece_ref in enumerate(piece_refs):
        part, step = divmod(at, count)
        put(held, me ^ step, piece_ref[...], side, part * piece_ref.shape[0])


def products(which, take, give, dims, table, held, tile_ref, total):
    width = total.shape[1]
    slots = tile_ref.shape[0]

    def run(first, length):
        for lane in range(length):
            at = first + lane
            term = lax.dot_general(
                held[table[which * FIELDS + take, at]],
                tile_ref[table[which * FIELDS + SLOT, at]],
                dims,
                preferred_element_type=jnp.float32,
            )
            if term.shape[0] > width:
                term = term[:width] + term[width:]
            total[table[which * FIELDS + give, at]] += term

    if isinstance(which, int):
        run(0, slots)
        return

    def step(g, carry):
        run(slots // 2 + g * GROUP, GROUP)
        return carry

    run(0, slots // 2)
    rest = jnp.maximum(table[SINGLES, which] - slots // 2, 0)
    lax.fori_loop(0, jnp.minimum((rest + GROUP - 1) // GROUP, slots // 2 // GROUP), step, 0)


forward = functools.partial(products, take=PRODUCT_TAKE, give=QUERY_GIVE, dims=NT)
backward = functools.partial(products, take=QUERY_TAKE, give=PRODUCT_GIVE, dims=NN)


def emit_half(total, out_ref, me, side, flip):
    for step in range(out_ref.shape[0]):
        get(total, me ^ (2 * step + flip), out_ref.at[step], side)


def collect_half(held, piece_refs, me, side, flip):
    for step, piece_ref in enumerate(piece_refs):
        put(held, me ^ (2 * step + flip), piece_ref[...], side)


def forward_body(n_in, table, *refs):
    pieces, (tile_ref, mine_ref, other_ref, held, total) = refs[:n_in], refs[n_in:]
    side = tile_ref.shape[1]
    collect(held, pieces, table[SINGLES, ROW_AT], side)
    total[...] = jnp.zeros_like(total)
    forward(ALL, table=table, held=held, tile_ref=tile_ref, total=total)
    emit_half(total, mine_ref, table[SINGLES, COL_AT], side, 0)
    emit_half(total, other_ref, table[SINGLES, COL_AT], side, 1)


def forward_other_body(n_in, table, *refs):
    pieces, (tile_ref, held, other_ref, total) = refs[:n_in], refs[n_in:]
    side, me = tile_ref.shape[1], table[SINGLES, COL_AT]
    collect(held, pieces, table[SINGLES, ROW_AT], side)
    total[...] = jnp.zeros_like(total)
    forward(1 - me % 2, table=table, held=held, tile_ref=tile_ref, total=total)
    emit_half(total, other_ref, me, side, 1)


def forward_mine_body(table, held, tile_ref, mine_ref, total):
    side, me = tile_ref.shape[1], table[SINGLES, COL_AT]
    total[...] = jnp.zeros_like(total)
    forward(me % 2, table=table, held=held, tile_ref=tile_ref, total=total)
    emit_half(total, mine_ref, me, side, 0)


def back_body(table, here_ref, there_ref, tile_ref, *refs):
    out_refs, (held, total) = refs[:-2], refs[-2:]
    side = tile_ref.shape[1]
    for flip, ref in enumerate((here_ref, there_ref)):
        collect_half(held, [ref.at[step] for step in range(ref.shape[0])], table[SINGLES, COL_AT], side, flip)
    total[...] = jnp.zeros_like(total)
    backward(ALL, table=table, held=held, tile_ref=tile_ref, total=total)
    emit(total, out_refs, table[SINGLES, ROW_AT], side)


def back_mine_body(n_in, table, *refs):
    pieces, (tile_ref, total, held) = refs[:n_in], refs[n_in:]
    me = table[SINGLES, COL_AT]
    collect_half(held, pieces, me, tile_ref.shape[1], 0)
    total[...] = jnp.zeros_like(total)
    backward(me % 2, table=table, held=held, tile_ref=tile_ref, total=total)


def back_other_body(table, there_ref, begun_ref, tile_ref, *refs):
    out_refs, (held, total) = refs[:-2], refs[-2:]
    side, me = tile_ref.shape[1], table[SINGLES, COL_AT]
    collect_half(held, [there_ref.at[step] for step in range(there_ref.shape[0])], me, side, 1)
    total[...] = begun_ref[...]
    backward(1 - me % 2, table=table, held=held, tile_ref=tile_ref, total=total)
    emit(total, out_refs, table[SINGLES, ROW_AT], side)


def pack_gram(gram, columns):
    per = columns // gram.shape[0]
    rows = gram.shape[0] // per
    return jnp.concatenate([gram[at * rows : (at + 1) * rows] for at in range(per)], axis=1)


def unpack_gram(rows, width):
    return jnp.concatenate([rows[:, at : at + width] for at in range(0, rows.shape[1], width)], axis=0)


def split_panel(pieces, scale_ref, spread, held, me):
    width, side = spread.shape[1:]
    collect(spread, pieces, me, side)
    for tile in range(spread.shape[0]):
        value = spread[tile] * scale_ref[:, tile * side : (tile + 1) * side]
        high = value.astype(jnp.bfloat16)
        held[tile, :width] = high
        held[tile, width:] = (value - high.astype(jnp.float32)).astype(jnp.bfloat16)
    gram = jnp.zeros((width, width), jnp.float32)
    for tile in range(spread.shape[0]):
        gram = gram + lax.dot_general(
            spread[tile], spread[tile], NT, precision=HIGH, preferred_element_type=jnp.float32
        )
    return gram


def emit_rows(total, out_ref, chips, me, side, flip):
    width = total.shape[1]
    for step in range(chips):
        get(total, me ^ (2 * step + flip), out_ref.at[step * width : (step + 1) * width], side)


def next_body(n_in, chips, table, *refs):
    pieces, (scale_ref, tile_ref, mine_ref, other_ref, gram_ref, spread, held, total) = refs[:n_in], refs[n_in:]
    side, me, width = tile_ref.shape[1], table[SINGLES, COL_AT], total.shape[1]
    rows = pack_gram(split_panel(pieces, scale_ref, spread, held, table[SINGLES, ROW_AT]), gram_ref.shape[1])
    gram_ref[...] = rows
    other_ref[chips * width :] = rows
    total[...] = jnp.zeros_like(total)
    forward(ALL, table=table, held=held, tile_ref=tile_ref, total=total)
    emit_rows(total, mine_ref, chips, me, side, 0)
    emit_rows(total, other_ref, chips, me, side, 1)


def next_other_body(n_in, chips, table, *refs):
    pieces, (scale_ref, tile_ref, held, other_ref, gram_ref, spread, total) = refs[:n_in], refs[n_in:]
    side, me, width = tile_ref.shape[1], table[SINGLES, COL_AT], total.shape[1]
    rows = pack_gram(split_panel(pieces, scale_ref, spread, held, table[SINGLES, ROW_AT]), gram_ref.shape[1])
    gram_ref[...] = rows
    other_ref[chips * width :] = rows
    total[...] = jnp.zeros_like(total)
    forward(1 - me % 2, table=table, held=held, tile_ref=tile_ref, total=total)
    emit_rows(total, other_ref, chips, me, side, 1)


def next_mine_body(chips, table, held, tile_ref, mine_ref, total):
    side, me = tile_ref.shape[1], table[SINGLES, COL_AT]
    total[...] = jnp.zeros_like(total)
    forward(me % 2, table=table, held=held, tile_ref=tile_ref, total=total)
    emit_rows(total, mine_ref, chips, me, side, 0)


def next_pair_body(width, mine_ref, got_ref, gram_ref, *outs):
    count = len(outs)
    gram = gram_ref[...] + got_ref[count * width :]
    for at, out_ref in enumerate(outs):
        step = (count - at) % count
        span = slice(step * width, (step + 1) * width)
        out_ref[:width] = mine_ref[span] + got_ref[span]
        out_ref[width:] = gram


def next_query_body(*refs):
    part_refs, scale_ref, out_ref = refs[:-2], refs[-2], refs[-1]
    width = out_ref.shape[0]
    total = add(part_refs)
    inverse = inverse_factor(unpack_gram(total[width:], width))
    current = lax.dot_general(inverse, total[:width], NN, precision=HIGH, preferred_element_type=jnp.float32)
    out_ref[...] = (current * scale_ref[...]).astype(out_ref.dtype)


def add(refs):
    total = refs[0][...].astype(jnp.float32)
    for ref in refs[1:]:
        total = total + ref[...].astype(jnp.float32)
    return total


def start_body(place, panel_ref, degree_ref, out_ref, held, degrees, sems):
    share = panel_ref.shape[1]
    at = pl.multiple_of(place[0] * share, 128)
    loads = [
        pltpu.make_async_copy(degree_ref, degrees, sems.at[0]),
        pltpu.make_async_copy(panel_ref, held, sems.at[1]),
    ]
    for load in loads:
        load.start()
    for load in loads:
        load.wait()
    scale = 1.0 / jnp.sqrt(degrees[:, pl.ds(at, share)].astype(jnp.float32))
    out_ref[...] = (held[...] * scale).astype(out_ref.dtype)


def write_table(table, ids, place, per, query_tiles, product_tiles):
    slots = ids.shape[1]
    for which in range(LISTS):
        table[SINGLES, which] = 0
        for at in range(slots):
            table[which * FIELDS + SLOT, at] = 0
            table[which * FIELDS + QUERY_GIVE, at] = query_tiles
            table[which * FIELDS + PRODUCT_TAKE, at] = 0
            table[which * FIELDS + QUERY_TAKE, at] = 0
            table[which * FIELDS + PRODUCT_GIVE, at] = product_tiles
    table[SINGLES, ROW_AT] = place[0]
    table[SINGLES, COL_AT] = place[1]

    def step(slot, carry):
        query, product = ids[0, slot], ids[1, slot]
        for which in (query // per % 2, ALL):
            at = table[SINGLES, which]
            table[which * FIELDS + SLOT, at] = slot
            table[which * FIELDS + QUERY_GIVE, at] = query
            table[which * FIELDS + PRODUCT_TAKE, at] = product
            table[which * FIELDS + QUERY_TAKE, at] = query
            table[which * FIELDS + PRODUCT_GIVE, at] = product
            table[SINGLES, which] = at + 1
        return carry

    lax.fori_loop(0, jnp.minimum(place[2], slots), step, 0)


def load_body(per, place, after_ref, tile_ref, id_ref, product_ref, query_ref, *refs):
    keep, my_product_ref, product_out, my_query_ref, table, ids, degrees, counts, sems = refs
    loads = [
        pltpu.make_async_copy(id_ref, ids, sems.at[0]),
        pltpu.make_async_copy(product_ref, degrees, sems.at[1]),
        pltpu.make_async_copy(query_ref, counts, sems.at[2]),
    ]
    part = tile_ref.shape[0] // LOADS
    for step in range(LOADS):
        span = pl.ds(step * part, part)
        loads.append(pltpu.make_async_copy(tile_ref.at[span], keep.at[span], sems.at[3 + step]))
    for load in loads:
        load.start()
    loads[0].wait()
    side = tile_ref.shape[1]
    write_table(table, ids, place, per, query_ref.shape[1] // side, product_ref.shape[1] // side)
    loads[1].wait()
    product_out[...] = 1.0 / jnp.sqrt(degrees[...].astype(jnp.float32))
    share = my_product_ref.shape[1]
    at = pl.multiple_of(place[0] * share, 128)
    my_product_ref[...] = product_out[:, pl.ds(at, share)]
    loads[2].wait()
    columns = my_query_ref.shape[1]
    if columns % 128 == 0:
        at = pl.multiple_of(place[1] * columns, 128)
        my_query_ref[...] = 1.0 / jnp.sqrt(counts[:, pl.ds(at, columns)].astype(jnp.float32))
    else:
        for step in range(counts.shape[1] // columns):

            @pl.when(place[1] == step)
            def _():
                degree = counts[:, step * columns : (step + 1) * columns]
                my_query_ref[...] = 1.0 / jnp.sqrt(degree.astype(jnp.float32))
    for load in loads[3:]:
        load.wait()


def pair_body(mine_ref, got_ref, *outs):
    count = len(outs)
    for at, out_ref in enumerate(outs):
        step = (count - at) % count
        out_ref[...] = (mine_ref[step] + got_ref[step]).astype(out_ref.dtype)


def join_body(*refs):
    for step, ref in enumerate(refs[:-1]):
        refs[-1][step] = ref[...]


def query_body(*refs):
    part_refs, scale_ref, out_ref = refs[:-2], refs[-2], refs[-1]
    out_ref[...] = (add(part_refs) * scale_ref[...]).astype(out_ref.dtype)


def lift_only_body(*refs):
    part_refs, scale_ref, lifted_ref = refs[:-2], refs[-2], refs[-1]
    lifted_ref[...] = add(part_refs) * scale_ref[...]


def lift_body(*refs):
    part_refs, scale_ref, lifted_ref, gram_ref = refs[:-3], refs[-3], refs[-2], refs[-1]
    lifted = add(part_refs) * scale_ref[...]
    lifted_ref[...] = lifted
    gram_ref[...] = lax.dot_general(lifted, lifted, NT, precision=HIGH, preferred_element_type=jnp.float32)


def sum_body(*refs):
    refs[-1][...] = add(refs[:-1])


def finish_body(after, *refs):
    grams, lifted_ref, out_ref = refs[:-2], refs[-2], refs[-1]
    out_ref[...] = (
        lax.dot_general(
            inverse_factor(add(grams)), lifted_ref[...], NN, precision=HIGH, preferred_element_type=jnp.float32
        )
        * after
    )


def swap(value, axis, step):
    return lax.ppermute(value, axis, [(i, i ^ step) for i in range(lax.axis_size(axis))])


def spread_to(value, axis, stride=1):
    return [value] + [swap(value, axis, step) for step in range(stride, lax.axis_size(axis), stride)]


def deal(values, axis, stride=1):
    count = len(values)
    return [values[0]] + [swap(value, axis, (count - at) * stride) for at, value in enumerate(values[1:], 1)]


def add_up(*values):
    return call(sum_body, "sum", [WHOLE] * len(values), f32(*values[0].shape))(*values)


def terms_over_col(gram):
    return spread_to(add_up(gram, swap(gram, "col", 1)), "col", 2)


def shards(tiles, tile_ids, tile_count, query_degree, product_degree, panel):
    tile_set = tiles[0, 0]
    ids = tile_ids[0, 0]
    slots, side, _ = tile_set.shape
    width, share = panel.shape
    queries, products = query_degree.shape[0], product_degree.shape[0]
    query_tiles, product_tiles = queries // side, products // side
    n_row, n_col = lax.axis_size("row"), lax.axis_size("col")
    chips = n_col // 2
    row_at, col_at = lax.axis_index("row").astype(jnp.int32), lax.axis_index("col").astype(jnp.int32)
    columns = queries // n_col
    work = dict(flops=2 * slots * width * side * side, moved=2 * slots * side * side)
    scaled = call(
        start_body,
        "start",
        [SCALARS, AWAY, AWAY],
        bf16(width, share),
        [
            pltpu.VMEM((width, share), jnp.float32),
            pltpu.VMEM((1, products), jnp.int32),
            pltpu.SemaphoreType.DMA((2,)),
        ],
    )(row_at[None], in_hbm(panel), in_hbm(product_degree[None, :]))
    pieces = spread_to(scaled, "row")
    split = columns % side == 0
    tile_set, my_pscale, pscale, my_qscale, table = call(
        functools.partial(load_body, max(columns // side, 1)),
        "load",
        [SCALARS, WHOLE] + [AWAY] * 4,
        [
            pltpu.VMEM((slots, side, side), jnp.bfloat16),
            f32(1, share),
            f32(1, products),
            f32(1, columns),
            jax.ShapeDtypeStruct((SINGLES + 1, slots), jnp.int32),
        ],
        [
            pltpu.SMEM(ids.shape, jnp.int32),
            pltpu.VMEM((1, products), jnp.int32),
            pltpu.VMEM((1, queries), jnp.int32),
            pltpu.SemaphoreType.DMA((3 + LOADS,)),
        ],
        moved=4 * slots * side * side,
        out_specs=[WHOLE] * 4 + [SCALARS],
    )(
        jnp.stack([row_at, col_at, tile_count[0, 0]]),
        scaled,
        in_hbm(tile_set),
        in_hbm(ids),
        in_hbm(product_degree[None, :]),
        in_hbm(query_degree[None, :]),
    )
    tile_set = pltpu.with_memory_space_constraint(tile_set, pltpu.VMEM)
    root_count = math.sqrt(products * n_col)
    half = f32(chips, width, columns)
    gram_rows = width * width // columns
    half_work = dict(flops=slots * width * side * side, moved=slots * side * side)
    query_scratch = pltpu.VMEM((query_tiles + 1, width, side), jnp.float32)
    product_scratch = pltpu.VMEM((product_tiles + 1, width, side), jnp.float32)
    query_held = pltpu.VMEM((query_tiles, width, side), jnp.bfloat16)
    for iteration in range(ITERS):
        sets = SETS if iteration < ITERS - 1 else 1
        if iteration > 0:
            pieces = [piece for part in lifted for piece in spread_to(part, "row")]
            arrays = [WHOLE] * (len(pieces) + 2)
            message = f32(chips * width + gram_rows, columns)
            spread = pltpu.VMEM((product_tiles, width, side), jnp.float32)
            if split:
                held, other, gram = call(
                    functools.partial(next_other_body, len(pieces), chips),
                    "forward",
                    [SCALARS] + arrays,
                    [bf16(product_tiles, 2 * width, side), message, f32(gram_rows, columns)],
                    [spread, query_scratch],
                    **half_work,
                )(table, *pieces, pscale, tile_set)
                got = swap(other, "col", 1)
                mine = call(
                    functools.partial(next_mine_body, chips),
                    "forward_rest",
                    [SCALARS] + [WHOLE] * 2,
                    f32(chips * width, columns),
                    [query_scratch],
                    **half_work,
                )(table, held, tile_set)
            else:
                mine, other, gram = call(
                    functools.partial(next_body, len(pieces), chips),
                    "forward",
                    [SCALARS] + arrays,
                    [f32(chips * width, columns), message, f32(gram_rows, columns)],
                    [spread, pltpu.VMEM((product_tiles, 2 * width, side), jnp.bfloat16), query_scratch],
                    **work,
                )(table, *pieces, pscale, tile_set)
                got = swap(other, "col", 1)
            sums = call(
                functools.partial(next_pair_body, width),
                "pair",
                [WHOLE] * 3,
                [f32(width + gram_rows, columns)] * chips,
            )(mine, got, gram)
        elif split:
            held, other = call(
                functools.partial(forward_other_body, n_row),
                "forward",
                [SCALARS] + [WHOLE] * (n_row + 1),
                [bf16(product_tiles, width, side), half],
                [query_scratch],
                **half_work,
            )(table, *pieces, tile_set)
            got = swap(other, "col", 1)
            mine = call(
                forward_mine_body,
                "forward_rest",
                [SCALARS] + [WHOLE] * 2,
                half,
                [query_scratch],
                **half_work,
            )(table, held, tile_set)
        else:
            mine, other = call(
                functools.partial(forward_body, n_row),
                "forward",
                [SCALARS] + [WHOLE] * (n_row + 1),
                [half] * 2,
                [pltpu.VMEM((product_tiles, width, side), jnp.bfloat16), query_scratch],
                **work,
            )(table, *pieces, tile_set)
            got = swap(other, "col", 1)
        if iteration == 0:
            sums = call(
                pair_body, "pair", [WHOLE] * 2, [f32(width, columns)] + [bf16(width, columns)] * (chips - 1)
            )(mine, got)
        parts = deal(sums, "col", 2)
        rounded = call(next_query_body if iteration else query_body, "query", [WHOLE] * (chips + 1), bf16(width, columns))(*parts, my_qscale)
        pieces = spread_to(rounded, "col", 2)
        here = call(join_body, "join", [WHOLE] * chips, bf16(chips, width, columns))(*pieces)
        there = swap(here, "col", 1)
        if split:
            begun = call(
                functools.partial(back_mine_body, chips),
                "backward",
                [SCALARS] + [WHOLE] * (chips + 1),
                f32(product_tiles + 1, width, side),
                [query_held],
                **half_work,
            )(table, *pieces, tile_set)
            sums = call(
                back_other_body,
                "backward_rest",
                [SCALARS] + [WHOLE] * 3,
                [f32(width // sets, share)] * (sets * n_row),
                [query_held, product_scratch],
                **half_work,
            )(table, there, begun, tile_set)
        else:
            sums = call(
                back_body,
                "backward",
                [SCALARS] + [WHOLE] * 3,
                [f32(width // sets, share)] * (sets * n_row),
                [query_held, product_scratch],
                **work,
            )(table, here, there, tile_set)
        parts = [deal(sums[n_row * part : n_row * (part + 1)], "row") for part in range(sets)]
        if iteration < ITERS - 1:
            lifted = [
                call(lift_only_body, "lift", [WHOLE] * (n_row + 1), f32(width // sets, share))(*part, my_pscale)
                for part in parts
            ]
    lifted, gram = call(
        lift_body, "lift", [WHOLE] * (n_row + 1), [f32(width, share), f32(width, width)]
    )(*parts[0], my_pscale)
    return call(
        functools.partial(finish_body, root_count), "finish", [WHOLE] * (chips + 1), f32(width, share)
    )(*terms_over_col(add_up(*spread_to(gram, "row"))), lifted)


def solution(mesh):
    in_specs = (
        P("row", "col", None, None, None),
        P("row", "col", None, None),
        P("row", "col"),
        P("row"),
        P("col"),
        P(None, ("col", "row")),
    )
    out_specs = P(None, ("col", "row"))
    return jax.shard_map(shards, mesh=mesh, in_specs=in_specs, out_specs=out_specs, check_vma=False)
```

```python
import functools
import math

import jax
import jax.numpy as jnp
from jax import lax
from jax.experimental import pallas as pl
from jax.experimental.pallas import tpu as pltpu
from jax.sharding import PartitionSpec as P

ITERS = 2
GROUP = 8
LOADS = 8
SETS = 2
PANEL_STEP = 8
HIGH = lax.Precision.HIGHEST
VMEM_BYTES = 12 * 1024 * 1024
NT = (((1,), (1,)), ((), ()))
NN = (((1,), (0,)), ((), ()))

def inverse_factor(gram):
    width = gram.shape[0]
    rows = lax.broadcasted_iota(jnp.int32, (width, width), 0)
    cols = lax.broadcasted_iota(jnp.int32, (width, width), 1)
    work = jnp.concatenate([gram, (rows == cols).astype(jnp.float32)], axis=1)
    done = []
    for first in range(0, width, PANEL_STEP):
        height = width - first
        columns = [
            jnp.broadcast_to(work[:, first + j : first + j + 1], (height, 2 * width))
            for j in range(PANEL_STEP)
        ]
        for j in range(PANEL_STEP):
            scale = lax.rsqrt(columns[j][j : j + 1, :])
            row = work[j : j + 1, :] * scale
            factor = columns[j] * scale
            done.append(row)
            for later in range(j + 1, PANEL_STEP):
                columns[later] = columns[later] - factor * (columns[later][j : j + 1, :] * scale)
            work = work - factor * row
        work = work[PANEL_STEP:, :]
    return jnp.concatenate(done, axis=0)[:, width:]


SLOT, QUERY_GIVE, PRODUCT_TAKE, QUERY_TAKE, PRODUCT_GIVE = range(5)
FIELDS, LISTS, ALL = 5, 3, 2
SINGLES = FIELDS * LISTS
ROW_AT, COL_AT = 3, 4
WHOLE = pl.BlockSpec(memory_space=pltpu.VMEM)
SCALARS = pl.BlockSpec(memory_space=pltpu.SMEM)
AWAY = pl.BlockSpec(memory_space=pltpu.MemorySpace.HBM)


def call(body, name, in_specs, out_shape, scratch=(), flops=0, moved=0, out_specs=None):
    many = isinstance(out_shape, (tuple, list))
    return pl.pallas_call(
        body,
        out_shape=out_shape,
        in_specs=in_specs,
        out_specs=out_specs or ([WHOLE] * len(out_shape) if many else WHOLE),
        scratch_shapes=scratch,
        compiler_params=pltpu.CompilerParams(vmem_limit_bytes=VMEM_BYTES),
        cost_estimate=pl.CostEstimate(flops=flops, bytes_accessed=moved, transcendentals=0),
        name=name,
    )


def in_hbm(value):
    return pltpu.with_memory_space_constraint(value, pltpu.MemorySpace.HBM)


def f32(*shape):
    return jax.ShapeDtypeStruct(shape, jnp.float32)


def bf16(*shape):
    return jax.ShapeDtypeStruct(shape, jnp.bfloat16)


def put(held, owner, value, side, row=0):
    span, share = slice(row, row + value.shape[0]), value.shape[1]
    if share >= side:
        per = share // side
        for piece in range(per):
            held[owner * per + piece, span] = value[:, piece * side : (piece + 1) * side]
    else:
        per = side // share
        for at in range(per):

            @pl.when(owner % per == at)
            def _():
                held[owner // per, span, at * share : (at + 1) * share] = value


def get(total, owner, out_ref, side, row=0):
    span, share = slice(row, row + out_ref.shape[0]), out_ref.shape[1]
    if share >= side:
        per = share // side
        for piece in range(per):
            out_ref[:, piece * side : (piece + 1) * side] = total[owner * per + piece, span].astype(out_ref.dtype)
    else:
        per = side // share
        for at in range(per):

            @pl.when(owner % per == at)
            def _():
                out_ref[...] = total[owner // per, span, at * share : (at + 1) * share].astype(out_ref.dtype)


def emit(total, out_refs, me, side):
    sets = total.shape[1] // out_refs[0].shape[0]
    count = len(out_refs) // sets
    for at, out_ref in enumerate(out_refs):
        part, at = divmod(at, count)
        get(total, me ^ ((count - at) % count), out_ref, side, part * out_ref.shape[0])


def collect(held, piece_refs, me, side):
    sets = held.shape[1] // piece_refs[0].shape[0]
    count = len(piece_refs) // sets
    for at, piece_ref in enumerate(piece_refs):
        part, step = divmod(at, count)
        put(held, me ^ step, piece_ref[...], side, part * piece_ref.shape[0])


def products(which, take, give, dims, table, held, tile_ref, total):
    width = total.shape[1]
    slots = tile_ref.shape[0]

    def run(first, length):
        for lane in range(length):
            at = first + lane
            term = lax.dot_general(
                held[table[which * FIELDS + take, at]],
                tile_ref[table[which * FIELDS + SLOT, at]],
                dims,
                preferred_element_type=jnp.float32,
            )
            if term.shape[0] > width:
                term = term[:width] + term[width:]
            total[table[which * FIELDS + give, at]] += term

    if isinstance(which, int):
        run(0, slots)
        return

    def step(g, carry):
        run(slots // 2 + g * GROUP, GROUP)
        return carry

    run(0, slots // 2)
    rest = jnp.maximum(table[SINGLES, which] - slots // 2, 0)
    lax.fori_loop(0, jnp.minimum((rest + GROUP - 1) // GROUP, slots // 2 // GROUP), step, 0)


forward = functools.partial(products, take=PRODUCT_TAKE, give=QUERY_GIVE, dims=NT)
backward = functools.partial(products, take=QUERY_TAKE, give=PRODUCT_GIVE, dims=NN)


def emit_half(total, out_ref, me, side, flip):
    for step in range(out_ref.shape[0]):
        get(total, me ^ (2 * step + flip), out_ref.at[step], side)


def collect_half(held, piece_refs, me, side, flip):
    for step, piece_ref in enumerate(piece_refs):
        put(held, me ^ (2 * step + flip), piece_ref[...], side)


def forward_body(n_in, table, *refs):
    pieces, (tile_ref, mine_ref, other_ref, held, total) = refs[:n_in], refs[n_in:]
    side = tile_ref.shape[1]
    collect(held, pieces, table[SINGLES, ROW_AT], side)
    total[...] = jnp.zeros_like(total)
    forward(ALL, table=table, held=held, tile_ref=tile_ref, total=total)
    emit_half(total, mine_ref, table[SINGLES, COL_AT], side, 0)
    emit_half(total, other_ref, table[SINGLES, COL_AT], side, 1)


def forward_other_body(n_in, table, *refs):
    pieces, (tile_ref, held, other_ref, total) = refs[:n_in], refs[n_in:]
    side, me = tile_ref.shape[1], table[SINGLES, COL_AT]
    collect(held, pieces, table[SINGLES, ROW_AT], side)
    total[...] = jnp.zeros_like(total)
    forward(1 - me % 2, table=table, held=held, tile_ref=tile_ref, total=total)
    emit_half(total, other_ref, me, side, 1)


def forward_mine_body(table, held, tile_ref, mine_ref, total):
    side, me = tile_ref.shape[1], table[SINGLES, COL_AT]
    total[...] = jnp.zeros_like(total)
    forward(me % 2, table=table, held=held, tile_ref=tile_ref, total=total)
    emit_half(total, mine_ref, me, side, 0)


def back_body(table, here_ref, there_ref, tile_ref, *refs):
    out_refs, (held, total) = refs[:-2], refs[-2:]
    side = tile_ref.shape[1]
    for flip, ref in enumerate((here_ref, there_ref)):
        collect_half(held, [ref.at[step] for step in range(ref.shape[0])], table[SINGLES, COL_AT], side, flip)
    total[...] = jnp.zeros_like(total)
    backward(ALL, table=table, held=held, tile_ref=tile_ref, total=total)
    emit(total, out_refs, table[SINGLES, ROW_AT], side)


def back_mine_body(n_in, table, *refs):
    pieces, (tile_ref, total, held) = refs[:n_in], refs[n_in:]
    me = table[SINGLES, COL_AT]
    collect_half(held, pieces, me, tile_ref.shape[1], 0)
    total[...] = jnp.zeros_like(total)
    backward(me % 2, table=table, held=held, tile_ref=tile_ref, total=total)


def back_other_body(table, there_ref, begun_ref, tile_ref, *refs):
    out_refs, (held, total) = refs[:-2], refs[-2:]
    side, me = tile_ref.shape[1], table[SINGLES, COL_AT]
    collect_half(held, [there_ref.at[step] for step in range(there_ref.shape[0])], me, side, 1)
    total[...] = begun_ref[...]
    backward(1 - me % 2, table=table, held=held, tile_ref=tile_ref, total=total)
    emit(total, out_refs, table[SINGLES, ROW_AT], side)


def pack_gram(gram, columns):
    per = columns // gram.shape[0]
    rows = gram.shape[0] // per
    return jnp.concatenate([gram[at * rows : (at + 1) * rows] for at in range(per)], axis=1)


def unpack_gram(rows, width):
    return jnp.concatenate([rows[:, at : at + width] for at in range(0, rows.shape[1], width)], axis=0)


def split_panel(pieces, scale_ref, spread, held, me):
    width, side = spread.shape[1:]
    collect(spread, pieces, me, side)
    for tile in range(spread.shape[0]):
        value = spread[tile] * scale_ref[:, tile * side : (tile + 1) * side]
        high = value.astype(jnp.bfloat16)
        held[tile, :width] = high
        held[tile, width:] = (value - high.astype(jnp.float32)).astype(jnp.bfloat16)
    gram = jnp.zeros((width, width), jnp.float32)
    for tile in range(spread.shape[0]):
        gram = gram + lax.dot_general(
            spread[tile], spread[tile], NT, precision=HIGH, preferred_element_type=jnp.float32
        )
    return gram


def emit_rows(total, out_ref, chips, me, side, flip):
    width = total.shape[1]
    for step in range(chips):
        get(total, me ^ (2 * step + flip), out_ref.at[step * width : (step + 1) * width], side)


def next_body(n_in, chips, table, *refs):
    pieces, (scale_ref, tile_ref, mine_ref, other_ref, gram_ref, spread, held, total) = refs[:n_in], refs[n_in:]
    side, me, width = tile_ref.shape[1], table[SINGLES, COL_AT], total.shape[1]
    rows = pack_gram(split_panel(pieces, scale_ref, spread, held, table[SINGLES, ROW_AT]), gram_ref.shape[1])
    gram_ref[...] = rows
    other_ref[chips * width :] = rows
    total[...] = jnp.zeros_like(total)
    forward(ALL, table=table, held=held, tile_ref=tile_ref, total=total)
    emit_rows(total, mine_ref, chips, me, side, 0)
    emit_rows(total, other_ref, chips, me, side, 1)


def next_other_body(n_in, chips, table, *refs):
    pieces, (scale_ref, tile_ref, held, other_ref, gram_ref, spread, total) = refs[:n_in], refs[n_in:]
    side, me, width = tile_ref.shape[1], table[SINGLES, COL_AT], total.shape[1]
    rows = pack_gram(split_panel(pieces, scale_ref, spread, held, table[SINGLES, ROW_AT]), gram_ref.shape[1])
    gram_ref[...] = rows
    other_ref[chips * width :] = rows
    total[...] = jnp.zeros_like(total)
    forward(1 - me % 2, table=table, held=held, tile_ref=tile_ref, total=total)
    emit_rows(total, other_ref, chips, me, side, 1)


def next_mine_body(chips, table, held, tile_ref, mine_ref, total):
    side, me = tile_ref.shape[1], table[SINGLES, COL_AT]
    total[...] = jnp.zeros_like(total)
    forward(me % 2, table=table, held=held, tile_ref=tile_ref, total=total)
    emit_rows(total, mine_ref, chips, me, side, 0)


def next_pair_body(width, chips, mine_ref, got_ref, gram_ref, *outs):
    columns = outs[0].shape[1]
    gram = pack_gram(unpack_gram(gram_ref[...] + got_ref[chips * width :], width), columns)
    for at, out_ref in enumerate(outs):
        part, at = divmod(at, chips)
        step = (chips - at) % chips
        block = slice(step * width, (step + 1) * width), slice(part * columns, (part + 1) * columns)
        out_ref[:width] = mine_ref[block] + got_ref[block]
        if part == 0:
            out_ref[width:] = gram


def factor_query_body(*refs):
    part_refs, scale_ref, inverse_ref, out_ref = refs[:-3], refs[-3], refs[-2], refs[-1]
    width, columns = out_ref.shape
    total = add(part_refs)
    inverse = inverse_factor(unpack_gram(total[width:], width))
    inverse_ref[...] = inverse
    current = lax.dot_general(inverse, total[:width], NN, precision=HIGH, preferred_element_type=jnp.float32)
    out_ref[...] = (current * scale_ref[:, :columns]).astype(out_ref.dtype)


def rest_query_body(*refs):
    part_refs, inverse_ref, begun_ref, scale_ref, out_ref = refs[:-4], *refs[-4:]
    columns = begun_ref.shape[1]
    current = lax.dot_general(
        inverse_ref[...], add(part_refs), NN, precision=HIGH, preferred_element_type=jnp.float32
    )
    out_ref[:, :columns] = begun_ref[...]
    out_ref[:, columns:] = (current * scale_ref[:, columns:]).astype(out_ref.dtype)


def next_query_body(*refs):
    part_refs, scale_ref, out_ref = refs[:-2], refs[-2], refs[-1]
    width = out_ref.shape[0]
    total = add(part_refs)
    inverse = inverse_factor(unpack_gram(total[width:], width))
    current = lax.dot_general(inverse, total[:width], NN, precision=HIGH, preferred_element_type=jnp.float32)
    out_ref[...] = (current * scale_ref[...]).astype(out_ref.dtype)


def add(refs):
    total = refs[0][...].astype(jnp.float32)
    for ref in refs[1:]:
        total = total + ref[...].astype(jnp.float32)
    return total


def start_body(place, panel_ref, degree_ref, out_ref, held, degrees, sems):
    share = panel_ref.shape[1]
    at = pl.multiple_of(place[0] * share, 128)
    loads = [
        pltpu.make_async_copy(degree_ref, degrees, sems.at[0]),
        pltpu.make_async_copy(panel_ref, held, sems.at[1]),
    ]
    for load in loads:
        load.start()
    for load in loads:
        load.wait()
    scale = 1.0 / jnp.sqrt(degrees[:, pl.ds(at, share)].astype(jnp.float32))
    out_ref[...] = (held[...] * scale).astype(out_ref.dtype)


def write_table(table, ids, place, per, query_tiles, product_tiles):
    slots = ids.shape[1]
    for which in range(LISTS):
        table[SINGLES, which] = 0
        for at in range(slots):
            table[which * FIELDS + SLOT, at] = 0
            table[which * FIELDS + QUERY_GIVE, at] = query_tiles
            table[which * FIELDS + PRODUCT_TAKE, at] = 0
            table[which * FIELDS + QUERY_TAKE, at] = 0
            table[which * FIELDS + PRODUCT_GIVE, at] = product_tiles
    table[SINGLES, ROW_AT] = place[0]
    table[SINGLES, COL_AT] = place[1]

    def step(slot, carry):
        query, product = ids[0, slot], ids[1, slot]
        for which in (query // per % 2, ALL):
            at = table[SINGLES, which]
            table[which * FIELDS + SLOT, at] = slot
            table[which * FIELDS + QUERY_GIVE, at] = query
            table[which * FIELDS + PRODUCT_TAKE, at] = product
            table[which * FIELDS + QUERY_TAKE, at] = query
            table[which * FIELDS + PRODUCT_GIVE, at] = product
            table[SINGLES, which] = at + 1
        return carry

    lax.fori_loop(0, jnp.minimum(place[2], slots), step, 0)


def load_body(per, place, after_ref, tile_ref, id_ref, product_ref, query_ref, *refs):
    keep, my_product_ref, product_out, my_query_ref, table, ids, degrees, counts, sems = refs
    loads = [
        pltpu.make_async_copy(id_ref, ids, sems.at[0]),
        pltpu.make_async_copy(product_ref, degrees, sems.at[1]),
        pltpu.make_async_copy(query_ref, counts, sems.at[2]),
    ]
    part = tile_ref.shape[0] // LOADS
    for step in range(LOADS):
        span = pl.ds(step * part, part)
        loads.append(pltpu.make_async_copy(tile_ref.at[span], keep.at[span], sems.at[3 + step]))
    for load in loads:
        load.start()
    loads[0].wait()
    side = tile_ref.shape[1]
    write_table(table, ids, place, per, query_ref.shape[1] // side, product_ref.shape[1] // side)
    loads[1].wait()
    product_out[...] = 1.0 / jnp.sqrt(degrees[...].astype(jnp.float32))
    share = my_product_ref.shape[1]
    at = pl.multiple_of(place[0] * share, 128)
    my_product_ref[...] = product_out[:, pl.ds(at, share)]
    loads[2].wait()
    columns = my_query_ref.shape[1]
    if columns % 128 == 0:
        at = pl.multiple_of(place[1] * columns, 128)
        my_query_ref[...] = 1.0 / jnp.sqrt(counts[:, pl.ds(at, columns)].astype(jnp.float32))
    else:
        for step in range(counts.shape[1] // columns):

            @pl.when(place[1] == step)
            def _():
                degree = counts[:, step * columns : (step + 1) * columns]
                my_query_ref[...] = 1.0 / jnp.sqrt(degree.astype(jnp.float32))
    for load in loads[3:]:
        load.wait()


def pair_body(mine_ref, got_ref, *outs):
    count = len(outs)
    for at, out_ref in enumerate(outs):
        step = (count - at) % count
        out_ref[...] = (mine_ref[step] + got_ref[step]).astype(out_ref.dtype)


def join_body(*refs):
    for step, ref in enumerate(refs[:-1]):
        refs[-1][step] = ref[...]


def query_body(*refs):
    part_refs, scale_ref, out_ref = refs[:-2], refs[-2], refs[-1]
    out_ref[...] = (add(part_refs) * scale_ref[...]).astype(out_ref.dtype)


def lift_only_body(*refs):
    part_refs, scale_ref, lifted_ref = refs[:-2], refs[-2], refs[-1]
    lifted_ref[...] = add(part_refs) * scale_ref[...]


def lift_body(*refs):
    part_refs, scale_ref, lifted_ref, gram_ref = refs[:-3], refs[-3], refs[-2], refs[-1]
    lifted = add(part_refs) * scale_ref[...]
    lifted_ref[...] = lifted
    gram_ref[...] = lax.dot_general(lifted, lifted, NT, precision=HIGH, preferred_element_type=jnp.float32)


def sum_body(*refs):
    refs[-1][...] = add(refs[:-1])


def finish_body(after, *refs):
    grams, lifted_ref, out_ref = refs[:-2], refs[-2], refs[-1]
    out_ref[...] = (
        lax.dot_general(
            inverse_factor(add(grams)), lifted_ref[...], NN, precision=HIGH, preferred_element_type=jnp.float32
        )
        * after
    )


def swap(value, axis, step):
    return lax.ppermute(value, axis, [(i, i ^ step) for i in range(lax.axis_size(axis))])


def spread_to(value, axis, stride=1):
    return [value] + [swap(value, axis, step) for step in range(stride, lax.axis_size(axis), stride)]


def deal(values, axis, stride=1):
    count = len(values)
    return [values[0]] + [swap(value, axis, (count - at) * stride) for at, value in enumerate(values[1:], 1)]


def add_up(*values):
    return call(sum_body, "sum", [WHOLE] * len(values), f32(*values[0].shape))(*values)


def terms_over_col(gram):
    return spread_to(add_up(gram, swap(gram, "col", 1)), "col", 2)


def shards(tiles, tile_ids, tile_count, query_degree, product_degree, panel):
    tile_set = tiles[0, 0]
    ids = tile_ids[0, 0]
    slots, side, _ = tile_set.shape
    width, share = panel.shape
    queries, products = query_degree.shape[0], product_degree.shape[0]
    query_tiles, product_tiles = queries // side, products // side
    n_row, n_col = lax.axis_size("row"), lax.axis_size("col")
    chips = n_col // 2
    row_at, col_at = lax.axis_index("row").astype(jnp.int32), lax.axis_index("col").astype(jnp.int32)
    columns = queries // n_col
    work = dict(flops=2 * slots * width * side * side, moved=2 * slots * side * side)
    scaled = call(
        start_body,
        "start",
        [SCALARS, AWAY, AWAY],
        bf16(width, share),
        [
            pltpu.VMEM((width, share), jnp.float32),
            pltpu.VMEM((1, products), jnp.int32),
            pltpu.SemaphoreType.DMA((2,)),
        ],
    )(row_at[None], in_hbm(panel), in_hbm(product_degree[None, :]))
    pieces = spread_to(scaled, "row")
    split = columns % side == 0
    tile_set, my_pscale, pscale, my_qscale, table = call(
        functools.partial(load_body, max(columns // side, 1)),
        "load",
        [SCALARS, WHOLE] + [AWAY] * 4,
        [
            pltpu.VMEM((slots, side, side), jnp.bfloat16),
            f32(1, share),
            f32(1, products),
            f32(1, columns),
            jax.ShapeDtypeStruct((SINGLES + 1, slots), jnp.int32),
        ],
        [
            pltpu.SMEM(ids.shape, jnp.int32),
            pltpu.VMEM((1, products), jnp.int32),
            pltpu.VMEM((1, queries), jnp.int32),
            pltpu.SemaphoreType.DMA((3 + LOADS,)),
        ],
        moved=4 * slots * side * side,
        out_specs=[WHOLE] * 4 + [SCALARS],
    )(
        jnp.stack([row_at, col_at, tile_count[0, 0]]),
        scaled,
        in_hbm(tile_set),
        in_hbm(ids),
        in_hbm(product_degree[None, :]),
        in_hbm(query_degree[None, :]),
    )
    tile_set = pltpu.with_memory_space_constraint(tile_set, pltpu.VMEM)
    root_count = math.sqrt(products * n_col)
    half = f32(chips, width, columns)
    gram_rows = width * width // columns
    half_work = dict(flops=slots * width * side * side, moved=slots * side * side)
    query_scratch = pltpu.VMEM((query_tiles + 1, width, side), jnp.float32)
    product_scratch = pltpu.VMEM((product_tiles + 1, width, side), jnp.float32)
    query_held = pltpu.VMEM((query_tiles, width, side), jnp.bfloat16)
    for iteration in range(ITERS):
        sets = SETS if iteration < ITERS - 1 else 1
        if iteration > 0:
            pieces = [piece for part in lifted for piece in spread_to(part, "row")]
            arrays = [WHOLE] * (len(pieces) + 2)
            message = f32(chips * width + gram_rows, columns)
            spread = pltpu.VMEM((product_tiles, width, side), jnp.float32)
            if split:
                held, other, gram = call(
                    functools.partial(next_other_body, len(pieces), chips),
                    "forward",
                    [SCALARS] + arrays,
                    [bf16(product_tiles, 2 * width, side), message, f32(gram_rows, columns)],
                    [spread, query_scratch],
                    **half_work,
                )(table, *pieces, pscale, tile_set)
                got = swap(other, "col", 1)
                mine = call(
                    functools.partial(next_mine_body, chips),
                    "forward_rest",
                    [SCALARS] + [WHOLE] * 2,
                    f32(chips * width, columns),
                    [query_scratch],
                    **half_work,
                )(table, held, tile_set)
            else:
                mine, other, gram = call(
                    functools.partial(next_body, len(pieces), chips),
                    "forward",
                    [SCALARS] + arrays,
                    [f32(chips * width, columns), message, f32(gram_rows, columns)],
                    [spread, pltpu.VMEM((product_tiles, 2 * width, side), jnp.bfloat16), query_scratch],
                    **work,
                )(table, *pieces, pscale, tile_set)
                got = swap(other, "col", 1)
            halves = 2 if columns % 256 == 0 else 1
            span = columns // halves
            shapes = [f32(width + width * width // span, span)] * chips + [f32(width, span)] * chips
            sums = call(
                functools.partial(next_pair_body, width, chips), "pair", [WHOLE] * 3, shapes[: halves * chips]
            )(mine, got, gram)
            parts = deal(sums[:chips], "col", 2)
            if halves == 1:
                rounded = call(next_query_body, "query", [WHOLE] * (chips + 1), bf16(width, columns))(
                    *parts, my_qscale
                )
            else:
                more = deal(sums[chips:], "col", 2)
                inverse, begun = call(
                    factor_query_body,
                    "query",
                    [WHOLE] * (chips + 1),
                    [f32(width, width), bf16(width, span)],
                    flops=2 * slots * width * side * side,
                )(*parts, my_qscale)
                rounded = call(rest_query_body, "query_rest", [WHOLE] * (chips + 3), bf16(width, columns))(
                    *more, inverse, begun, my_qscale
                )
        elif split:
            held, other = call(
                functools.partial(forward_other_body, n_row),
                "forward",
                [SCALARS] + [WHOLE] * (n_row + 1),
                [bf16(product_tiles, width, side), half],
                [query_scratch],
                **half_work,
            )(table, *pieces, tile_set)
            got = swap(other, "col", 1)
            mine = call(
                forward_mine_body,
                "forward_rest",
                [SCALARS] + [WHOLE] * 2,
                half,
                [query_scratch],
                **half_work,
            )(table, held, tile_set)
        else:
            mine, other = call(
                functools.partial(forward_body, n_row),
                "forward",
                [SCALARS] + [WHOLE] * (n_row + 1),
                [half] * 2,
                [pltpu.VMEM((product_tiles, width, side), jnp.bfloat16), query_scratch],
                **work,
            )(table, *pieces, tile_set)
            got = swap(other, "col", 1)
        if iteration == 0:
            sums = call(
                pair_body, "pair", [WHOLE] * 2, [f32(width, columns)] + [bf16(width, columns)] * (chips - 1)
            )(mine, got)
            parts = deal(sums, "col", 2)
            rounded = call(query_body, "query", [WHOLE] * (chips + 1), bf16(width, columns))(*parts, my_qscale)
        pieces = spread_to(rounded, "col", 2)
        here = call(join_body, "join", [WHOLE] * chips, bf16(chips, width, columns))(*pieces)
        there = swap(here, "col", 1)
        if split:
            begun = call(
                functools.partial(back_mine_body, chips),
                "backward",
                [SCALARS] + [WHOLE] * (chips + 1),
                f32(product_tiles + 1, width, side),
                [query_held],
                **half_work,
            )(table, *pieces, tile_set)
            sums = call(
                back_other_body,
                "backward_rest",
                [SCALARS] + [WHOLE] * 3,
                [f32(width // sets, share)] * (sets * n_row),
                [query_held, product_scratch],
                **half_work,
            )(table, there, begun, tile_set)
        else:
            sums = call(
                back_body,
                "backward",
                [SCALARS] + [WHOLE] * 3,
                [f32(width // sets, share)] * (sets * n_row),
                [query_held, product_scratch],
                **work,
            )(table, here, there, tile_set)
        parts = [deal(sums[n_row * part : n_row * (part + 1)], "row") for part in range(sets)]
        if iteration < ITERS - 1:
            lifted = [
                call(lift_only_body, "lift", [WHOLE] * (n_row + 1), f32(width // sets, share))(*part, my_pscale)
                for part in parts
            ]
    lifted, gram = call(
        lift_body, "lift", [WHOLE] * (n_row + 1), [f32(width, share), f32(width, width)]
    )(*parts[0], my_pscale)
    return call(
        functools.partial(finish_body, root_count), "finish", [WHOLE] * (chips + 1), f32(width, share)
    )(*terms_over_col(add_up(*spread_to(gram, "row"))), lifted)


def solution(mesh):
    in_specs = (
        P("row", "col", None, None, None),
        P("row", "col", None, None),
        P("row", "col"),
        P("row"),
        P("col"),
        P(None, ("col", "row")),
    )
    out_specs = P(None, ("col", "row"))
    return jax.shard_map(shards, mesh=mesh, in_specs=in_specs, out_specs=out_specs, check_vma=False)
```

```python
import functools
import math

import jax
import jax.numpy as jnp
from jax import lax
from jax.experimental import pallas as pl
from jax.experimental.pallas import tpu as pltpu
from jax.sharding import PartitionSpec as P

ITERS = 2
GROUP = 8
LOADS = 8
SETS = 2
PANEL_STEP = 8
HIGH = lax.Precision.HIGHEST
VMEM_BYTES = 12 * 1024 * 1024
NT = (((1,), (1,)), ((), ()))
NN = (((1,), (0,)), ((), ()))

def inverse_factor(gram):
    width = gram.shape[0]
    rows = lax.broadcasted_iota(jnp.int32, (width, width), 0)
    cols = lax.broadcasted_iota(jnp.int32, (width, width), 1)
    work = jnp.concatenate([gram, (rows == cols).astype(jnp.float32)], axis=1)
    done = []
    for first in range(0, width, PANEL_STEP):
        height = width - first
        columns = [
            jnp.broadcast_to(work[:, first + j : first + j + 1], (height, 2 * width))
            for j in range(PANEL_STEP)
        ]
        for j in range(PANEL_STEP):
            scale = lax.rsqrt(columns[j][j : j + 1, :])
            row = work[j : j + 1, :] * scale
            factor = columns[j] * scale
            done.append(row)
            for later in range(j + 1, PANEL_STEP):
                columns[later] = columns[later] - factor * (columns[later][j : j + 1, :] * scale)
            work = work - factor * row
        work = work[PANEL_STEP:, :]
    return jnp.concatenate(done, axis=0)[:, width:]


SLOT, QUERY, PRODUCT = range(3)
FIELDS, LISTS, ALL = 3, 3, 2
SINGLES = FIELDS * LISTS
ROW_AT, COL_AT = 3, 4
WHOLE = pl.BlockSpec(memory_space=pltpu.VMEM)
SCALARS = pl.BlockSpec(memory_space=pltpu.SMEM)
AWAY = pl.BlockSpec(memory_space=pltpu.MemorySpace.HBM)


def call(body, name, in_specs, out_shape, scratch=(), flops=0, moved=0, out_specs=None):
    many = isinstance(out_shape, (tuple, list))
    return pl.pallas_call(
        body,
        out_shape=out_shape,
        in_specs=in_specs,
        out_specs=out_specs or ([WHOLE] * len(out_shape) if many else WHOLE),
        scratch_shapes=scratch,
        compiler_params=pltpu.CompilerParams(vmem_limit_bytes=VMEM_BYTES),
        cost_estimate=pl.CostEstimate(flops=flops, bytes_accessed=moved, transcendentals=0),
        name=name,
    )


def in_hbm(value):
    return pltpu.with_memory_space_constraint(value, pltpu.MemorySpace.HBM)


def f32(*shape):
    return jax.ShapeDtypeStruct(shape, jnp.float32)


def bf16(*shape):
    return jax.ShapeDtypeStruct(shape, jnp.bfloat16)


def put(held, owner, value, side, row=0):
    span, share = slice(row, row + value.shape[0]), value.shape[1]
    if share >= side:
        per = share // side
        for piece in range(per):
            held[owner * per + piece, span] = value[:, piece * side : (piece + 1) * side]
    else:
        per = side // share
        for at in range(per):

            @pl.when(owner % per == at)
            def _():
                held[owner // per, span, at * share : (at + 1) * share] = value


def get(total, owner, out_ref, side, row=0):
    span, share = slice(row, row + out_ref.shape[0]), out_ref.shape[1]
    if share >= side:
        per = share // side
        for piece in range(per):
            out_ref[:, piece * side : (piece + 1) * side] = total[owner * per + piece, span].astype(out_ref.dtype)
    else:
        per = side // share
        for at in range(per):

            @pl.when(owner % per == at)
            def _():
                out_ref[...] = total[owner // per, span, at * share : (at + 1) * share].astype(out_ref.dtype)


def emit(total, out_refs, me, side):
    sets = total.shape[1] // out_refs[0].shape[0]
    count = len(out_refs) // sets
    for at, out_ref in enumerate(out_refs):
        part, at = divmod(at, count)
        get(total, me ^ ((count - at) % count), out_ref, side, part * out_ref.shape[0])


def spare(held):
    held[held.shape[0] - 1] = jnp.zeros(held.shape[1:], held.dtype)


def collect(held, piece_refs, me, side):
    sets = held.shape[1] // piece_refs[0].shape[0]
    count = len(piece_refs) // sets
    for at, piece_ref in enumerate(piece_refs):
        part, step = divmod(at, count)
        put(held, me ^ step, piece_ref[...], side, part * piece_ref.shape[0])


def products(which, take, give, dims, table, held, tile_ref, total):
    width = total.shape[1]
    slots = tile_ref.shape[0]

    def run(first, length):
        for lane in range(length):
            at = first + lane
            term = lax.dot_general(
                held[table[which * FIELDS + take, at]],
                tile_ref[table[which * FIELDS + SLOT, at]],
                dims,
                preferred_element_type=jnp.float32,
            )
            if term.shape[0] > width:
                term = term[:width] + term[width:]
            total[table[which * FIELDS + give, at]] += term

    if isinstance(which, int):
        run(0, slots)
        return

    def step(g, carry):
        run(slots // 2 + g * GROUP, GROUP)
        return carry

    run(0, slots // 2)
    rest = jnp.maximum(table[SINGLES, which] - slots // 2, 0)
    lax.fori_loop(0, jnp.minimum((rest + GROUP - 1) // GROUP, slots // 2 // GROUP), step, 0)


forward = functools.partial(products, take=PRODUCT, give=QUERY, dims=NT)
backward = functools.partial(products, take=QUERY, give=PRODUCT, dims=NN)


def emit_half(total, out_ref, me, side, flip):
    for step in range(out_ref.shape[0]):
        get(total, me ^ (2 * step + flip), out_ref.at[step], side)


def collect_half(held, piece_refs, me, side, flip):
    for step, piece_ref in enumerate(piece_refs):
        put(held, me ^ (2 * step + flip), piece_ref[...], side)


def forward_body(n_in, table, *refs):
    pieces, (tile_ref, mine_ref, other_ref, held, total) = refs[:n_in], refs[n_in:]
    side = tile_ref.shape[1]
    collect(held, pieces, table[SINGLES, ROW_AT], side)
    spare(held)
    total[...] = jnp.zeros_like(total)
    forward(ALL, table=table, held=held, tile_ref=tile_ref, total=total)
    emit_half(total, mine_ref, table[SINGLES, COL_AT], side, 0)
    emit_half(total, other_ref, table[SINGLES, COL_AT], side, 1)


def forward_other_body(n_in, table, *refs):
    pieces, (tile_ref, held, other_ref, total) = refs[:n_in], refs[n_in:]
    side, me = tile_ref.shape[1], table[SINGLES, COL_AT]
    collect(held, pieces, table[SINGLES, ROW_AT], side)
    spare(held)
    total[...] = jnp.zeros_like(total)
    forward(1 - me % 2, table=table, held=held, tile_ref=tile_ref, total=total)
    emit_half(total, other_ref, me, side, 1)


def forward_mine_body(table, held, tile_ref, mine_ref, total):
    side, me = tile_ref.shape[1], table[SINGLES, COL_AT]
    total[...] = jnp.zeros_like(total)
    forward(me % 2, table=table, held=held, tile_ref=tile_ref, total=total)
    emit_half(total, mine_ref, me, side, 0)


def back_body(table, here_ref, there_ref, tile_ref, *refs):
    out_refs, (held, total) = refs[:-2], refs[-2:]
    side = tile_ref.shape[1]
    for flip, ref in enumerate((here_ref, there_ref)):
        collect_half(held, [ref.at[step] for step in range(ref.shape[0])], table[SINGLES, COL_AT], side, flip)
    spare(held)
    total[...] = jnp.zeros_like(total)
    backward(ALL, table=table, held=held, tile_ref=tile_ref, total=total)
    emit(total, out_refs, table[SINGLES, ROW_AT], side)


def back_mine_body(n_in, table, *refs):
    pieces, (tile_ref, total, held) = refs[:n_in], refs[n_in:]
    me = table[SINGLES, COL_AT]
    collect_half(held, pieces, me, tile_ref.shape[1], 0)
    spare(held)
    total[...] = jnp.zeros_like(total)
    backward(me % 2, table=table, held=held, tile_ref=tile_ref, total=total)


def back_other_body(table, there_ref, begun_ref, tile_ref, *refs):
    out_refs, (held, total) = refs[:-2], refs[-2:]
    side, me = tile_ref.shape[1], table[SINGLES, COL_AT]
    collect_half(held, [there_ref.at[step] for step in range(there_ref.shape[0])], me, side, 1)
    spare(held)
    total[...] = begun_ref[...]
    backward(1 - me % 2, table=table, held=held, tile_ref=tile_ref, total=total)
    emit(total, out_refs, table[SINGLES, ROW_AT], side)


def pack_gram(gram, columns):
    per = columns // gram.shape[0]
    rows = gram.shape[0] // per
    return jnp.concatenate([gram[at * rows : (at + 1) * rows] for at in range(per)], axis=1)


def unpack_gram(rows, width):
    return jnp.concatenate([rows[:, at : at + width] for at in range(0, rows.shape[1], width)], axis=0)


def split_panel(pieces, scale_ref, spread, held, me):
    width, side = spread.shape[1:]
    collect(spread, pieces, me, side)
    spare(held)
    for tile in range(spread.shape[0]):
        value = spread[tile] * scale_ref[:, tile * side : (tile + 1) * side]
        high = value.astype(jnp.bfloat16)
        held[tile, :width] = high
        held[tile, width:] = (value - high.astype(jnp.float32)).astype(jnp.bfloat16)
    gram = jnp.zeros((width, width), jnp.float32)
    for tile in range(spread.shape[0]):
        gram = gram + lax.dot_general(
            spread[tile], spread[tile], NT, precision=HIGH, preferred_element_type=jnp.float32
        )
    return gram


def emit_rows(total, out_ref, chips, me, side, flip):
    width = total.shape[1]
    for step in range(chips):
        get(total, me ^ (2 * step + flip), out_ref.at[step * width : (step + 1) * width], side)


def next_body(n_in, chips, table, *refs):
    pieces, (scale_ref, tile_ref, mine_ref, other_ref, gram_ref, spread, held, total) = refs[:n_in], refs[n_in:]
    side, me, width = tile_ref.shape[1], table[SINGLES, COL_AT], total.shape[1]
    rows = pack_gram(split_panel(pieces, scale_ref, spread, held, table[SINGLES, ROW_AT]), gram_ref.shape[1])
    gram_ref[...] = rows
    other_ref[chips * width :] = rows
    total[...] = jnp.zeros_like(total)
    forward(ALL, table=table, held=held, tile_ref=tile_ref, total=total)
    emit_rows(total, mine_ref, chips, me, side, 0)
    emit_rows(total, other_ref, chips, me, side, 1)


def next_other_body(n_in, chips, table, *refs):
    pieces, (scale_ref, tile_ref, held, other_ref, gram_ref, spread, total) = refs[:n_in], refs[n_in:]
    side, me, width = tile_ref.shape[1], table[SINGLES, COL_AT], total.shape[1]
    rows = pack_gram(split_panel(pieces, scale_ref, spread, held, table[SINGLES, ROW_AT]), gram_ref.shape[1])
    gram_ref[...] = rows
    other_ref[chips * width :] = rows
    total[...] = jnp.zeros_like(total)
    forward(1 - me % 2, table=table, held=held, tile_ref=tile_ref, total=total)
    emit_rows(total, other_ref, chips, me, side, 1)


def next_mine_body(chips, table, held, tile_ref, mine_ref, total):
    side, me = tile_ref.shape[1], table[SINGLES, COL_AT]
    total[...] = jnp.zeros_like(total)
    forward(me % 2, table=table, held=held, tile_ref=tile_ref, total=total)
    emit_rows(total, mine_ref, chips, me, side, 0)


def next_pair_body(width, chips, mine_ref, got_ref, gram_ref, *outs):
    columns = outs[0].shape[1]
    gram = pack_gram(unpack_gram(gram_ref[...] + got_ref[chips * width :], width), columns)
    for at, out_ref in enumerate(outs):
        part, at = divmod(at, chips)
        step = (chips - at) % chips
        block = slice(step * width, (step + 1) * width), slice(part * columns, (part + 1) * columns)
        out_ref[:width] = mine_ref[block] + got_ref[block]
        if part == 0:
            out_ref[width:] = gram


def factor_query_body(*refs):
    part_refs, scale_ref, inverse_ref, out_ref = refs[:-3], refs[-3], refs[-2], refs[-1]
    width, columns = out_ref.shape
    total = add(part_refs)
    inverse = inverse_factor(unpack_gram(total[width:], width))
    inverse_ref[...] = inverse
    current = lax.dot_general(inverse, total[:width], NN, precision=HIGH, preferred_element_type=jnp.float32)
    out_ref[...] = (current * scale_ref[:, :columns]).astype(out_ref.dtype)


def rest_query_body(*refs):
    part_refs, inverse_ref, begun_ref, scale_ref, out_ref = refs[:-4], *refs[-4:]
    columns = begun_ref.shape[1]
    current = lax.dot_general(
        inverse_ref[...], add(part_refs), NN, precision=HIGH, preferred_element_type=jnp.float32
    )
    out_ref[:, :columns] = begun_ref[...]
    out_ref[:, columns:] = (current * scale_ref[:, columns:]).astype(out_ref.dtype)


def next_query_body(*refs):
    part_refs, scale_ref, out_ref = refs[:-2], refs[-2], refs[-1]
    width = out_ref.shape[0]
    total = add(part_refs)
    inverse = inverse_factor(unpack_gram(total[width:], width))
    current = lax.dot_general(inverse, total[:width], NN, precision=HIGH, preferred_element_type=jnp.float32)
    out_ref[...] = (current * scale_ref[...]).astype(out_ref.dtype)


def add(refs):
    total = refs[0][...].astype(jnp.float32)
    for ref in refs[1:]:
        total = total + ref[...].astype(jnp.float32)
    return total


def start_body(place, panel_ref, degree_ref, out_ref, held, degrees, sems):
    share = panel_ref.shape[1]
    at = pl.multiple_of(place[0] * share, 128)
    loads = [
        pltpu.make_async_copy(degree_ref, degrees, sems.at[0]),
        pltpu.make_async_copy(panel_ref, held, sems.at[1]),
    ]
    for load in loads:
        load.start()
    for load in loads:
        load.wait()
    scale = 1.0 / jnp.sqrt(degrees[:, pl.ds(at, share)].astype(jnp.float32))
    out_ref[...] = (held[...] * scale).astype(out_ref.dtype)


def clear_table(table, lists, query_tiles, product_tiles):
    for which in lists:
        table[SINGLES, which] = 0
        for at in range(table.shape[1]):
            table[which * FIELDS + SLOT, at] = 0
            table[which * FIELDS + QUERY, at] = query_tiles
            table[which * FIELDS + PRODUCT, at] = product_tiles


def fill_table(table, ids, place, per):
    table[SINGLES, ROW_AT] = place[0]
    table[SINGLES, COL_AT] = place[1]

    def step(slot, carry):
        query, product = ids[0, slot], ids[1, slot]
        which = query // per % 2 if per else ALL
        at = table[SINGLES, which]
        table[which * FIELDS + SLOT, at] = slot
        table[which * FIELDS + QUERY, at] = query
        table[which * FIELDS + PRODUCT, at] = product
        table[SINGLES, which] = at + 1
        return carry

    lax.fori_loop(0, jnp.minimum(place[2], ids.shape[1]), step, 0)


def load_body(per, place, after_ref, tile_ref, id_ref, product_ref, query_ref, *refs):
    keep, my_product_ref, product_out, my_query_ref, table, ids, degrees, counts, sems = refs
    loads = [
        pltpu.make_async_copy(id_ref, ids, sems.at[0]),
        pltpu.make_async_copy(product_ref, degrees, sems.at[1]),
        pltpu.make_async_copy(query_ref, counts, sems.at[2]),
    ]
    part = tile_ref.shape[0] // LOADS
    for step in range(LOADS):
        span = pl.ds(step * part, part)
        loads.append(pltpu.make_async_copy(tile_ref.at[span], keep.at[span], sems.at[3 + step]))
    for load in loads:
        load.start()
    side = tile_ref.shape[1]
    lists = (0, 1) if per else (ALL,)
    clear_table(table, lists, query_ref.shape[1] // side, product_ref.shape[1] // side)
    loads[0].wait()
    fill_table(table, ids, place, per)
    loads[1].wait()
    product_out[...] = 1.0 / jnp.sqrt(degrees[...].astype(jnp.float32))
    share = my_product_ref.shape[1]
    at = pl.multiple_of(place[0] * share, 128)
    my_product_ref[...] = product_out[:, pl.ds(at, share)]
    loads[2].wait()
    columns = my_query_ref.shape[1]
    if columns % 128 == 0:
        at = pl.multiple_of(place[1] * columns, 128)
        my_query_ref[...] = 1.0 / jnp.sqrt(counts[:, pl.ds(at, columns)].astype(jnp.float32))
    else:
        for step in range(counts.shape[1] // columns):

            @pl.when(place[1] == step)
            def _():
                degree = counts[:, step * columns : (step + 1) * columns]
                my_query_ref[...] = 1.0 / jnp.sqrt(degree.astype(jnp.float32))
    for load in loads[3:]:
        load.wait()


def pair_body(mine_ref, got_ref, *outs):
    count = len(outs)
    for at, out_ref in enumerate(outs):
        step = (count - at) % count
        out_ref[...] = (mine_ref[step] + got_ref[step]).astype(out_ref.dtype)


def join_body(*refs):
    for step, ref in enumerate(refs[:-1]):
        refs[-1][step] = ref[...]


def query_body(*refs):
    part_refs, scale_ref, out_ref = refs[:-2], refs[-2], refs[-1]
    out_ref[...] = (add(part_refs) * scale_ref[...]).astype(out_ref.dtype)


def lift_only_body(*refs):
    part_refs, scale_ref, lifted_ref = refs[:-2], refs[-2], refs[-1]
    lifted_ref[...] = add(part_refs) * scale_ref[...]


def lift_body(*refs):
    part_refs, scale_ref, lifted_ref, gram_ref = refs[:-3], refs[-3], refs[-2], refs[-1]
    lifted = add(part_refs) * scale_ref[...]
    lifted_ref[...] = lifted
    gram_ref[...] = lax.dot_general(lifted, lifted, NT, precision=HIGH, preferred_element_type=jnp.float32)


def sum_body(*refs):
    refs[-1][...] = add(refs[:-1])


def finish_body(after, *refs):
    grams, lifted_ref, out_ref = refs[:-2], refs[-2], refs[-1]
    out_ref[...] = (
        lax.dot_general(
            inverse_factor(add(grams)), lifted_ref[...], NN, precision=HIGH, preferred_element_type=jnp.float32
        )
        * after
    )


def swap(value, axis, step):
    return lax.ppermute(value, axis, [(i, i ^ step) for i in range(lax.axis_size(axis))])


def spread_to(value, axis, stride=1):
    return [value] + [swap(value, axis, step) for step in range(stride, lax.axis_size(axis), stride)]


def deal(values, axis, stride=1):
    count = len(values)
    return [values[0]] + [swap(value, axis, (count - at) * stride) for at, value in enumerate(values[1:], 1)]


def add_up(*values):
    return call(sum_body, "sum", [WHOLE] * len(values), f32(*values[0].shape))(*values)


def terms_over_col(gram):
    return spread_to(add_up(gram, swap(gram, "col", 1)), "col", 2)


def shards(tiles, tile_ids, tile_count, query_degree, product_degree, panel):
    tile_set = tiles[0, 0]
    ids = tile_ids[0, 0]
    slots, side, _ = tile_set.shape
    width, share = panel.shape
    queries, products = query_degree.shape[0], product_degree.shape[0]
    query_tiles, product_tiles = queries // side, products // side
    n_row, n_col = lax.axis_size("row"), lax.axis_size("col")
    chips = n_col // 2
    row_at, col_at = lax.axis_index("row").astype(jnp.int32), lax.axis_index("col").astype(jnp.int32)
    columns = queries // n_col
    work = dict(flops=2 * slots * width * side * side, moved=2 * slots * side * side)
    scaled = call(
        start_body,
        "start",
        [SCALARS, AWAY, AWAY],
        bf16(width, share),
        [
            pltpu.VMEM((width, share), jnp.float32),
            pltpu.VMEM((1, products), jnp.int32),
            pltpu.SemaphoreType.DMA((2,)),
        ],
    )(row_at[None], in_hbm(panel), in_hbm(product_degree[None, :]))
    pieces = spread_to(scaled, "row")
    split = columns % side == 0
    tile_set, my_pscale, pscale, my_qscale, table = call(
        functools.partial(load_body, columns // side if split else 0),
        "load",
        [SCALARS, WHOLE] + [AWAY] * 4,
        [
            pltpu.VMEM((slots, side, side), jnp.bfloat16),
            f32(1, share),
            f32(1, products),
            f32(1, columns),
            jax.ShapeDtypeStruct((SINGLES + 1, slots), jnp.int32),
        ],
        [
            pltpu.SMEM(ids.shape, jnp.int32),
            pltpu.VMEM((1, products), jnp.int32),
            pltpu.VMEM((1, queries), jnp.int32),
            pltpu.SemaphoreType.DMA((3 + LOADS,)),
        ],
        moved=4 * slots * side * side,
        out_specs=[WHOLE] * 4 + [SCALARS],
    )(
        jnp.stack([row_at, col_at, tile_count[0, 0]]),
        scaled,
        in_hbm(tile_set),
        in_hbm(ids),
        in_hbm(product_degree[None, :]),
        in_hbm(query_degree[None, :]),
    )
    tile_set = pltpu.with_memory_space_constraint(tile_set, pltpu.VMEM)
    root_count = math.sqrt(products * n_col)
    half = f32(chips, width, columns)
    gram_rows = width * width // columns
    half_work = dict(flops=slots * width * side * side, moved=slots * side * side)
    query_scratch = pltpu.VMEM((query_tiles + 1, width, side), jnp.float32)
    product_scratch = pltpu.VMEM((product_tiles + 1, width, side), jnp.float32)
    query_held = pltpu.VMEM((query_tiles + 1, width, side), jnp.bfloat16)
    for iteration in range(ITERS):
        sets = SETS if iteration < ITERS - 1 else 1
        if iteration > 0:
            pieces = [piece for part in lifted for piece in spread_to(part, "row")]
            arrays = [WHOLE] * (len(pieces) + 2)
            message = f32(chips * width + gram_rows, columns)
            spread = pltpu.VMEM((product_tiles, width, side), jnp.float32)
            if split:
                held, other, gram = call(
                    functools.partial(next_other_body, len(pieces), chips),
                    "forward",
                    [SCALARS] + arrays,
                    [bf16(product_tiles + 1, 2 * width, side), message, f32(gram_rows, columns)],
                    [spread, query_scratch],
                    **half_work,
                )(table, *pieces, pscale, tile_set)
                got = swap(other, "col", 1)
                mine = call(
                    functools.partial(next_mine_body, chips),
                    "forward_rest",
                    [SCALARS] + [WHOLE] * 2,
                    f32(chips * width, columns),
                    [query_scratch],
                    **half_work,
                )(table, held, tile_set)
            else:
                mine, other, gram = call(
                    functools.partial(next_body, len(pieces), chips),
                    "forward",
                    [SCALARS] + arrays,
                    [f32(chips * width, columns), message, f32(gram_rows, columns)],
                    [spread, pltpu.VMEM((product_tiles + 1, 2 * width, side), jnp.bfloat16), query_scratch],
                    **work,
                )(table, *pieces, pscale, tile_set)
                got = swap(other, "col", 1)
            halves = 2 if columns % 256 == 0 else 1
            span = columns // halves
            shapes = [f32(width + width * width // span, span)] * chips + [f32(width, span)] * chips
            sums = call(
                functools.partial(next_pair_body, width, chips), "pair", [WHOLE] * 3, shapes[: halves * chips]
            )(mine, got, gram)
            parts = deal(sums[:chips], "col", 2)
            if halves == 1:
                rounded = call(next_query_body, "query", [WHOLE] * (chips + 1), bf16(width, columns))(
                    *parts, my_qscale
                )
            else:
                more = deal(sums[chips:], "col", 2)
                inverse, begun = call(
                    factor_query_body,
                    "query",
                    [WHOLE] * (chips + 1),
                    [f32(width, width), bf16(width, span)],
                    flops=2 * slots * width * side * side,
                )(*parts, my_qscale)
                rounded = call(rest_query_body, "query_rest", [WHOLE] * (chips + 3), bf16(width, columns))(
                    *more, inverse, begun, my_qscale
                )
        elif split:
            held, other = call(
                functools.partial(forward_other_body, n_row),
                "forward",
                [SCALARS] + [WHOLE] * (n_row + 1),
                [bf16(product_tiles + 1, width, side), half],
                [query_scratch],
                **half_work,
            )(table, *pieces, tile_set)
            got = swap(other, "col", 1)
            mine = call(
                forward_mine_body,
                "forward_rest",
                [SCALARS] + [WHOLE] * 2,
                half,
                [query_scratch],
                **half_work,
            )(table, held, tile_set)
        else:
            mine, other = call(
                functools.partial(forward_body, n_row),
                "forward",
                [SCALARS] + [WHOLE] * (n_row + 1),
                [half] * 2,
                [pltpu.VMEM((product_tiles + 1, width, side), jnp.bfloat16), query_scratch],
                **work,
            )(table, *pieces, tile_set)
            got = swap(other, "col", 1)
        if iteration == 0:
            sums = call(
                pair_body, "pair", [WHOLE] * 2, [f32(width, columns)] + [bf16(width, columns)] * (chips - 1)
            )(mine, got)
            parts = deal(sums, "col", 2)
            rounded = call(query_body, "query", [WHOLE] * (chips + 1), bf16(width, columns))(*parts, my_qscale)
        pieces = spread_to(rounded, "col", 2)
        here = call(join_body, "join", [WHOLE] * chips, bf16(chips, width, columns))(*pieces)
        there = swap(here, "col", 1)
        if split:
            begun = call(
                functools.partial(back_mine_body, chips),
                "backward",
                [SCALARS] + [WHOLE] * (chips + 1),
                f32(product_tiles + 1, width, side),
                [query_held],
                **half_work,
            )(table, *pieces, tile_set)
            sums = call(
                back_other_body,
                "backward_rest",
                [SCALARS] + [WHOLE] * 3,
                [f32(width // sets, share)] * (sets * n_row),
                [query_held, product_scratch],
                **half_work,
            )(table, there, begun, tile_set)
        else:
            sums = call(
                back_body,
                "backward",
                [SCALARS] + [WHOLE] * 3,
                [f32(width // sets, share)] * (sets * n_row),
                [query_held, product_scratch],
                **work,
            )(table, here, there, tile_set)
        parts = [deal(sums[n_row * part : n_row * (part + 1)], "row") for part in range(sets)]
        if iteration < ITERS - 1:
            lifted = [
                call(lift_only_body, "lift", [WHOLE] * (n_row + 1), f32(width // sets, share))(*part, my_pscale)
                for part in parts
            ]
    lifted, gram = call(
        lift_body, "lift", [WHOLE] * (n_row + 1), [f32(width, share), f32(width, width)]
    )(*parts[0], my_pscale)
    return call(
        functools.partial(finish_body, root_count), "finish", [WHOLE] * (chips + 1), f32(width, share)
    )(*terms_over_col(add_up(*spread_to(gram, "row"))), lifted)


def solution(mesh):
    in_specs = (
        P("row", "col", None, None, None),
        P("row", "col", None, None),
        P("row", "col"),
        P("row"),
        P("col"),
        P(None, ("col", "row")),
    )
    out_specs = P(None, ("col", "row"))
    return jax.shard_map(shards, mesh=mesh, in_specs=in_specs, out_specs=out_specs, check_vma=False)
```

```python
import functools
import math

import jax
import jax.numpy as jnp
from jax import lax
from jax.experimental import pallas as pl
from jax.experimental.pallas import tpu as pltpu
from jax.sharding import PartitionSpec as P

ITERS = 2
GROUP = 8
LOADS = 8
SETS = 2
PANEL_STEP = 8
HIGH = lax.Precision.HIGHEST
VMEM_BYTES = 12 * 1024 * 1024
NT = (((1,), (1,)), ((), ()))
NN = (((1,), (0,)), ((), ()))

def inverse_factor(gram):
    width = gram.shape[0]
    rows = lax.broadcasted_iota(jnp.int32, (width, width), 0)
    cols = lax.broadcasted_iota(jnp.int32, (width, width), 1)
    work = jnp.concatenate([gram, (rows == cols).astype(jnp.float32)], axis=1)
    done = []
    for first in range(0, width, PANEL_STEP):
        height = width - first
        columns = [
            jnp.broadcast_to(work[:, first + j : first + j + 1], (height, 2 * width))
            for j in range(PANEL_STEP)
        ]
        for j in range(PANEL_STEP):
            scale = lax.rsqrt(columns[j][j : j + 1, :])
            row = work[j : j + 1, :] * scale
            factor = columns[j] * scale
            done.append(row)
            for later in range(j + 1, PANEL_STEP):
                columns[later] = columns[later] - factor * (columns[later][j : j + 1, :] * scale)
            work = work - factor * row
        work = work[PANEL_STEP:, :]
    return jnp.concatenate(done, axis=0)[:, width:]


SLOT, QUERY, PRODUCT = range(3)
FIELDS, LISTS, ALL = 3, 3, 2
SINGLES = FIELDS * LISTS
ROW_AT, COL_AT = 3, 4
WHOLE = pl.BlockSpec(memory_space=pltpu.VMEM)
SCALARS = pl.BlockSpec(memory_space=pltpu.SMEM)
AWAY = pl.BlockSpec(memory_space=pltpu.MemorySpace.HBM)


def call(body, name, in_specs, out_shape, scratch=(), flops=0, moved=0, out_specs=None):
    many = isinstance(out_shape, (tuple, list))
    return pl.pallas_call(
        body,
        out_shape=out_shape,
        in_specs=in_specs,
        out_specs=out_specs or ([WHOLE] * len(out_shape) if many else WHOLE),
        scratch_shapes=scratch,
        compiler_params=pltpu.CompilerParams(vmem_limit_bytes=VMEM_BYTES),
        cost_estimate=pl.CostEstimate(flops=flops, bytes_accessed=moved, transcendentals=0),
        name=name,
    )


def in_hbm(value):
    return pltpu.with_memory_space_constraint(value, pltpu.MemorySpace.HBM)


def f32(*shape):
    return jax.ShapeDtypeStruct(shape, jnp.float32)


def bf16(*shape):
    return jax.ShapeDtypeStruct(shape, jnp.bfloat16)


def put(held, owner, value, side, row=0):
    span, share = slice(row, row + value.shape[0]), value.shape[1]
    if share >= side:
        per = share // side
        for piece in range(per):
            held[owner * per + piece, span] = value[:, piece * side : (piece + 1) * side]
    else:
        per = side // share
        for at in range(per):

            @pl.when(owner % per == at)
            def _():
                held[owner // per, span, at * share : (at + 1) * share] = value


def get(total, owner, out_ref, side, row=0):
    span, share = slice(row, row + out_ref.shape[0]), out_ref.shape[1]
    if share >= side:
        per = share // side
        for piece in range(per):
            out_ref[:, piece * side : (piece + 1) * side] = total[owner * per + piece, span].astype(out_ref.dtype)
    else:
        per = side // share
        for at in range(per):

            @pl.when(owner % per == at)
            def _():
                out_ref[...] = total[owner // per, span, at * share : (at + 1) * share].astype(out_ref.dtype)


def emit(total, out_refs, me, side):
    sets = total.shape[1] // out_refs[0].shape[0]
    count = len(out_refs) // sets
    for at, out_ref in enumerate(out_refs):
        part, at = divmod(at, count)
        get(total, me ^ ((count - at) % count), out_ref, side, part * out_ref.shape[0])


def spare(held):
    held[held.shape[0] - 1] = jnp.zeros(held.shape[1:], held.dtype)


def collect(held, piece_refs, me, side):
    sets = held.shape[1] // piece_refs[0].shape[0]
    count = len(piece_refs) // sets
    for at, piece_ref in enumerate(piece_refs):
        part, step = divmod(at, count)
        put(held, me ^ step, piece_ref[...], side, part * piece_ref.shape[0])


def products(which, take, give, dims, table, held, tile_ref, total):
    width = total.shape[1]
    slots = tile_ref.shape[0]

    def run(first, length):
        for lane in range(length):
            at = first + lane
            term = lax.dot_general(
                held[table[which * FIELDS + take, at]],
                tile_ref[table[which * FIELDS + SLOT, at]],
                dims,
                preferred_element_type=jnp.float32,
            )
            if term.shape[0] > width:
                term = term[:width] + term[width:]
            total[table[which * FIELDS + give, at]] += term

    if isinstance(which, int):
        run(0, slots)
        return

    def step(g, carry):
        run(slots // 2 + g * GROUP, GROUP)
        return carry

    run(0, slots // 2)
    rest = jnp.maximum(table[SINGLES, which] - slots // 2, 0)
    lax.fori_loop(0, jnp.minimum((rest + GROUP - 1) // GROUP, slots // 2 // GROUP), step, 0)


forward = functools.partial(products, take=PRODUCT, give=QUERY, dims=NT)
backward = functools.partial(products, take=QUERY, give=PRODUCT, dims=NN)


def emit_half(total, out_ref, me, side, flip):
    for step in range(out_ref.shape[0]):
        get(total, me ^ (2 * step + flip), out_ref.at[step], side)


def collect_half(held, piece_refs, me, side, flip):
    for step, piece_ref in enumerate(piece_refs):
        put(held, me ^ (2 * step + flip), piece_ref[...], side)


def forward_body(n_in, table, *refs):
    pieces, (tile_ref, mine_ref, other_ref, held, total) = refs[:n_in], refs[n_in:]
    side = tile_ref.shape[1]
    collect(held, pieces, table[SINGLES, ROW_AT], side)
    spare(held)
    total[...] = jnp.zeros_like(total)
    forward(ALL, table=table, held=held, tile_ref=tile_ref, total=total)
    emit_half(total, mine_ref, table[SINGLES, COL_AT], side, 0)
    emit_half(total, other_ref, table[SINGLES, COL_AT], side, 1)


def forward_other_body(n_in, table, *refs):
    pieces, (tile_ref, held, other_ref, total) = refs[:n_in], refs[n_in:]
    side, me = tile_ref.shape[1], table[SINGLES, COL_AT]
    collect(held, pieces, table[SINGLES, ROW_AT], side)
    spare(held)
    total[...] = jnp.zeros_like(total)
    forward(1 - me % 2, table=table, held=held, tile_ref=tile_ref, total=total)
    emit_half(total, other_ref, me, side, 1)


def forward_mine_body(table, held, tile_ref, mine_ref, total):
    side, me = tile_ref.shape[1], table[SINGLES, COL_AT]
    total[...] = jnp.zeros_like(total)
    forward(me % 2, table=table, held=held, tile_ref=tile_ref, total=total)
    emit_half(total, mine_ref, me, side, 0)


def back_body(table, here_ref, there_ref, tile_ref, *refs):
    out_refs, (held, total) = refs[:-2], refs[-2:]
    side = tile_ref.shape[1]
    for flip, ref in enumerate((here_ref, there_ref)):
        collect_half(held, [ref.at[step] for step in range(ref.shape[0])], table[SINGLES, COL_AT], side, flip)
    spare(held)
    total[...] = jnp.zeros_like(total)
    backward(ALL, table=table, held=held, tile_ref=tile_ref, total=total)
    emit(total, out_refs, table[SINGLES, ROW_AT], side)


def back_mine_body(n_in, table, *refs):
    pieces, (tile_ref, total, held) = refs[:n_in], refs[n_in:]
    me = table[SINGLES, COL_AT]
    collect_half(held, pieces, me, tile_ref.shape[1], 0)
    spare(held)
    total[...] = jnp.zeros_like(total)
    backward(me % 2, table=table, held=held, tile_ref=tile_ref, total=total)


def back_other_body(table, there_ref, begun_ref, tile_ref, *refs):
    out_refs, (held, total) = refs[:-2], refs[-2:]
    side, me = tile_ref.shape[1], table[SINGLES, COL_AT]
    collect_half(held, [there_ref.at[step] for step in range(there_ref.shape[0])], me, side, 1)
    spare(held)
    total[...] = begun_ref[...]
    backward(1 - me % 2, table=table, held=held, tile_ref=tile_ref, total=total)
    emit(total, out_refs, table[SINGLES, ROW_AT], side)


def pack_gram(gram, columns):
    per = columns // gram.shape[0]
    rows = gram.shape[0] // per
    return jnp.concatenate([gram[at * rows : (at + 1) * rows] for at in range(per)], axis=1)


def unpack_gram(rows, width):
    return jnp.concatenate([rows[:, at : at + width] for at in range(0, rows.shape[1], width)], axis=0)


def split_panel(pieces, scale_ref, spread, held, me):
    width, side = spread.shape[1:]
    collect(spread, pieces, me, side)
    spare(held)
    for tile in range(spread.shape[0]):
        value = spread[tile] * scale_ref[:, tile * side : (tile + 1) * side]
        high = value.astype(jnp.bfloat16)
        held[tile, :width] = high
        held[tile, width:] = (value - high.astype(jnp.float32)).astype(jnp.bfloat16)
    gram = jnp.zeros((width, width), jnp.float32)
    for tile in range(spread.shape[0]):
        gram = gram + lax.dot_general(
            spread[tile], spread[tile], NT, precision=HIGH, preferred_element_type=jnp.float32
        )
    return gram


def emit_rows(total, out_ref, chips, me, side, flip):
    width = total.shape[1]
    for step in range(chips):
        get(total, me ^ (2 * step + flip), out_ref.at[step * width : (step + 1) * width], side)


def next_body(n_in, chips, table, *refs):
    pieces, (scale_ref, tile_ref, mine_ref, other_ref, gram_ref, spread, held, total) = refs[:n_in], refs[n_in:]
    side, me, width = tile_ref.shape[1], table[SINGLES, COL_AT], total.shape[1]
    rows = pack_gram(split_panel(pieces, scale_ref, spread, held, table[SINGLES, ROW_AT]), gram_ref.shape[1])
    gram_ref[...] = rows
    other_ref[chips * width :] = rows
    total[...] = jnp.zeros_like(total)
    forward(ALL, table=table, held=held, tile_ref=tile_ref, total=total)
    emit_rows(total, mine_ref, chips, me, side, 0)
    emit_rows(total, other_ref, chips, me, side, 1)


def next_other_body(n_in, chips, table, *refs):
    pieces, (scale_ref, tile_ref, held, other_ref, gram_ref, spread, total) = refs[:n_in], refs[n_in:]
    side, me, width = tile_ref.shape[1], table[SINGLES, COL_AT], total.shape[1]
    rows = pack_gram(split_panel(pieces, scale_ref, spread, held, table[SINGLES, ROW_AT]), gram_ref.shape[1])
    gram_ref[...] = rows
    other_ref[chips * width :] = rows
    total[...] = jnp.zeros_like(total)
    forward(1 - me % 2, table=table, held=held, tile_ref=tile_ref, total=total)
    emit_rows(total, other_ref, chips, me, side, 1)


def next_mine_body(chips, table, held, tile_ref, mine_ref, total):
    side, me = tile_ref.shape[1], table[SINGLES, COL_AT]
    total[...] = jnp.zeros_like(total)
    forward(me % 2, table=table, held=held, tile_ref=tile_ref, total=total)
    emit_rows(total, mine_ref, chips, me, side, 0)


def next_pair_body(width, chips, mine_ref, got_ref, gram_ref, *outs):
    columns = outs[0].shape[1]
    gram = pack_gram(unpack_gram(gram_ref[...] + got_ref[chips * width :], width), columns)
    for at, out_ref in enumerate(outs):
        part, at = divmod(at, chips)
        step = (chips - at) % chips
        block = slice(step * width, (step + 1) * width), slice(part * columns, (part + 1) * columns)
        out_ref[:width] = mine_ref[block] + got_ref[block]
        if part == 0:
            out_ref[width:] = gram


def factor_query_body(*refs):
    part_refs, scale_ref, inverse_ref, out_ref = refs[:-3], refs[-3], refs[-2], refs[-1]
    width, columns = out_ref.shape
    total = add(part_refs)
    inverse = inverse_factor(unpack_gram(total[width:], width))
    inverse_ref[...] = inverse
    current = lax.dot_general(inverse, total[:width], NN, precision=HIGH, preferred_element_type=jnp.float32)
    out_ref[...] = (current * scale_ref[:, :columns]).astype(out_ref.dtype)


def rest_query_body(*refs):
    part_refs, inverse_ref, begun_ref, scale_ref, out_ref = refs[:-4], *refs[-4:]
    columns = begun_ref.shape[1]
    current = lax.dot_general(
        inverse_ref[...], add(part_refs), NN, precision=HIGH, preferred_element_type=jnp.float32
    )
    out_ref[:, :columns] = begun_ref[...]
    out_ref[:, columns:] = (current * scale_ref[:, columns:]).astype(out_ref.dtype)


def next_query_body(*refs):
    part_refs, scale_ref, out_ref = refs[:-2], refs[-2], refs[-1]
    width = out_ref.shape[0]
    total = add(part_refs)
    inverse = inverse_factor(unpack_gram(total[width:], width))
    current = lax.dot_general(inverse, total[:width], NN, precision=HIGH, preferred_element_type=jnp.float32)
    out_ref[...] = (current * scale_ref[...]).astype(out_ref.dtype)


def add(refs):
    total = refs[0][...].astype(jnp.float32)
    for ref in refs[1:]:
        total = total + ref[...].astype(jnp.float32)
    return total


def start_body(place, panel_ref, degree_ref, out_ref, held, degrees, sems):
    share = panel_ref.shape[1]
    at = pl.multiple_of(place[0] * share, 128)
    loads = [
        pltpu.make_async_copy(degree_ref, degrees, sems.at[0]),
        pltpu.make_async_copy(panel_ref, held, sems.at[1]),
    ]
    for load in loads:
        load.start()
    for load in loads:
        load.wait()
    scale = 1.0 / jnp.sqrt(degrees[:, pl.ds(at, share)].astype(jnp.float32))
    out_ref[...] = (held[...] * scale).astype(out_ref.dtype)


def clear_table(table, lists, query_tiles, product_tiles):
    for which in lists:
        table[SINGLES, which] = 0
        for at in range(table.shape[1]):
            table[which * FIELDS + SLOT, at] = 0
            table[which * FIELDS + QUERY, at] = query_tiles
            table[which * FIELDS + PRODUCT, at] = product_tiles


def fill_table(table, ids, place, per):
    table[SINGLES, ROW_AT] = place[0]
    table[SINGLES, COL_AT] = place[1]

    def step(slot, carry):
        query, product = ids[0, slot], ids[1, slot]
        which = query // per % 2 if per else ALL
        at = table[SINGLES, which]
        table[which * FIELDS + SLOT, at] = slot
        table[which * FIELDS + QUERY, at] = query
        table[which * FIELDS + PRODUCT, at] = product
        table[SINGLES, which] = at + 1
        return carry

    lax.fori_loop(0, jnp.minimum(place[2], ids.shape[1]), step, 0)


def load_body(per, place, after_ref, tile_ref, id_ref, product_ref, query_ref, *refs):
    keep, my_product_ref, product_out, my_query_ref, table, ids, degrees, counts, sems = refs
    loads = [
        pltpu.make_async_copy(id_ref, ids, sems.at[0]),
        pltpu.make_async_copy(product_ref, degrees, sems.at[1]),
        pltpu.make_async_copy(query_ref, counts, sems.at[2]),
    ]
    part = tile_ref.shape[0] // LOADS
    for step in range(LOADS):
        span = pl.ds(step * part, part)
        loads.append(pltpu.make_async_copy(tile_ref.at[span], keep.at[span], sems.at[3 + step]))
    for load in loads:
        load.start()
    side = tile_ref.shape[1]
    lists = (0, 1) if per else (ALL,)
    clear_table(table, lists, query_ref.shape[1] // side, product_ref.shape[1] // side)
    loads[0].wait()
    fill_table(table, ids, place, per)
    loads[1].wait()
    product_out[...] = 1.0 / jnp.sqrt(degrees[...].astype(jnp.float32))
    share = my_product_ref.shape[1]
    at = pl.multiple_of(place[0] * share, 128)
    my_product_ref[...] = product_out[:, pl.ds(at, share)]
    loads[2].wait()
    columns = my_query_ref.shape[1]
    if columns % 128 == 0:
        at = pl.multiple_of(place[1] * columns, 128)
        my_query_ref[...] = 1.0 / jnp.sqrt(counts[:, pl.ds(at, columns)].astype(jnp.float32))
    else:
        for step in range(counts.shape[1] // columns):

            @pl.when(place[1] == step)
            def _():
                degree = counts[:, step * columns : (step + 1) * columns]
                my_query_ref[...] = 1.0 / jnp.sqrt(degree.astype(jnp.float32))
    for load in loads[3:]:
        load.wait()


def pair_body(mine_ref, got_ref, *outs):
    count = len(outs)
    for at, out_ref in enumerate(outs):
        step = (count - at) % count
        out_ref[...] = (mine_ref[step] + got_ref[step]).astype(out_ref.dtype)


def join_body(*refs):
    for step, ref in enumerate(refs[:-1]):
        refs[-1][step] = ref[...]


def query_body(*refs):
    part_refs, scale_ref, out_ref = refs[:-2], refs[-2], refs[-1]
    out_ref[...] = (add(part_refs) * scale_ref[...]).astype(out_ref.dtype)


def lift_only_body(*refs):
    part_refs, scale_ref, lifted_ref = refs[:-2], refs[-2], refs[-1]
    lifted_ref[...] = add(part_refs) * scale_ref[...]


def lift_body(*refs):
    part_refs, scale_ref, lifted_ref, gram_ref = refs[:-3], refs[-3], refs[-2], refs[-1]
    lifted = add(part_refs) * scale_ref[...]
    lifted_ref[...] = lifted
    gram_ref[...] = lax.dot_general(lifted, lifted, NT, precision=HIGH, preferred_element_type=jnp.float32)


def sum_body(*refs):
    refs[-1][...] = add(refs[:-1])


def finish_body(after, table, total_ref, got_ref, lifted_ref, out_ref):
    gram = jnp.where(table[SINGLES, COL_AT] % 2 == 1, total_ref[...], got_ref[...])
    out_ref[...] = (
        lax.dot_general(
            inverse_factor(gram), lifted_ref[...], NN, precision=HIGH, preferred_element_type=jnp.float32
        )
        * after
    )


def swap(value, axis, step):
    return lax.ppermute(value, axis, [(i, i ^ step) for i in range(lax.axis_size(axis))])


def spread_to(value, axis, stride=1):
    return [value] + [swap(value, axis, step) for step in range(stride, lax.axis_size(axis), stride)]


def deal(values, axis, stride=1):
    count = len(values)
    return [values[0]] + [swap(value, axis, (count - at) * stride) for at, value in enumerate(values[1:], 1)]


def add_up(*values):
    return call(sum_body, "sum", [WHOLE] * len(values), f32(*values[0].shape))(*values)


def core_one_terms(value, axis):
    n_row, n_col = lax.axis_size("row"), lax.axis_size("col")
    terms = [value]
    reach = [(step, 0) for step in range(1, n_row)] if axis == "row" else [(0, step) for step in range(2, n_col, 2)]
    for row_step, col_step in reach:
        pairs = [
            (row * n_col + col, (row ^ row_step) * n_col + (col ^ col_step))
            for row in range(n_row)
            for col in range(1, n_col, 2)
        ]
        terms.append(lax.ppermute(value, ("row", "col"), pairs))
    return terms


def hand_over(value):
    return lax.ppermute(value, "col", [(col, col - 1) for col in range(1, lax.axis_size("col"), 2)])


def shards(tiles, tile_ids, tile_count, query_degree, product_degree, panel):
    tile_set = tiles[0, 0]
    ids = tile_ids[0, 0]
    slots, side, _ = tile_set.shape
    width, share = panel.shape
    queries, products = query_degree.shape[0], product_degree.shape[0]
    query_tiles, product_tiles = queries // side, products // side
    n_row, n_col = lax.axis_size("row"), lax.axis_size("col")
    chips = n_col // 2
    row_at, col_at = lax.axis_index("row").astype(jnp.int32), lax.axis_index("col").astype(jnp.int32)
    columns = queries // n_col
    work = dict(flops=2 * slots * width * side * side, moved=2 * slots * side * side)
    scaled = call(
        start_body,
        "start",
        [SCALARS, AWAY, AWAY],
        bf16(width, share),
        [
            pltpu.VMEM((width, share), jnp.float32),
            pltpu.VMEM((1, products), jnp.int32),
            pltpu.SemaphoreType.DMA((2,)),
        ],
    )(row_at[None], in_hbm(panel), in_hbm(product_degree[None, :]))
    pieces = spread_to(scaled, "row")
    split = columns % side == 0
    tile_set, my_pscale, pscale, my_qscale, table = call(
        functools.partial(load_body, columns // side if split else 0),
        "load",
        [SCALARS, WHOLE] + [AWAY] * 4,
        [
            pltpu.VMEM((slots, side, side), jnp.bfloat16),
            f32(1, share),
            f32(1, products),
            f32(1, columns),
            jax.ShapeDtypeStruct((SINGLES + 1, slots), jnp.int32),
        ],
        [
            pltpu.SMEM(ids.shape, jnp.int32),
            pltpu.VMEM((1, products), jnp.int32),
            pltpu.VMEM((1, queries), jnp.int32),
            pltpu.SemaphoreType.DMA((3 + LOADS,)),
        ],
        moved=4 * slots * side * side,
        out_specs=[WHOLE] * 4 + [SCALARS],
    )(
        jnp.stack([row_at, col_at, tile_count[0, 0]]),
        scaled,
        in_hbm(tile_set),
        in_hbm(ids),
        in_hbm(product_degree[None, :]),
        in_hbm(query_degree[None, :]),
    )
    tile_set = pltpu.with_memory_space_constraint(tile_set, pltpu.VMEM)
    root_count = math.sqrt(products * n_col)
    half = f32(chips, width, columns)
    gram_rows = width * width // columns
    half_work = dict(flops=slots * width * side * side, moved=slots * side * side)
    query_scratch = pltpu.VMEM((query_tiles + 1, width, side), jnp.float32)
    product_scratch = pltpu.VMEM((product_tiles + 1, width, side), jnp.float32)
    query_held = pltpu.VMEM((query_tiles + 1, width, side), jnp.bfloat16)
    for iteration in range(ITERS):
        sets = SETS if iteration < ITERS - 1 else 1
        if iteration > 0:
            pieces = [piece for part in lifted for piece in spread_to(part, "row")]
            arrays = [WHOLE] * (len(pieces) + 2)
            message = f32(chips * width + gram_rows, columns)
            spread = pltpu.VMEM((product_tiles, width, side), jnp.float32)
            if split:
                held, other, gram = call(
                    functools.partial(next_other_body, len(pieces), chips),
                    "forward",
                    [SCALARS] + arrays,
                    [bf16(product_tiles + 1, 2 * width, side), message, f32(gram_rows, columns)],
                    [spread, query_scratch],
                    **half_work,
                )(table, *pieces, pscale, tile_set)
                got = swap(other, "col", 1)
                mine = call(
                    functools.partial(next_mine_body, chips),
                    "forward_rest",
                    [SCALARS] + [WHOLE] * 2,
                    f32(chips * width, columns),
                    [query_scratch],
                    **half_work,
                )(table, held, tile_set)
            else:
                mine, other, gram = call(
                    functools.partial(next_body, len(pieces), chips),
                    "forward",
                    [SCALARS] + arrays,
                    [f32(chips * width, columns), message, f32(gram_rows, columns)],
                    [spread, pltpu.VMEM((product_tiles + 1, 2 * width, side), jnp.bfloat16), query_scratch],
                    **work,
                )(table, *pieces, pscale, tile_set)
                got = swap(other, "col", 1)
            halves = 2 if columns % 256 == 0 else 1
            span = columns // halves
            shapes = [f32(width + width * width // span, span)] * chips + [f32(width, span)] * chips
            sums = call(
                functools.partial(next_pair_body, width, chips), "pair", [WHOLE] * 3, shapes[: halves * chips]
            )(mine, got, gram)
            parts = deal(sums[:chips], "col", 2)
            if halves == 1:
                rounded = call(next_query_body, "query", [WHOLE] * (chips + 1), bf16(width, columns))(
                    *parts, my_qscale
                )
            else:
                more = deal(sums[chips:], "col", 2)
                inverse, begun = call(
                    factor_query_body,
                    "query",
                    [WHOLE] * (chips + 1),
                    [f32(width, width), bf16(width, span)],
                    flops=2 * slots * width * side * side,
                )(*parts, my_qscale)
                rounded = call(rest_query_body, "query_rest", [WHOLE] * (chips + 3), bf16(width, columns))(
                    *more, inverse, begun, my_qscale
                )
        elif split:
            held, other = call(
                functools.partial(forward_other_body, n_row),
                "forward",
                [SCALARS] + [WHOLE] * (n_row + 1),
                [bf16(product_tiles + 1, width, side), half],
                [query_scratch],
                **half_work,
            )(table, *pieces, tile_set)
            got = swap(other, "col", 1)
            mine = call(
                forward_mine_body,
                "forward_rest",
                [SCALARS] + [WHOLE] * 2,
                half,
                [query_scratch],
                **half_work,
            )(table, held, tile_set)
        else:
            mine, other = call(
                functools.partial(forward_body, n_row),
                "forward",
                [SCALARS] + [WHOLE] * (n_row + 1),
                [half] * 2,
                [pltpu.VMEM((product_tiles + 1, width, side), jnp.bfloat16), query_scratch],
                **work,
            )(table, *pieces, tile_set)
            got = swap(other, "col", 1)
        if iteration == 0:
            sums = call(
                pair_body, "pair", [WHOLE] * 2, [f32(width, columns)] + [bf16(width, columns)] * (chips - 1)
            )(mine, got)
            parts = deal(sums, "col", 2)
            rounded = call(query_body, "query", [WHOLE] * (chips + 1), bf16(width, columns))(*parts, my_qscale)
        pieces = spread_to(rounded, "col", 2)
        here = call(join_body, "join", [WHOLE] * chips, bf16(chips, width, columns))(*pieces)
        there = swap(here, "col", 1)
        if split:
            begun = call(
                functools.partial(back_mine_body, chips),
                "backward",
                [SCALARS] + [WHOLE] * (chips + 1),
                f32(product_tiles + 1, width, side),
                [query_held],
                **half_work,
            )(table, *pieces, tile_set)
            sums = call(
                back_other_body,
                "backward_rest",
                [SCALARS] + [WHOLE] * 3,
                [f32(width // sets, share)] * (sets * n_row),
                [query_held, product_scratch],
                **half_work,
            )(table, there, begun, tile_set)
        else:
            sums = call(
                back_body,
                "backward",
                [SCALARS] + [WHOLE] * 3,
                [f32(width // sets, share)] * (sets * n_row),
                [query_held, product_scratch],
                **work,
            )(table, here, there, tile_set)
        parts = [deal(sums[n_row * part : n_row * (part + 1)], "row") for part in range(sets)]
        if iteration < ITERS - 1:
            lifted = [
                call(lift_only_body, "lift", [WHOLE] * (n_row + 1), f32(width // sets, share))(*part, my_pscale)
                for part in parts
            ]
    lifted, gram = call(
        lift_body, "lift", [WHOLE] * (n_row + 1), [f32(width, share), f32(width, width)]
    )(*parts[0], my_pscale)
    total = add_up(gram, swap(gram, "col", 1))
    for axis in ("row", "col"):
        total = add_up(*core_one_terms(total, axis))
    return call(
        functools.partial(finish_body, root_count), "finish", [SCALARS] + [WHOLE] * 3, f32(width, share)
    )(table, total, hand_over(total), lifted)


def solution(mesh):
    in_specs = (
        P("row", "col", None, None, None),
        P("row", "col", None, None),
        P("row", "col"),
        P("row"),
        P("col"),
        P(None, ("col", "row")),
    )
    out_specs = P(None, ("col", "row"))
    return jax.shard_map(shards, mesh=mesh, in_specs=in_specs, out_specs=out_specs, check_vma=False)
```

```python
import functools
import math

import jax
import jax.numpy as jnp
from jax import lax
from jax.experimental import pallas as pl
from jax.experimental.pallas import tpu as pltpu
from jax.sharding import PartitionSpec as P

ITERS = 2
GROUP = 8
LOADS = 8
SETS = 2
PANEL_STEP = 8
HIGH = lax.Precision.HIGHEST
VMEM_BYTES = 12 * 1024 * 1024
NT = (((1,), (1,)), ((), ()))
NN = (((1,), (0,)), ((), ()))

def inverse_factor(gram):
    width = gram.shape[0]
    rows = lax.broadcasted_iota(jnp.int32, (width, width), 0)
    cols = lax.broadcasted_iota(jnp.int32, (width, width), 1)
    work = jnp.concatenate([gram, (rows == cols).astype(jnp.float32)], axis=1)
    done = []
    for first in range(0, width, PANEL_STEP):
        height = width - first
        columns = [
            jnp.broadcast_to(work[:, first + j : first + j + 1], (height, 2 * width))
            for j in range(PANEL_STEP)
        ]
        for j in range(PANEL_STEP):
            scale = lax.rsqrt(columns[j][j : j + 1, :])
            row = work[j : j + 1, :] * scale
            factor = columns[j] * scale
            done.append(row)
            for later in range(j + 1, PANEL_STEP):
                columns[later] = columns[later] - factor * (columns[later][j : j + 1, :] * scale)
            work = work - factor * row
        work = work[PANEL_STEP:, :]
    return jnp.concatenate(done, axis=0)[:, width:]


SLOT, QUERY, PRODUCT = range(3)
FIELDS, LISTS, ALL = 3, 3, 2
SINGLES = FIELDS * LISTS
ROW_AT, COL_AT = 3, 4
WHOLE = pl.BlockSpec(memory_space=pltpu.VMEM)
SCALARS = pl.BlockSpec(memory_space=pltpu.SMEM)
AWAY = pl.BlockSpec(memory_space=pltpu.MemorySpace.HBM)


def call(body, name, in_specs, out_shape, scratch=(), flops=0, moved=0, out_specs=None):
    many = isinstance(out_shape, (tuple, list))
    return pl.pallas_call(
        body,
        out_shape=out_shape,
        in_specs=in_specs,
        out_specs=out_specs or ([WHOLE] * len(out_shape) if many else WHOLE),
        scratch_shapes=scratch,
        compiler_params=pltpu.CompilerParams(vmem_limit_bytes=VMEM_BYTES),
        cost_estimate=pl.CostEstimate(flops=flops, bytes_accessed=moved, transcendentals=0),
        name=name,
    )


def in_hbm(value):
    return pltpu.with_memory_space_constraint(value, pltpu.MemorySpace.HBM)


def f32(*shape):
    return jax.ShapeDtypeStruct(shape, jnp.float32)


def bf16(*shape):
    return jax.ShapeDtypeStruct(shape, jnp.bfloat16)


def put(held, owner, value, side, row=0):
    span, share = slice(row, row + value.shape[0]), value.shape[1]
    if share >= side:
        per = share // side
        for piece in range(per):
            held[owner * per + piece, span] = value[:, piece * side : (piece + 1) * side]
    else:
        per = side // share
        for at in range(per):

            @pl.when(owner % per == at)
            def _():
                held[owner // per, span, at * share : (at + 1) * share] = value


def get(total, owner, out_ref, side, row=0):
    span, share = slice(row, row + out_ref.shape[0]), out_ref.shape[1]
    if share >= side:
        per = share // side
        for piece in range(per):
            out_ref[:, piece * side : (piece + 1) * side] = total[owner * per + piece, span].astype(out_ref.dtype)
    else:
        per = side // share
        for at in range(per):

            @pl.when(owner % per == at)
            def _():
                out_ref[...] = total[owner // per, span, at * share : (at + 1) * share].astype(out_ref.dtype)


def emit(total, out_refs, me, side):
    sets = total.shape[1] // out_refs[0].shape[0]
    count = len(out_refs) // sets
    for at, out_ref in enumerate(out_refs):
        part, at = divmod(at, count)
        get(total, me ^ ((count - at) % count), out_ref, side, part * out_ref.shape[0])


def spare(held):
    held[held.shape[0] - 1] = jnp.zeros(held.shape[1:], held.dtype)


def collect(held, piece_refs, me, side):
    sets = held.shape[1] // piece_refs[0].shape[0]
    count = len(piece_refs) // sets
    for at, piece_ref in enumerate(piece_refs):
        part, step = divmod(at, count)
        put(held, me ^ step, piece_ref[...], side, part * piece_ref.shape[0])


def products(which, take, give, dims, table, held, tile_ref, total):
    width = total.shape[1]
    slots = tile_ref.shape[0]

    def run(first, length):
        for lane in range(length):
            at = first + lane
            term = lax.dot_general(
                held[table[which * FIELDS + take, at]],
                tile_ref[table[which * FIELDS + SLOT, at]],
                dims,
                preferred_element_type=jnp.float32,
            )
            if term.shape[0] > width:
                term = term[:width] + term[width:]
            total[table[which * FIELDS + give, at]] += term

    if isinstance(which, int):
        run(0, slots)
        return

    def step(g, carry):
        run(slots // 2 + g * GROUP, GROUP)
        return carry

    run(0, slots // 2)
    rest = jnp.maximum(table[SINGLES, which] - slots // 2, 0)
    lax.fori_loop(0, jnp.minimum((rest + GROUP - 1) // GROUP, slots // 2 // GROUP), step, 0)


forward = functools.partial(products, take=PRODUCT, give=QUERY, dims=NT)
backward = functools.partial(products, take=QUERY, give=PRODUCT, dims=NN)


def emit_half(total, out_ref, me, side, flip):
    for step in range(out_ref.shape[0]):
        get(total, me ^ (2 * step + flip), out_ref.at[step], side)


def collect_half(held, piece_refs, me, side, flip):
    for step, piece_ref in enumerate(piece_refs):
        put(held, me ^ (2 * step + flip), piece_ref[...], side)


def forward_body(n_in, table, *refs):
    pieces, (tile_ref, mine_ref, other_ref, held, total) = refs[:n_in], refs[n_in:]
    side = tile_ref.shape[1]
    collect(held, pieces, table[SINGLES, ROW_AT], side)
    spare(held)
    total[...] = jnp.zeros_like(total)
    forward(ALL, table=table, held=held, tile_ref=tile_ref, total=total)
    emit_half(total, mine_ref, table[SINGLES, COL_AT], side, 0)
    emit_half(total, other_ref, table[SINGLES, COL_AT], side, 1)


def forward_other_body(n_in, table, *refs):
    pieces, (tile_ref, held, other_ref, total) = refs[:n_in], refs[n_in:]
    side, me = tile_ref.shape[1], table[SINGLES, COL_AT]
    collect(held, pieces, table[SINGLES, ROW_AT], side)
    spare(held)
    total[...] = jnp.zeros_like(total)
    forward(1 - me % 2, table=table, held=held, tile_ref=tile_ref, total=total)
    emit_half(total, other_ref, me, side, 1)


def forward_mine_body(table, held, tile_ref, mine_ref, total):
    side, me = tile_ref.shape[1], table[SINGLES, COL_AT]
    total[...] = jnp.zeros_like(total)
    forward(me % 2, table=table, held=held, tile_ref=tile_ref, total=total)
    emit_half(total, mine_ref, me, side, 0)


def back_body(table, here_ref, there_ref, tile_ref, *refs):
    out_refs, (held, total) = refs[:-2], refs[-2:]
    side = tile_ref.shape[1]
    for flip, ref in enumerate((here_ref, there_ref)):
        collect_half(held, [ref.at[step] for step in range(ref.shape[0])], table[SINGLES, COL_AT], side, flip)
    spare(held)
    total[...] = jnp.zeros_like(total)
    backward(ALL, table=table, held=held, tile_ref=tile_ref, total=total)
    emit(total, out_refs, table[SINGLES, ROW_AT], side)


def back_mine_body(n_in, table, *refs):
    pieces, (tile_ref, total, held) = refs[:n_in], refs[n_in:]
    me = table[SINGLES, COL_AT]
    collect_half(held, pieces, me, tile_ref.shape[1], 0)
    spare(held)
    total[...] = jnp.zeros_like(total)
    backward(me % 2, table=table, held=held, tile_ref=tile_ref, total=total)


def back_other_body(table, there_ref, begun_ref, tile_ref, *refs):
    out_refs, (held, total) = refs[:-2], refs[-2:]
    side, me = tile_ref.shape[1], table[SINGLES, COL_AT]
    collect_half(held, [there_ref.at[step] for step in range(there_ref.shape[0])], me, side, 1)
    spare(held)
    total[...] = begun_ref[...]
    backward(1 - me % 2, table=table, held=held, tile_ref=tile_ref, total=total)
    emit(total, out_refs, table[SINGLES, ROW_AT], side)


def pack_gram(gram, columns):
    per = columns // gram.shape[0]
    rows = gram.shape[0] // per
    return jnp.concatenate([gram[at * rows : (at + 1) * rows] for at in range(per)], axis=1)


def unpack_gram(rows, width):
    return jnp.concatenate([rows[:, at : at + width] for at in range(0, rows.shape[1], width)], axis=0)


def split_panel(pieces, scale_ref, spread, held, me):
    width, side = spread.shape[1:]
    collect(spread, pieces, me, side)
    spare(held)
    for tile in range(spread.shape[0]):
        value = spread[tile] * scale_ref[:, tile * side : (tile + 1) * side]
        high = value.astype(jnp.bfloat16)
        held[tile, :width] = high
        held[tile, width:] = (value - high.astype(jnp.float32)).astype(jnp.bfloat16)
    gram = jnp.zeros((width, width), jnp.float32)
    for tile in range(spread.shape[0]):
        gram = gram + lax.dot_general(
            spread[tile], spread[tile], NT, precision=HIGH, preferred_element_type=jnp.float32
        )
    return gram


def emit_rows(total, out_ref, chips, me, side, flip):
    width = total.shape[1]
    for step in range(chips):
        get(total, me ^ (2 * step + flip), out_ref.at[step * width : (step + 1) * width], side)


def next_body(n_in, chips, table, *refs):
    pieces, (scale_ref, tile_ref, mine_ref, other_ref, gram_ref, spread, held, total) = refs[:n_in], refs[n_in:]
    side, me, width = tile_ref.shape[1], table[SINGLES, COL_AT], total.shape[1]
    rows = pack_gram(split_panel(pieces, scale_ref, spread, held, table[SINGLES, ROW_AT]), gram_ref.shape[1])
    gram_ref[...] = rows
    other_ref[chips * width :] = rows
    total[...] = jnp.zeros_like(total)
    forward(ALL, table=table, held=held, tile_ref=tile_ref, total=total)
    emit_rows(total, mine_ref, chips, me, side, 0)
    emit_rows(total, other_ref, chips, me, side, 1)


def next_other_body(n_in, chips, table, *refs):
    pieces, (scale_ref, tile_ref, held, other_ref, gram_ref, spread, total) = refs[:n_in], refs[n_in:]
    side, me, width = tile_ref.shape[1], table[SINGLES, COL_AT], total.shape[1]
    rows = pack_gram(split_panel(pieces, scale_ref, spread, held, table[SINGLES, ROW_AT]), gram_ref.shape[1])
    gram_ref[...] = rows
    other_ref[chips * width :] = rows
    total[...] = jnp.zeros_like(total)
    forward(1 - me % 2, table=table, held=held, tile_ref=tile_ref, total=total)
    emit_rows(total, other_ref, chips, me, side, 1)


def next_mine_body(chips, table, held, tile_ref, mine_ref, total):
    side, me = tile_ref.shape[1], table[SINGLES, COL_AT]
    total[...] = jnp.zeros_like(total)
    forward(me % 2, table=table, held=held, tile_ref=tile_ref, total=total)
    emit_rows(total, mine_ref, chips, me, side, 0)


def next_pair_body(width, chips, mine_ref, got_ref, gram_ref, *outs):
    columns = outs[0].shape[1]
    gram = pack_gram(unpack_gram(gram_ref[...] + got_ref[chips * width :], width), columns)
    for at, out_ref in enumerate(outs):
        part, at = divmod(at, chips)
        step = (chips - at) % chips
        block = slice(step * width, (step + 1) * width), slice(part * columns, (part + 1) * columns)
        out_ref[:width] = mine_ref[block] + got_ref[block]
        if part == 0:
            out_ref[width:] = gram


def factor_query_body(*refs):
    part_refs, scale_ref, inverse_ref, out_ref = refs[:-3], refs[-3], refs[-2], refs[-1]
    width, columns = out_ref.shape
    total = add(part_refs)
    inverse = inverse_factor(unpack_gram(total[width:], width))
    inverse_ref[...] = inverse
    current = lax.dot_general(inverse, total[:width], NN, precision=HIGH, preferred_element_type=jnp.float32)
    out_ref[...] = (current * scale_ref[:, :columns]).astype(out_ref.dtype)


def rest_query_body(*refs):
    part_refs, inverse_ref, begun_ref, scale_ref, out_ref = refs[:-4], *refs[-4:]
    columns = begun_ref.shape[1]
    current = lax.dot_general(
        inverse_ref[...], add(part_refs), NN, precision=HIGH, preferred_element_type=jnp.float32
    )
    out_ref[:, :columns] = begun_ref[...]
    out_ref[:, columns:] = (current * scale_ref[:, columns:]).astype(out_ref.dtype)


def next_query_body(*refs):
    part_refs, scale_ref, out_ref = refs[:-2], refs[-2], refs[-1]
    width = out_ref.shape[0]
    total = add(part_refs)
    inverse = inverse_factor(unpack_gram(total[width:], width))
    current = lax.dot_general(inverse, total[:width], NN, precision=HIGH, preferred_element_type=jnp.float32)
    out_ref[...] = (current * scale_ref[...]).astype(out_ref.dtype)


def add(refs):
    total = refs[0][...].astype(jnp.float32)
    for ref in refs[1:]:
        total = total + ref[...].astype(jnp.float32)
    return total


def start_body(place, panel_ref, degree_ref, out_ref, held, degrees, sems):
    share = panel_ref.shape[1]
    at = pl.multiple_of(place[0] * share, 128)
    loads = [
        pltpu.make_async_copy(degree_ref, degrees, sems.at[0]),
        pltpu.make_async_copy(panel_ref, held, sems.at[1]),
    ]
    for load in loads:
        load.start()
    for load in loads:
        load.wait()
    scale = 1.0 / jnp.sqrt(degrees[:, pl.ds(at, share)].astype(jnp.float32))
    out_ref[...] = (held[...] * scale).astype(out_ref.dtype)


def clear_table(table, lists, query_tiles, product_tiles):
    for which in lists:
        table[SINGLES, which] = 0
        for at in range(table.shape[1]):
            table[which * FIELDS + SLOT, at] = 0
            table[which * FIELDS + QUERY, at] = query_tiles
            table[which * FIELDS + PRODUCT, at] = product_tiles


def fill_table(table, ids, place, per):
    table[SINGLES, ROW_AT] = place[0]
    table[SINGLES, COL_AT] = place[1]

    def step(slot, carry):
        query, product = ids[0, slot], ids[1, slot]
        which = query // per % 2 if per else ALL
        at = table[SINGLES, which]
        table[which * FIELDS + SLOT, at] = slot
        table[which * FIELDS + QUERY, at] = query
        table[which * FIELDS + PRODUCT, at] = product
        table[SINGLES, which] = at + 1
        return carry

    lax.fori_loop(0, jnp.minimum(place[2], ids.shape[1]), step, 0)


def load_body(per, place, after_ref, tile_ref, id_ref, product_ref, query_ref, *refs):
    keep, my_product_ref, product_out, my_query_ref, table, ids, degrees, counts, sems = refs
    loads = [
        pltpu.make_async_copy(id_ref, ids, sems.at[0]),
        pltpu.make_async_copy(product_ref, degrees, sems.at[1]),
        pltpu.make_async_copy(query_ref, counts, sems.at[2]),
    ]
    part = tile_ref.shape[0] // LOADS
    for step in range(LOADS):
        span = pl.ds(step * part, part)
        loads.append(pltpu.make_async_copy(tile_ref.at[span], keep.at[span], sems.at[3 + step]))
    for load in loads:
        load.start()
    side = tile_ref.shape[1]
    lists = (0, 1) if per else (ALL,)
    clear_table(table, lists, query_ref.shape[1] // side, product_ref.shape[1] // side)
    loads[0].wait()
    fill_table(table, ids, place, per)
    loads[1].wait()
    product_out[...] = 1.0 / jnp.sqrt(degrees[...].astype(jnp.float32))
    share = my_product_ref.shape[1]
    at = pl.multiple_of(place[0] * share, 128)
    my_product_ref[...] = product_out[:, pl.ds(at, share)]
    loads[2].wait()
    columns = my_query_ref.shape[1]
    if columns % 128 == 0:
        at = pl.multiple_of(place[1] * columns, 128)
        my_query_ref[...] = 1.0 / jnp.sqrt(counts[:, pl.ds(at, columns)].astype(jnp.float32))
    else:
        for step in range(counts.shape[1] // columns):

            @pl.when(place[1] == step)
            def _():
                degree = counts[:, step * columns : (step + 1) * columns]
                my_query_ref[...] = 1.0 / jnp.sqrt(degree.astype(jnp.float32))
    for load in loads[3:]:
        load.wait()


def pair_body(mine_ref, got_ref, *outs):
    count = len(outs)
    for at, out_ref in enumerate(outs):
        step = (count - at) % count
        out_ref[...] = (mine_ref[step] + got_ref[step]).astype(out_ref.dtype)


def join_body(*refs):
    for step, ref in enumerate(refs[:-1]):
        refs[-1][step] = ref[...]


def query_body(*refs):
    part_refs, scale_ref, out_ref = refs[:-2], refs[-2], refs[-1]
    out_ref[...] = (add(part_refs) * scale_ref[...]).astype(out_ref.dtype)


def lift_only_body(*refs):
    part_refs, scale_ref, lifted_ref = refs[:-2], refs[-2], refs[-1]
    lifted_ref[...] = add(part_refs) * scale_ref[...]


def lift_body(*refs):
    part_refs, scale_ref, lifted_ref, gram_ref = refs[:-3], refs[-3], refs[-2], refs[-1]
    lifted = add(part_refs) * scale_ref[...]
    lifted_ref[...] = lifted
    gram_ref[...] = lax.dot_general(lifted, lifted, NT, precision=HIGH, preferred_element_type=jnp.float32)


def sum_body(*refs):
    refs[-1][...] = add(refs[:-1])


def finish_body(after, table, total_ref, got_ref, lifted_ref, out_ref):
    gram = jnp.where(table[SINGLES, COL_AT] % 2 == 1, total_ref[...], got_ref[...])
    out_ref[...] = (
        lax.dot_general(
            inverse_factor(gram), lifted_ref[...], NN, precision=HIGH, preferred_element_type=jnp.float32
        )
        * after
    )


def swap(value, axis, step):
    return lax.ppermute(value, axis, [(i, i ^ step) for i in range(lax.axis_size(axis))])


def spread_to(value, axis, stride=1):
    return [value] + [swap(value, axis, step) for step in range(stride, lax.axis_size(axis), stride)]


def deal(values, axis, stride=1):
    count = len(values)
    return [values[0]] + [swap(value, axis, (count - at) * stride) for at, value in enumerate(values[1:], 1)]


def add_up(*values):
    return call(sum_body, "sum", [WHOLE] * len(values), f32(*values[0].shape))(*values)


def core_one_terms(value, axis):
    n_row, n_col = lax.axis_size("row"), lax.axis_size("col")
    terms = [value]
    reach = [(step, 0) for step in range(1, n_row)] if axis == "row" else [(0, step) for step in range(2, n_col, 2)]
    for row_step, col_step in reach:
        pairs = [
            (row * n_col + col, ((row ^ row_step) * n_col + (col ^ col_step)) if col % 2 else row * n_col + col)
            for row in range(n_row)
            for col in range(n_col)
        ]
        terms.append(lax.ppermute(value, ("row", "col"), pairs))
    return terms


def shards(tiles, tile_ids, tile_count, query_degree, product_degree, panel):
    tile_set = tiles[0, 0]
    ids = tile_ids[0, 0]
    slots, side, _ = tile_set.shape
    width, share = panel.shape
    queries, products = query_degree.shape[0], product_degree.shape[0]
    query_tiles, product_tiles = queries // side, products // side
    n_row, n_col = lax.axis_size("row"), lax.axis_size("col")
    chips = n_col // 2
    row_at, col_at = lax.axis_index("row").astype(jnp.int32), lax.axis_index("col").astype(jnp.int32)
    columns = queries // n_col
    work = dict(flops=2 * slots * width * side * side, moved=2 * slots * side * side)
    scaled = call(
        start_body,
        "start",
        [SCALARS, AWAY, AWAY],
        bf16(width, share),
        [
            pltpu.VMEM((width, share), jnp.float32),
            pltpu.VMEM((1, products), jnp.int32),
            pltpu.SemaphoreType.DMA((2,)),
        ],
    )(row_at[None], in_hbm(panel), in_hbm(product_degree[None, :]))
    pieces = spread_to(scaled, "row")
    split = columns % side == 0
    tile_set, my_pscale, pscale, my_qscale, table = call(
        functools.partial(load_body, columns // side if split else 0),
        "load",
        [SCALARS, WHOLE] + [AWAY] * 4,
        [
            pltpu.VMEM((slots, side, side), jnp.bfloat16),
            f32(1, share),
            f32(1, products),
            f32(1, columns),
            jax.ShapeDtypeStruct((SINGLES + 1, slots), jnp.int32),
        ],
        [
            pltpu.SMEM(ids.shape, jnp.int32),
            pltpu.VMEM((1, products), jnp.int32),
            pltpu.VMEM((1, queries), jnp.int32),
            pltpu.SemaphoreType.DMA((3 + LOADS,)),
        ],
        moved=4 * slots * side * side,
        out_specs=[WHOLE] * 4 + [SCALARS],
    )(
        jnp.stack([row_at, col_at, tile_count[0, 0]]),
        scaled,
        in_hbm(tile_set),
        in_hbm(ids),
        in_hbm(product_degree[None, :]),
        in_hbm(query_degree[None, :]),
    )
    tile_set = pltpu.with_memory_space_constraint(tile_set, pltpu.VMEM)
    root_count = math.sqrt(products * n_col)
    half = f32(chips, width, columns)
    gram_rows = width * width // columns
    half_work = dict(flops=slots * width * side * side, moved=slots * side * side)
    query_scratch = pltpu.VMEM((query_tiles + 1, width, side), jnp.float32)
    product_scratch = pltpu.VMEM((product_tiles + 1, width, side), jnp.float32)
    query_held = pltpu.VMEM((query_tiles + 1, width, side), jnp.bfloat16)
    for iteration in range(ITERS):
        sets = SETS if iteration < ITERS - 1 else 1
        if iteration > 0:
            pieces = [piece for part in lifted for piece in spread_to(part, "row")]
            arrays = [WHOLE] * (len(pieces) + 2)
            message = f32(chips * width + gram_rows, columns)
            spread = pltpu.VMEM((product_tiles, width, side), jnp.float32)
            if split:
                held, other, gram = call(
                    functools.partial(next_other_body, len(pieces), chips),
                    "forward",
                    [SCALARS] + arrays,
                    [bf16(product_tiles + 1, 2 * width, side), message, f32(gram_rows, columns)],
                    [spread, query_scratch],
                    **half_work,
                )(table, *pieces, pscale, tile_set)
                got = swap(other, "col", 1)
                mine = call(
                    functools.partial(next_mine_body, chips),
                    "forward_rest",
                    [SCALARS] + [WHOLE] * 2,
                    f32(chips * width, columns),
                    [query_scratch],
                    **half_work,
                )(table, held, tile_set)
            else:
                mine, other, gram = call(
                    functools.partial(next_body, len(pieces), chips),
                    "forward",
                    [SCALARS] + arrays,
                    [f32(chips * width, columns), message, f32(gram_rows, columns)],
                    [spread, pltpu.VMEM((product_tiles + 1, 2 * width, side), jnp.bfloat16), query_scratch],
                    **work,
                )(table, *pieces, pscale, tile_set)
                got = swap(other, "col", 1)
            halves = 2 if columns % 256 == 0 else 1
            span = columns // halves
            shapes = [f32(width + width * width // span, span)] * chips + [f32(width, span)] * chips
            sums = call(
                functools.partial(next_pair_body, width, chips), "pair", [WHOLE] * 3, shapes[: halves * chips]
            )(mine, got, gram)
            parts = deal(sums[:chips], "col", 2)
            if halves == 1:
                rounded = call(next_query_body, "query", [WHOLE] * (chips + 1), bf16(width, columns))(
                    *parts, my_qscale
                )
            else:
                more = deal(sums[chips:], "col", 2)
                inverse, begun = call(
                    factor_query_body,
                    "query",
                    [WHOLE] * (chips + 1),
                    [f32(width, width), bf16(width, span)],
                    flops=2 * slots * width * side * side,
                )(*parts, my_qscale)
                rounded = call(rest_query_body, "query_rest", [WHOLE] * (chips + 3), bf16(width, columns))(
                    *more, inverse, begun, my_qscale
                )
        elif split:
            held, other = call(
                functools.partial(forward_other_body, n_row),
                "forward",
                [SCALARS] + [WHOLE] * (n_row + 1),
                [bf16(product_tiles + 1, width, side), half],
                [query_scratch],
                **half_work,
            )(table, *pieces, tile_set)
            got = swap(other, "col", 1)
            mine = call(
                forward_mine_body,
                "forward_rest",
                [SCALARS] + [WHOLE] * 2,
                half,
                [query_scratch],
                **half_work,
            )(table, held, tile_set)
        else:
            mine, other = call(
                functools.partial(forward_body, n_row),
                "forward",
                [SCALARS] + [WHOLE] * (n_row + 1),
                [half] * 2,
                [pltpu.VMEM((product_tiles + 1, width, side), jnp.bfloat16), query_scratch],
                **work,
            )(table, *pieces, tile_set)
            got = swap(other, "col", 1)
        if iteration == 0:
            sums = call(
                pair_body, "pair", [WHOLE] * 2, [f32(width, columns)] + [bf16(width, columns)] * (chips - 1)
            )(mine, got)
            parts = deal(sums, "col", 2)
            rounded = call(query_body, "query", [WHOLE] * (chips + 1), bf16(width, columns))(*parts, my_qscale)
        pieces = spread_to(rounded, "col", 2)
        here = call(join_body, "join", [WHOLE] * chips, bf16(chips, width, columns))(*pieces)
        there = swap(here, "col", 1)
        if split:
            begun = call(
                functools.partial(back_mine_body, chips),
                "backward",
                [SCALARS] + [WHOLE] * (chips + 1),
                f32(product_tiles + 1, width, side),
                [query_held],
                **half_work,
            )(table, *pieces, tile_set)
            sums = call(
                back_other_body,
                "backward_rest",
                [SCALARS] + [WHOLE] * 3,
                [f32(width // sets, share)] * (sets * n_row),
                [query_held, product_scratch],
                **half_work,
            )(table, there, begun, tile_set)
        else:
            sums = call(
                back_body,
                "backward",
                [SCALARS] + [WHOLE] * 3,
                [f32(width // sets, share)] * (sets * n_row),
                [query_held, product_scratch],
                **work,
            )(table, here, there, tile_set)
        parts = [deal(sums[n_row * part : n_row * (part + 1)], "row") for part in range(sets)]
        if iteration < ITERS - 1:
            lifted = [
                call(lift_only_body, "lift", [WHOLE] * (n_row + 1), f32(width // sets, share))(*part, my_pscale)
                for part in parts
            ]
    lifted, gram = call(
        lift_body, "lift", [WHOLE] * (n_row + 1), [f32(width, share), f32(width, width)]
    )(*parts[0], my_pscale)
    total = add_up(gram, swap(gram, "col", 1))
    for axis in ("row", "col"):
        total = add_up(*core_one_terms(total, axis))
    return call(
        functools.partial(finish_body, root_count), "finish", [SCALARS] + [WHOLE] * 3, f32(width, share)
    )(table, total, swap(total, "col", 1), lifted)


def solution(mesh):
    in_specs = (
        P("row", "col", None, None, None),
        P("row", "col", None, None),
        P("row", "col"),
        P("row"),
        P("col"),
        P(None, ("col", "row")),
    )
    out_specs = P(None, ("col", "row"))
    return jax.shard_map(shards, mesh=mesh, in_specs=in_specs, out_specs=out_specs, check_vma=False)
```

```python
import functools
import math

import jax
import jax.numpy as jnp
from jax import lax
from jax.experimental import pallas as pl
from jax.experimental.pallas import tpu as pltpu
from jax.sharding import PartitionSpec as P

ITERS = 2
GROUP = 8
LOADS = 8
SETS = 2
PANEL_STEP = 8
HIGH = lax.Precision.HIGHEST
VMEM_BYTES = 12 * 1024 * 1024
NT = (((1,), (1,)), ((), ()))
NN = (((1,), (0,)), ((), ()))

def inverse_factor(gram):
    width = gram.shape[0]
    rows = lax.broadcasted_iota(jnp.int32, (width, width), 0)
    cols = lax.broadcasted_iota(jnp.int32, (width, width), 1)
    work = jnp.concatenate([gram, (rows == cols).astype(jnp.float32)], axis=1)
    done = []
    for first in range(0, width, PANEL_STEP):
        height = width - first
        columns = [
            jnp.broadcast_to(work[:, first + j : first + j + 1], (height, 2 * width))
            for j in range(PANEL_STEP)
        ]
        for j in range(PANEL_STEP):
            scale = lax.rsqrt(columns[j][j : j + 1, :])
            row = work[j : j + 1, :] * scale
            factor = columns[j] * scale
            done.append(row)
            for later in range(j + 1, PANEL_STEP):
                columns[later] = columns[later] - factor * (columns[later][j : j + 1, :] * scale)
            work = work - factor * row
        work = work[PANEL_STEP:, :]
    return jnp.concatenate(done, axis=0)[:, width:]


SLOT, QUERY, PRODUCT = range(3)
FIELDS, LISTS, ALL = 3, 3, 2
SINGLES = FIELDS * LISTS
ROW_AT, COL_AT = 3, 4
WHOLE = pl.BlockSpec(memory_space=pltpu.VMEM)
SCALARS = pl.BlockSpec(memory_space=pltpu.SMEM)
AWAY = pl.BlockSpec(memory_space=pltpu.MemorySpace.HBM)


def call(body, name, in_specs, out_shape, scratch=(), flops=0, moved=0, out_specs=None):
    many = isinstance(out_shape, (tuple, list))
    return pl.pallas_call(
        body,
        out_shape=out_shape,
        in_specs=in_specs,
        out_specs=out_specs or ([WHOLE] * len(out_shape) if many else WHOLE),
        scratch_shapes=scratch,
        compiler_params=pltpu.CompilerParams(vmem_limit_bytes=VMEM_BYTES),
        cost_estimate=pl.CostEstimate(flops=flops, bytes_accessed=moved, transcendentals=0),
        name=name,
    )


def in_hbm(value):
    return pltpu.with_memory_space_constraint(value, pltpu.MemorySpace.HBM)


def f32(*shape):
    return jax.ShapeDtypeStruct(shape, jnp.float32)


def bf16(*shape):
    return jax.ShapeDtypeStruct(shape, jnp.bfloat16)


def put(held, owner, value, side, row=0):
    span, share = slice(row, row + value.shape[0]), value.shape[1]
    if share >= side:
        per = share // side
        for piece in range(per):
            held[owner * per + piece, span] = value[:, piece * side : (piece + 1) * side]
    else:
        per = side // share
        for at in range(per):

            @pl.when(owner % per == at)
            def _():
                held[owner // per, span, at * share : (at + 1) * share] = value


def get(total, owner, out_ref, side, row=0):
    span, share = slice(row, row + out_ref.shape[0]), out_ref.shape[1]
    if share >= side:
        per = share // side
        for piece in range(per):
            out_ref[:, piece * side : (piece + 1) * side] = total[owner * per + piece, span].astype(out_ref.dtype)
    else:
        per = side // share
        for at in range(per):

            @pl.when(owner % per == at)
            def _():
                out_ref[...] = total[owner // per, span, at * share : (at + 1) * share].astype(out_ref.dtype)


def emit(total, out_refs, me, side):
    sets = total.shape[1] // out_refs[0].shape[0]
    count = len(out_refs) // sets
    for at, out_ref in enumerate(out_refs):
        part, at = divmod(at, count)
        get(total, me ^ ((count - at) % count), out_ref, side, part * out_ref.shape[0])


def spare(held):
    held[held.shape[0] - 1] = jnp.zeros(held.shape[1:], held.dtype)


def collect(held, piece_refs, me, side):
    sets = held.shape[1] // piece_refs[0].shape[0]
    count = len(piece_refs) // sets
    for at, piece_ref in enumerate(piece_refs):
        part, step = divmod(at, count)
        put(held, me ^ step, piece_ref[...], side, part * piece_ref.shape[0])


def products(which, take, give, dims, table, held, tile_ref, total):
    width = total.shape[1]
    slots = tile_ref.shape[0]

    def run(first, length):
        for lane in range(length):
            at = first + lane
            term = lax.dot_general(
                held[table[which * FIELDS + take, at]],
                tile_ref[table[which * FIELDS + SLOT, at]],
                dims,
                preferred_element_type=jnp.float32,
            )
            if term.shape[0] > width:
                term = term[:width] + term[width:]
            total[table[which * FIELDS + give, at]] += term

    if isinstance(which, int):
        run(0, slots)
        return

    def step(g, carry):
        run(slots // 2 + g * GROUP, GROUP)
        return carry

    run(0, slots // 2)
    rest = jnp.maximum(table[SINGLES, which] - slots // 2, 0)
    lax.fori_loop(0, jnp.minimum((rest + GROUP - 1) // GROUP, slots // 2 // GROUP), step, 0)


forward = functools.partial(products, take=PRODUCT, give=QUERY, dims=NT)
backward = functools.partial(products, take=QUERY, give=PRODUCT, dims=NN)


def emit_half(total, out_ref, me, side, flip):
    for step in range(out_ref.shape[0]):
        get(total, me ^ (2 * step + flip), out_ref.at[step], side)


def collect_half(held, piece_refs, me, side, flip):
    for step, piece_ref in enumerate(piece_refs):
        put(held, me ^ (2 * step + flip), piece_ref[...], side)


def forward_body(n_in, table, *refs):
    pieces, (tile_ref, mine_ref, other_ref, held, total) = refs[:n_in], refs[n_in:]
    side = tile_ref.shape[1]
    collect(held, pieces, table[SINGLES, ROW_AT], side)
    spare(held)
    total[...] = jnp.zeros_like(total)
    forward(ALL, table=table, held=held, tile_ref=tile_ref, total=total)
    emit_half(total, mine_ref, table[SINGLES, COL_AT], side, 0)
    emit_half(total, other_ref, table[SINGLES, COL_AT], side, 1)


def forward_other_body(n_in, table, *refs):
    pieces, (tile_ref, held, other_ref, total) = refs[:n_in], refs[n_in:]
    side, me = tile_ref.shape[1], table[SINGLES, COL_AT]
    collect(held, pieces, table[SINGLES, ROW_AT], side)
    spare(held)
    total[...] = jnp.zeros_like(total)
    forward(1 - me % 2, table=table, held=held, tile_ref=tile_ref, total=total)
    emit_half(total, other_ref, me, side, 1)


def forward_mine_body(table, held, tile_ref, mine_ref, total):
    side, me = tile_ref.shape[1], table[SINGLES, COL_AT]
    total[...] = jnp.zeros_like(total)
    forward(me % 2, table=table, held=held, tile_ref=tile_ref, total=total)
    emit_half(total, mine_ref, me, side, 0)


def back_body(table, here_ref, there_ref, tile_ref, *refs):
    out_refs, (held, total) = refs[:-2], refs[-2:]
    side = tile_ref.shape[1]
    for flip, ref in enumerate((here_ref, there_ref)):
        collect_half(held, [ref.at[step] for step in range(ref.shape[0])], table[SINGLES, COL_AT], side, flip)
    spare(held)
    total[...] = jnp.zeros_like(total)
    backward(ALL, table=table, held=held, tile_ref=tile_ref, total=total)
    emit(total, out_refs, table[SINGLES, ROW_AT], side)


def back_mine_body(n_in, table, *refs):
    pieces, (tile_ref, total, held) = refs[:n_in], refs[n_in:]
    me = table[SINGLES, COL_AT]
    collect_half(held, pieces, me, tile_ref.shape[1], 0)
    spare(held)
    total[...] = jnp.zeros_like(total)
    backward(me % 2, table=table, held=held, tile_ref=tile_ref, total=total)


def back_other_body(table, there_ref, begun_ref, tile_ref, *refs):
    out_refs, (held, total) = refs[:-2], refs[-2:]
    side, me = tile_ref.shape[1], table[SINGLES, COL_AT]
    collect_half(held, [there_ref.at[step] for step in range(there_ref.shape[0])], me, side, 1)
    spare(held)
    total[...] = begun_ref[...]
    backward(1 - me % 2, table=table, held=held, tile_ref=tile_ref, total=total)
    emit(total, out_refs, table[SINGLES, ROW_AT], side)


def pack_gram(gram, columns):
    per = columns // gram.shape[0]
    rows = gram.shape[0] // per
    return jnp.concatenate([gram[at * rows : (at + 1) * rows] for at in range(per)], axis=1)


def unpack_gram(rows, width):
    return jnp.concatenate([rows[:, at : at + width] for at in range(0, rows.shape[1], width)], axis=0)


def split_panel(pieces, scale_ref, spread, held, me):
    width, side = spread.shape[1:]
    collect(spread, pieces, me, side)
    spare(held)
    for tile in range(spread.shape[0]):
        value = spread[tile] * scale_ref[:, tile * side : (tile + 1) * side]
        high = value.astype(jnp.bfloat16)
        held[tile, :width] = high
        held[tile, width:] = (value - high.astype(jnp.float32)).astype(jnp.bfloat16)
    gram = jnp.zeros((width, width), jnp.float32)
    for tile in range(spread.shape[0]):
        gram = gram + lax.dot_general(
            spread[tile], spread[tile], NT, precision=HIGH, preferred_element_type=jnp.float32
        )
    return gram


def emit_rows(total, out_ref, chips, me, side, flip):
    width = total.shape[1]
    for step in range(chips):
        get(total, me ^ (2 * step + flip), out_ref.at[step * width : (step + 1) * width], side)


def next_body(n_in, chips, table, *refs):
    pieces, (scale_ref, tile_ref, mine_ref, other_ref, gram_ref, spread, held, total) = refs[:n_in], refs[n_in:]
    side, me, width = tile_ref.shape[1], table[SINGLES, COL_AT], total.shape[1]
    rows = pack_gram(split_panel(pieces, scale_ref, spread, held, table[SINGLES, ROW_AT]), gram_ref.shape[1])
    gram_ref[...] = rows
    other_ref[chips * width :] = rows
    total[...] = jnp.zeros_like(total)
    forward(ALL, table=table, held=held, tile_ref=tile_ref, total=total)
    emit_rows(total, mine_ref, chips, me, side, 0)
    emit_rows(total, other_ref, chips, me, side, 1)


def next_other_body(n_in, chips, table, *refs):
    pieces, (scale_ref, tile_ref, held, other_ref, gram_ref, spread, total) = refs[:n_in], refs[n_in:]
    side, me, width = tile_ref.shape[1], table[SINGLES, COL_AT], total.shape[1]
    rows = pack_gram(split_panel(pieces, scale_ref, spread, held, table[SINGLES, ROW_AT]), gram_ref.shape[1])
    gram_ref[...] = rows
    other_ref[chips * width :] = rows
    total[...] = jnp.zeros_like(total)
    forward(1 - me % 2, table=table, held=held, tile_ref=tile_ref, total=total)
    emit_rows(total, other_ref, chips, me, side, 1)


def next_mine_body(chips, table, held, tile_ref, mine_ref, total):
    side, me = tile_ref.shape[1], table[SINGLES, COL_AT]
    total[...] = jnp.zeros_like(total)
    forward(me % 2, table=table, held=held, tile_ref=tile_ref, total=total)
    emit_rows(total, mine_ref, chips, me, side, 0)


def next_pair_body(width, chips, mine_ref, got_ref, gram_ref, *outs):
    columns = outs[0].shape[1]
    gram = pack_gram(unpack_gram(gram_ref[...] + got_ref[chips * width :], width), columns)
    for at, out_ref in enumerate(outs):
        part, at = divmod(at, chips)
        step = (chips - at) % chips
        block = slice(step * width, (step + 1) * width), slice(part * columns, (part + 1) * columns)
        out_ref[:width] = mine_ref[block] + got_ref[block]
        if part == 0:
            out_ref[width:] = gram


def factor_query_body(*refs):
    part_refs, scale_ref, inverse_ref, out_ref = refs[:-3], refs[-3], refs[-2], refs[-1]
    width, columns = out_ref.shape
    total = add(part_refs)
    inverse = inverse_factor(unpack_gram(total[width:], width))
    inverse_ref[...] = inverse
    current = lax.dot_general(inverse, total[:width], NN, precision=HIGH, preferred_element_type=jnp.float32)
    out_ref[...] = (current * scale_ref[:, :columns]).astype(out_ref.dtype)


def rest_query_body(*refs):
    part_refs, inverse_ref, begun_ref, scale_ref, out_ref = refs[:-4], *refs[-4:]
    columns = begun_ref.shape[1]
    current = lax.dot_general(
        inverse_ref[...], add(part_refs), NN, precision=HIGH, preferred_element_type=jnp.float32
    )
    out_ref[:, :columns] = begun_ref[...]
    out_ref[:, columns:] = (current * scale_ref[:, columns:]).astype(out_ref.dtype)


def next_query_body(*refs):
    part_refs, scale_ref, out_ref = refs[:-2], refs[-2], refs[-1]
    width = out_ref.shape[0]
    total = add(part_refs)
    inverse = inverse_factor(unpack_gram(total[width:], width))
    current = lax.dot_general(inverse, total[:width], NN, precision=HIGH, preferred_element_type=jnp.float32)
    out_ref[...] = (current * scale_ref[...]).astype(out_ref.dtype)


def add(refs):
    total = refs[0][...].astype(jnp.float32)
    for ref in refs[1:]:
        total = total + ref[...].astype(jnp.float32)
    return total


def start_body(place, panel_ref, degree_ref, out_ref, held, degrees, sems):
    share = panel_ref.shape[1]
    at = pl.multiple_of(place[0] * share, 128)
    loads = [
        pltpu.make_async_copy(degree_ref, degrees, sems.at[0]),
        pltpu.make_async_copy(panel_ref, held, sems.at[1]),
    ]
    for load in loads:
        load.start()
    for load in loads:
        load.wait()
    scale = 1.0 / jnp.sqrt(degrees[:, pl.ds(at, share)].astype(jnp.float32))
    out_ref[...] = (held[...] * scale).astype(out_ref.dtype)


def clear_table(table, lists, query_tiles, product_tiles):
    for which in lists:
        table[SINGLES, which] = 0
        for at in range(table.shape[1]):
            table[which * FIELDS + SLOT, at] = 0
            table[which * FIELDS + QUERY, at] = query_tiles
            table[which * FIELDS + PRODUCT, at] = product_tiles


def fill_table(table, ids, place, per):
    table[SINGLES, ROW_AT] = place[0]
    table[SINGLES, COL_AT] = place[1]

    def step(slot, carry):
        query, product = ids[0, slot], ids[1, slot]
        which = query // per % 2 if per else ALL
        at = table[SINGLES, which]
        table[which * FIELDS + SLOT, at] = slot
        table[which * FIELDS + QUERY, at] = query
        table[which * FIELDS + PRODUCT, at] = product
        table[SINGLES, which] = at + 1
        return carry

    lax.fori_loop(0, jnp.minimum(place[2], ids.shape[1]), step, 0)


def load_body(per, place, after_ref, tile_ref, id_ref, product_ref, query_ref, *refs):
    keep, my_product_ref, product_out, my_query_ref, table, ids, degrees, counts, sems = refs
    loads = [
        pltpu.make_async_copy(id_ref, ids, sems.at[0]),
        pltpu.make_async_copy(product_ref, degrees, sems.at[1]),
        pltpu.make_async_copy(query_ref, counts, sems.at[2]),
    ]
    part = tile_ref.shape[0] // LOADS
    for step in range(LOADS):
        span = pl.ds(step * part, part)
        loads.append(pltpu.make_async_copy(tile_ref.at[span], keep.at[span], sems.at[3 + step]))
    for load in loads:
        load.start()
    side = tile_ref.shape[1]
    lists = (0, 1) if per else (ALL,)
    clear_table(table, lists, query_ref.shape[1] // side, product_ref.shape[1] // side)
    loads[0].wait()
    fill_table(table, ids, place, per)
    loads[1].wait()
    product_out[...] = 1.0 / jnp.sqrt(degrees[...].astype(jnp.float32))
    share = my_product_ref.shape[1]
    at = pl.multiple_of(place[0] * share, 128)
    my_product_ref[...] = product_out[:, pl.ds(at, share)]
    loads[2].wait()
    columns = my_query_ref.shape[1]
    if columns % 128 == 0:
        at = pl.multiple_of(place[1] * columns, 128)
        my_query_ref[...] = 1.0 / jnp.sqrt(counts[:, pl.ds(at, columns)].astype(jnp.float32))
    else:
        for step in range(counts.shape[1] // columns):

            @pl.when(place[1] == step)
            def _():
                degree = counts[:, step * columns : (step + 1) * columns]
                my_query_ref[...] = 1.0 / jnp.sqrt(degree.astype(jnp.float32))
    for load in loads[3:]:
        load.wait()


def pair_body(mine_ref, got_ref, *outs):
    count = len(outs)
    for at, out_ref in enumerate(outs):
        step = (count - at) % count
        out_ref[...] = (mine_ref[step] + got_ref[step]).astype(out_ref.dtype)


def join_body(*refs):
    for step, ref in enumerate(refs[:-1]):
        refs[-1][step] = ref[...]


def query_body(*refs):
    part_refs, scale_ref, out_ref = refs[:-2], refs[-2], refs[-1]
    out_ref[...] = (add(part_refs) * scale_ref[...]).astype(out_ref.dtype)


def lift_only_body(*refs):
    part_refs, scale_ref, lifted_ref = refs[:-2], refs[-2], refs[-1]
    lifted_ref[...] = add(part_refs) * scale_ref[...]


def lift_body(*refs):
    part_refs, scale_ref, lifted_ref, gram_ref = refs[:-3], refs[-3], refs[-2], refs[-1]
    lifted = add(part_refs) * scale_ref[...]
    lifted_ref[...] = lifted
    gram_ref[...] = lax.dot_general(lifted, lifted, NT, precision=HIGH, preferred_element_type=jnp.float32)


def sum_body(*refs):
    refs[-1][...] = add(refs[:-1])


def finish_body(after, *refs):
    grams, lifted_ref, out_ref = refs[:-2], refs[-2], refs[-1]
    out_ref[...] = (
        lax.dot_general(
            inverse_factor(add(grams)), lifted_ref[...], NN, precision=HIGH, preferred_element_type=jnp.float32
        )
        * after
    )


def swap(value, axis, step):
    return lax.ppermute(value, axis, [(i, i ^ step) for i in range(lax.axis_size(axis))])


def spread_to(value, axis, stride=1):
    return [value] + [swap(value, axis, step) for step in range(stride, lax.axis_size(axis), stride)]


def deal(values, axis, stride=1):
    count = len(values)
    return [values[0]] + [swap(value, axis, (count - at) * stride) for at, value in enumerate(values[1:], 1)]


def add_up(*values):
    return call(sum_body, "sum", [WHOLE] * len(values), f32(*values[0].shape))(*values)


def crossed_terms(value, axis):
    n_row, n_col = lax.axis_size("row"), lax.axis_size("col")
    terms = [value]
    reach = [(step, 1) for step in range(1, n_row)] if axis == "row" else [(0, step + 1) for step in range(2, n_col, 2)]
    for row_step, col_step in reach:
        pairs = [
            (row * n_col + col, (row ^ row_step) * n_col + (col ^ col_step))
            for row in range(n_row)
            for col in range(n_col)
        ]
        terms.append(lax.ppermute(value, ("row", "col"), pairs))
    return terms


def shards(tiles, tile_ids, tile_count, query_degree, product_degree, panel):
    tile_set = tiles[0, 0]
    ids = tile_ids[0, 0]
    slots, side, _ = tile_set.shape
    width, share = panel.shape
    queries, products = query_degree.shape[0], product_degree.shape[0]
    query_tiles, product_tiles = queries // side, products // side
    n_row, n_col = lax.axis_size("row"), lax.axis_size("col")
    chips = n_col // 2
    row_at, col_at = lax.axis_index("row").astype(jnp.int32), lax.axis_index("col").astype(jnp.int32)
    columns = queries // n_col
    work = dict(flops=2 * slots * width * side * side, moved=2 * slots * side * side)
    scaled = call(
        start_body,
        "start",
        [SCALARS, AWAY, AWAY],
        bf16(width, share),
        [
            pltpu.VMEM((width, share), jnp.float32),
            pltpu.VMEM((1, products), jnp.int32),
            pltpu.SemaphoreType.DMA((2,)),
        ],
    )(row_at[None], in_hbm(panel), in_hbm(product_degree[None, :]))
    pieces = spread_to(scaled, "row")
    split = columns % side == 0
    tile_set, my_pscale, pscale, my_qscale, table = call(
        functools.partial(load_body, columns // side if split else 0),
        "load",
        [SCALARS, WHOLE] + [AWAY] * 4,
        [
            pltpu.VMEM((slots, side, side), jnp.bfloat16),
            f32(1, share),
            f32(1, products),
            f32(1, columns),
            jax.ShapeDtypeStruct((SINGLES + 1, slots), jnp.int32),
        ],
        [
            pltpu.SMEM(ids.shape, jnp.int32),
            pltpu.VMEM((1, products), jnp.int32),
            pltpu.VMEM((1, queries), jnp.int32),
            pltpu.SemaphoreType.DMA((3 + LOADS,)),
        ],
        moved=4 * slots * side * side,
        out_specs=[WHOLE] * 4 + [SCALARS],
    )(
        jnp.stack([row_at, col_at, tile_count[0, 0]]),
        scaled,
        in_hbm(tile_set),
        in_hbm(ids),
        in_hbm(product_degree[None, :]),
        in_hbm(query_degree[None, :]),
    )
    tile_set = pltpu.with_memory_space_constraint(tile_set, pltpu.VMEM)
    root_count = math.sqrt(products * n_col)
    half = f32(chips, width, columns)
    gram_rows = width * width // columns
    half_work = dict(flops=slots * width * side * side, moved=slots * side * side)
    query_scratch = pltpu.VMEM((query_tiles + 1, width, side), jnp.float32)
    product_scratch = pltpu.VMEM((product_tiles + 1, width, side), jnp.float32)
    query_held = pltpu.VMEM((query_tiles + 1, width, side), jnp.bfloat16)
    for iteration in range(ITERS):
        sets = SETS if iteration < ITERS - 1 else 1
        if iteration > 0:
            pieces = [piece for part in lifted for piece in spread_to(part, "row")]
            arrays = [WHOLE] * (len(pieces) + 2)
            message = f32(chips * width + gram_rows, columns)
            spread = pltpu.VMEM((product_tiles, width, side), jnp.float32)
            if split:
                held, other, gram = call(
                    functools.partial(next_other_body, len(pieces), chips),
                    "forward",
                    [SCALARS] + arrays,
                    [bf16(product_tiles + 1, 2 * width, side), message, f32(gram_rows, columns)],
                    [spread, query_scratch],
                    **half_work,
                )(table, *pieces, pscale, tile_set)
                got = swap(other, "col", 1)
                mine = call(
                    functools.partial(next_mine_body, chips),
                    "forward_rest",
                    [SCALARS] + [WHOLE] * 2,
                    f32(chips * width, columns),
                    [query_scratch],
                    **half_work,
                )(table, held, tile_set)
            else:
                mine, other, gram = call(
                    functools.partial(next_body, len(pieces), chips),
                    "forward",
                    [SCALARS] + arrays,
                    [f32(chips * width, columns), message, f32(gram_rows, columns)],
                    [spread, pltpu.VMEM((product_tiles + 1, 2 * width, side), jnp.bfloat16), query_scratch],
                    **work,
                )(table, *pieces, pscale, tile_set)
                got = swap(other, "col", 1)
            halves = 2 if columns % 256 == 0 else 1
            span = columns // halves
            shapes = [f32(width + width * width // span, span)] * chips + [f32(width, span)] * chips
            sums = call(
                functools.partial(next_pair_body, width, chips), "pair", [WHOLE] * 3, shapes[: halves * chips]
            )(mine, got, gram)
            parts = deal(sums[:chips], "col", 2)
            if halves == 1:
                rounded = call(next_query_body, "query", [WHOLE] * (chips + 1), bf16(width, columns))(
                    *parts, my_qscale
                )
            else:
                more = deal(sums[chips:], "col", 2)
                inverse, begun = call(
                    factor_query_body,
                    "query",
                    [WHOLE] * (chips + 1),
                    [f32(width, width), bf16(width, span)],
                    flops=2 * slots * width * side * side,
                )(*parts, my_qscale)
                rounded = call(rest_query_body, "query_rest", [WHOLE] * (chips + 3), bf16(width, columns))(
                    *more, inverse, begun, my_qscale
                )
        elif split:
            held, other = call(
                functools.partial(forward_other_body, n_row),
                "forward",
                [SCALARS] + [WHOLE] * (n_row + 1),
                [bf16(product_tiles + 1, width, side), half],
                [query_scratch],
                **half_work,
            )(table, *pieces, tile_set)
            got = swap(other, "col", 1)
            mine = call(
                forward_mine_body,
                "forward_rest",
                [SCALARS] + [WHOLE] * 2,
                half,
                [query_scratch],
                **half_work,
            )(table, held, tile_set)
        else:
            mine, other = call(
                functools.partial(forward_body, n_row),
                "forward",
                [SCALARS] + [WHOLE] * (n_row + 1),
                [half] * 2,
                [pltpu.VMEM((product_tiles + 1, width, side), jnp.bfloat16), query_scratch],
                **work,
            )(table, *pieces, tile_set)
            got = swap(other, "col", 1)
        if iteration == 0:
            sums = call(
                pair_body, "pair", [WHOLE] * 2, [f32(width, columns)] + [bf16(width, columns)] * (chips - 1)
            )(mine, got)
            parts = deal(sums, "col", 2)
            rounded = call(query_body, "query", [WHOLE] * (chips + 1), bf16(width, columns))(*parts, my_qscale)
        pieces = spread_to(rounded, "col", 2)
        here = call(join_body, "join", [WHOLE] * chips, bf16(chips, width, columns))(*pieces)
        there = swap(here, "col", 1)
        if split:
            begun = call(
                functools.partial(back_mine_body, chips),
                "backward",
                [SCALARS] + [WHOLE] * (chips + 1),
                f32(product_tiles + 1, width, side),
                [query_held],
                **half_work,
            )(table, *pieces, tile_set)
            sums = call(
                back_other_body,
                "backward_rest",
                [SCALARS] + [WHOLE] * 3,
                [f32(width // sets, share)] * (sets * n_row),
                [query_held, product_scratch],
                **half_work,
            )(table, there, begun, tile_set)
        else:
            sums = call(
                back_body,
                "backward",
                [SCALARS] + [WHOLE] * 3,
                [f32(width // sets, share)] * (sets * n_row),
                [query_held, product_scratch],
                **work,
            )(table, here, there, tile_set)
        parts = [deal(sums[n_row * part : n_row * (part + 1)], "row") for part in range(sets)]
        if iteration < ITERS - 1:
            lifted = [
                call(lift_only_body, "lift", [WHOLE] * (n_row + 1), f32(width // sets, share))(*part, my_pscale)
                for part in parts
            ]
    lifted, gram = call(
        lift_body, "lift", [WHOLE] * (n_row + 1), [f32(width, share), f32(width, width)]
    )(*parts[0], my_pscale)
    total = add_up(*crossed_terms(gram, "row"))
    return call(
        functools.partial(finish_body, root_count), "finish", [WHOLE] * (chips + 1), f32(width, share)
    )(*crossed_terms(add_up(total, swap(total, "col", 1)), "col"), lifted)


def solution(mesh):
    in_specs = (
        P("row", "col", None, None, None),
        P("row", "col", None, None),
        P("row", "col"),
        P("row"),
        P("col"),
        P(None, ("col", "row")),
    )
    out_specs = P(None, ("col", "row"))
    return jax.shard_map(shards, mesh=mesh, in_specs=in_specs, out_specs=out_specs, check_vma=False)
```
